128 devices in a mesh: tok: 8 (over x_lo, z), ffn: 16 (over y, x_hi, core).
Axes of the slice: x: 4 (x_hi: 2, x_lo: 2; x = x_hi * 2 + x_lo), y: 4, z: 4, core: 2. Of those that a mesh axis runs over, the one named last changes fastest.
Arguments:
- tokens: bfloat16 [2, 8192, 1024], P(None, ('tok', 'ffn')), may hold values from -6 to 6
- memory: bfloat16 [2, 4096, 1024], P(None, ('tok', 'ffn')), may hold values from -6 to 6
- segment_ids: int32 [2, 8192], P(None, 'tok'), may hold values from 0 to 2, as said below
- buckets: int32 [1024], replicated, may hold values from 0 to 31, as said below
- w_query: bfloat16 [1024, 1024], P(('tok', 'ffn')), may hold values from -0.1875 to 0.1875
- w_keyval: bfloat16 [1024, 1024], P(('tok', 'ffn')), may hold values from -0.1875 to 0.1875
- w_output: bfloat16 [1024, 1024], P(('tok', 'ffn')), may hold values from -1.5 to 1.5
- w_cross_query: bfloat16 [1024, 1024], P(('tok', 'ffn')), may hold values from -0.1875 to 0.1875
- w_cross_keyval: bfloat16 [1024, 1024], P(('tok', 'ffn')), may hold values from -0.1875 to 0.1875
- w_cross_output: bfloat16 [1024, 1024], P(('tok', 'ffn')), may hold values from -1.5 to 1.5
- norm_self: bfloat16 [1024], P(('tok', 'ffn')), may hold values from 0.5 to 1.5
- norm_cross: bfloat16 [1024], P(('tok', 'ffn')), may hold values from 0.5 to 1.5
- norm_ffn: bfloat16 [1024], P(('tok', 'ffn')), may hold values from 0.5 to 1.5
- bias_table: bfloat16 [512], P(('tok', 'ffn')), may hold values from -4 to 4
- w_gate: bfloat16 [1024, 2816], P('tok', 'ffn'), may hold values from -0.1875 to 0.1875
- w_up: bfloat16 [1024, 2816], P('tok', 'ffn'), may hold values from -0.1875 to 0.1875
- w_down: bfloat16 [2816, 1024], P('ffn', 'tok'), may hold values from -0.109375 to 0.109375
- cotangent: bfloat16 [2, 8192, 1024], P(None, ('tok', 'ffn')), may hold values from -6 to 6
Outputs:
- output: float32 [2, 8192, 1024], P(None, ('tok', 'ffn'))
- d_tokens: float32 [2, 8192, 1024], P(None, ('tok', 'ffn'))
- d_memory: float32 [2, 4096, 1024], P(None, ('tok', 'ffn'))
- d_w_query: float32 [1024, 1024], P(('tok', 'ffn'))
- d_w_keyval: float32 [1024, 1024], P(('tok', 'ffn'))
- d_w_output: float32 [1024, 1024], P(('tok', 'ffn'))
- d_w_cross_query: float32 [1024, 1024], P(('tok', 'ffn'))
- d_w_cross_keyval: float32 [1024, 1024], P(('tok', 'ffn'))
- d_w_cross_output: float32 [1024, 1024], P(('tok', 'ffn'))
- d_norm_self: float32 [1024], P(('tok', 'ffn'))
- d_norm_cross: float32 [1024], P(('tok', 'ffn'))
- d_norm_ffn: float32 [1024], P(('tok', 'ffn'))
- d_bias_table: float32 [512], P(('tok', 'ffn'))
- d_w_gate: float32 [1024, 2816], P('tok', 'ffn')
- d_w_up: float32 [1024, 2816], P('tok', 'ffn')
- d_w_down: float32 [2816, 1024], P('ffn', 'tok')
The draws below stay inside these ranges and needn't reach their ends.
Inputs may be any that keep to these rules, and one draw needn't show every extreme that they name: `segment_ids`: within a sequence the ids never fall; document 1 starts within the first 64 positions and ends within the last 64, documents 0 and 2 fill the rest. buckets never fall as the distance grows, buckets[d] = d for d < 16, and the last entry is 31.
All inputs are finite; a program needn't handle non-finite values.
Results may differ from the reference program's by a relative error of at most 0.04.
Values may be sent and summed in bfloat16 or wider, within the bound.
No kernel may reach another device: no remote copies, remote signals or barrier semaphores. Data moves between devices by JAX's collectives and lax.ppermute only.
A program may use at most 384 MiB of HBM per device.

```python
import jax
import jax.numpy as jnp
from jax import lax

D = 1024
FF = 2816
HEADS = 16
HEAD_DIM = 64
BUCKETS = 32
KV_HEADS = 8
MEM = 512
SEQ = 1024
MICRO = 2
ROWS = 8
TOKENS_MB = 8192
MEM_ROWS = 4096
KV_WIDTH = 1024


def draw_segment_ids(key, part):
    key = jax.random.fold_in(key, 3)
    margin = SEQ // 16
    lower_key, upper_key = jax.random.split(key)
    lower_edge = jax.random.randint(lower_key, (MICRO, ROWS, 1), 1, margin)
    upper_edge = jax.random.randint(upper_key, (MICRO, ROWS, 1), SEQ - margin + 1, SEQ)
    places = jnp.arange(SEQ, dtype=jnp.int32)[None, None, :]
    segment = (places >= lower_edge).astype(jnp.int32) + (places >= upper_edge).astype(jnp.int32)
    return segment.reshape(MICRO, ROWS * SEQ)


def draw_buckets(key, part):
    key = jax.random.fold_in(key, 5)
    places = jnp.arange(SEQ, dtype=jnp.int32)
    rolls = jax.random.randint(key, (SEQ,), 0, places + 1)
    advance = jnp.where(places < BUCKETS // 2, 1, (rolls < 8).astype(jnp.int32))
    advance = jnp.where(places == 0, 0, advance)
    levels = jnp.minimum(jnp.cumsum(advance), BUCKETS - 1)
    return jnp.where(places == SEQ - 1, BUCKETS - 1, levels).astype(jnp.int32)


def steps_of(key, extent, cuts, least, top_value):
    def one(dim, blocks):
        heights = jax.random.uniform(jax.random.fold_in(jax.random.fold_in(key, 6), dim), (blocks,), jnp.float32, least / len(cuts), top_value / len(cuts))
        return jnp.repeat(jnp.exp(heights), extent[dim] // blocks).reshape((-1,) + (1,) * (len(extent) - dim - 1))

    factor_of = one(*cuts[0])
    for cut in cuts[1:]:
        factor_of = factor_of * one(*cut)
    return factor_of


def normal_values(key, dims, deviation, reach, cuts=(), kind=jnp.bfloat16):
    loudness = steps_of(key, dims, cuts, -0.22, 0.18) if cuts else 1.0
    drawn = jax.random.normal(key, dims, jnp.float32) * deviation * loudness
    return jnp.minimum(jnp.maximum(drawn, -reach), reach).astype(kind)


def setup_inputs(seed: int = 0) -> dict:
    streams_of = jax.random.split(jax.random.key(seed), 19)
    return {
        "tokens": normal_values(streams_of[0], (MICRO, TOKENS_MB, D), 1.0, 6.0, ((1, 128),)),
        "memory": normal_values(streams_of[1], (MICRO, MEM_ROWS, D), 1.0, 6.0, ((1, 128),)),
        "segment_ids": draw_segment_ids(jax.random.fold_in(streams_of[18], 71), 0),
        "buckets": draw_buckets(jax.random.fold_in(streams_of[18], 71), 0),
        "w_query": normal_values(streams_of[4], (D, D), D ** -0.5, 0.1875, ((0, 128),)),
        "w_keyval": normal_values(streams_of[5], (D, KV_WIDTH), D ** -0.5, 0.1875, ((0, 128),)),
        "w_output": normal_values(streams_of[6], (D, D), (D // 64) ** -0.5, 1.5, ((0, 128),)),
        "w_cross_query": normal_values(streams_of[7], (D, D), D ** -0.5, 0.1875, ((0, 128),)),
        "w_cross_keyval": normal_values(streams_of[8], (D, KV_WIDTH), D ** -0.5, 0.1875, ((0, 128),)),
        "w_cross_output": normal_values(streams_of[9], (D, D), (D // 64) ** -0.5, 1.5, ((0, 128),)),
        "norm_self": jnp.clip(1.0 + 0.1 * jax.random.normal(streams_of[10], (D,), jnp.float32), 0.5, 1.5).astype(jnp.bfloat16),
        "norm_cross": jnp.clip(1.0 + 0.1 * jax.random.normal(streams_of[11], (D,), jnp.float32), 0.5, 1.5).astype(jnp.bfloat16),
        "norm_ffn": jnp.clip(1.0 + 0.1 * jax.random.normal(streams_of[12], (D,), jnp.float32), 0.5, 1.5).astype(jnp.bfloat16),
        "bias_table": normal_values(streams_of[13], (HEADS * BUCKETS,), 1.0, 4.0, ((0, 128),)),
        "w_gate": normal_values(streams_of[14], (D, FF), D ** -0.5, 0.1875, ((0, 8), (1, 16))),
        "w_up": normal_values(streams_of[15], (D, FF), D ** -0.5, 0.1875, ((0, 8), (1, 16))),
        "w_down": normal_values(streams_of[16], (FF, D), FF ** -0.5, 0.109375, ((0, 16), (1, 8))),
        "cotangent": normal_values(streams_of[17], (MICRO, TOKENS_MB, D), 1.0, 6.0, ((1, 128),)),
    }


@jax.custom_vjp
def low(v):
    return lax.optimization_barrier(v.astype(jnp.bfloat16)).astype(jnp.float32)

@jax.custom_vjp
def low_back(v):
    return v

def low_keep(v):
    return (low(v), None)

def low_pass(kept, grad):
    return (grad,)

def back_keep(v):
    return (v, None)

def back_low(kept, grad):
    return (low(grad),)
low.defvjp(low_keep, low_pass)
low_back.defvjp(back_keep, back_low)
epsilon = 1e-06
masked_score = -1e+30

def scaled_norm(values, gains):
    inverse = lax.rsqrt(lax.optimization_barrier(jnp.mean(values * values, axis=-1, keepdims=True)) + epsilon)
    return values * inverse * gains

def product(left, right):
    return jnp.dot(left, right, precision=lax.Precision.HIGHEST)

def split_heads(keyvals):
    half_width = KV_HEADS * HEAD_DIM
    key_heads = keyvals[:, :half_width].reshape(-1, KV_HEADS, HEAD_DIM)
    value_heads = keyvals[:, half_width:].reshape(-1, KV_HEADS, HEAD_DIM)
    return (key_heads, value_heads)

def attend(row_block, key_heads, value_heads, bias_terms, allowed):
    scaling = HEAD_DIM ** (-0.5)
    raw_scores = jnp.einsum('qngd,knd->ngqk', row_block, key_heads, precision=lax.Precision.HIGHEST)
    scores = low_back(raw_scores * scaling + bias_terms)
    scores = jnp.where(allowed, scores, masked_score)
    highest = lax.optimization_barrier(jnp.max(scores, axis=-1, keepdims=True))
    exponent = jnp.exp(scores - highest)
    attention = low(exponent / lax.optimization_barrier(jnp.sum(exponent, axis=-1, keepdims=True)))
    output = jnp.einsum('ngqk,knd->qngd', attention, value_heads, precision=lax.Precision.HIGHEST)
    return output.reshape(row_block.shape[0], HEADS * HEAD_DIM)

def self_sequence(queries, keyvals, segment, buckets, table):
    key_heads, value_heads = split_heads(keyvals)
    head_table = table.reshape(KV_HEADS, HEADS // KV_HEADS, BUCKETS)
    block_rows = min(512, SEQ)
    key_pos = jnp.arange(SEQ, dtype=jnp.int32)

    def one_block(first_row):
        query_pos = first_row + jnp.arange(block_rows, dtype=jnp.int32)
        row_block = lax.dynamic_slice_in_dim(queries, first_row, block_rows, 0)
        row_block = row_block.reshape(block_rows, KV_HEADS, HEADS // KV_HEADS, HEAD_DIM)
        distance = jnp.clip(query_pos[:, None] - key_pos[None, :], 0, SEQ - 1)
        bias_terms = head_table[:, :, buckets[distance]]
        segment_rows = lax.dynamic_slice_in_dim(segment, first_row, block_rows, 0)
        allowed = (key_pos[None, :] <= query_pos[:, None]) & (segment[None, :] == segment_rows[:, None])
        return attend(row_block, key_heads, value_heads, bias_terms, allowed)
    starts = jnp.arange(SEQ // block_rows, dtype=jnp.int32) * block_rows
    return lax.map(jax.checkpoint(one_block), starts).reshape(SEQ, HEADS * HEAD_DIM)

def cross_sequence(queries, keyvals):
    key_heads, value_heads = split_heads(keyvals)
    block_rows = min(512, SEQ)

    def one_block(first_row):
        row_block = lax.dynamic_slice_in_dim(queries, first_row, block_rows, 0)
        row_block = row_block.reshape(block_rows, KV_HEADS, HEADS // KV_HEADS, HEAD_DIM)
        return attend(row_block, key_heads, value_heads, 0.0, True)
    starts = jnp.arange(SEQ // block_rows, dtype=jnp.int32) * block_rows
    return lax.map(jax.checkpoint(one_block), starts).reshape(SEQ, HEADS * HEAD_DIM)

def reference(tokens, memory, segment_ids, buckets, w_query, w_keyval, w_output, w_cross_query, w_cross_keyval, w_cross_output, norm_self, norm_cross, norm_ffn, bias_table, w_gate, w_up, w_down, cotangent):
    sequences = MICRO * ROWS
    params = tuple((weight.astype(jnp.float32) for weight in (w_query, w_keyval, w_output, w_cross_query, w_cross_keyval, w_cross_output, norm_self, norm_cross, norm_ffn, bias_table, w_gate, w_up, w_down)))
    inputs = tokens.astype(jnp.float32).reshape(sequences, SEQ, D)
    encoded = memory.astype(jnp.float32).reshape(sequences, MEM, D)
    segments = segment_ids.reshape(sequences, SEQ)

    def forward(inputs, encoded, params):
        query_w, keyval_w, output_w, cross_query_w, cross_keyval_w, cross_output_w, gain_self, gain_cross, feedforward_gain, table, gate_w, up_w, down_w = params
        flat_rows = inputs.reshape(-1, D)
        normed = low(scaled_norm(flat_rows, gain_self))
        queries = low_back(low(product(normed, query_w)))
        keyvals = low_back(low(product(normed, keyval_w)))
        attended = lax.map(lambda packed: self_sequence(packed[0], packed[1], packed[2], buckets, table), (queries.reshape(sequences, SEQ, D), keyvals.reshape(sequences, SEQ, KV_WIDTH), segments))
        attended = low_back(low(attended.reshape(-1, D)))
        after_self = flat_rows + low_back(product(attended, output_w))
        normed_cross = low(scaled_norm(after_self, gain_cross))
        cross_queries = low_back(low(product(normed_cross, cross_query_w)))
        cross_keyvals = low_back(low(product(encoded.reshape(-1, D), cross_keyval_w)))
        crossed = lax.map(lambda packed: cross_sequence(packed[0], packed[1]), (cross_queries.reshape(sequences, SEQ, D), cross_keyvals.reshape(sequences, MEM, KV_WIDTH)))
        crossed = low_back(low(crossed.reshape(-1, D)))
        after_cross = after_self + low_back(product(crossed, cross_output_w))
        normed_ffn = low(scaled_norm(after_cross, feedforward_gain))
        gate_values = low_back(product(normed_ffn, gate_w))
        up_values = low_back(product(normed_ffn, up_w))
        hidden = low(jax.nn.gelu(gate_values, approximate=True) * up_values)
        return after_cross + low_back(product(hidden, down_w))
    result, pullback = jax.vjp(forward, inputs, encoded, params)
    grad_inputs, grad_encoded, grad_params = pullback(cotangent.astype(jnp.float32).reshape(-1, D))
    return (result.reshape(MICRO, ROWS * SEQ, D), grad_inputs.reshape(MICRO, ROWS * SEQ, D), grad_encoded.reshape(MICRO, ROWS * MEM, D), grad_params[0], grad_params[1], grad_params[2], grad_params[3], grad_params[4], grad_params[5], grad_params[6], grad_params[7], grad_params[8], grad_params[9], grad_params[10], grad_params[11], grad_params[12])
```

```python
import jax
import jax.numpy as jnp
from jax import lax
from jax.experimental import pallas as pl
from jax.experimental.pallas import tpu as pltpu
from jax.sharding import Mesh, PartitionSpec as P

HEADS = 16
HEAD_DIM = 64
BUCKETS = 32
KV_HEADS = 8
D = 1024
HALF = 512
SEQ = 1024
MEM = 512
BLOCK = 256

epsilon = 1e-06
masked_score = -1e30
scaling = HEAD_DIM ** (-0.5)

bf16 = jnp.bfloat16
f32 = jnp.float32

FFN = ("y", "xh", "c")
CHIPS = ("xl", "z", "y", "xh")
EVERY = ("xl", "z", "y", "xh", "c")


def dot(a, b):
    return lax.dot_general(a, b, (((1,), (0,)), ((), ())), preferred_element_type=f32)


def dot_nt(a, b):
    return lax.dot_general(a, b, (((1,), (1,)), ((), ())), preferred_element_type=f32)


def dot_tn(a, b):
    return lax.dot_general(a, b, (((0,), (0,)), ((), ())), preferred_element_type=f32)


def inverse_rms(a):
    return lax.rsqrt(jnp.mean(a * a, axis=-1, keepdims=True) + epsilon)


def norm_back(a, gain, e):
    n = inverse_rms(a)
    weighted = e * gain
    centre = jnp.mean(weighted * a, axis=-1, keepdims=True)
    grad_a = n * weighted - a * (n * n * n * centre)
    grad_gain = jnp.sum(e * a * n, axis=0, keepdims=True)
    return grad_a, grad_gain


def call(kernel, outs, *args, scratch=(), limit=48):
    return pl.pallas_call(
        kernel,
        out_shape=tuple(jax.ShapeDtypeStruct(s, t) for s, t in outs),
        scratch_shapes=list(scratch),
        compiler_params=pltpu.CompilerParams(vmem_limit_bytes=limit * 1024 * 1024),
    )(*args)


def to_all(x, axes):
    n = lax.axis_size(axes)
    return lax.all_to_all(jnp.broadcast_to(x[None], (n, *x.shape)), axes, 0, 0, tiled=True)


def exchange(x, axes):
    return lax.all_to_all(x, axes, 0, 0, tiled=True)


def sum_of_all(x, axes):
    return jnp.sum(exchange(x, axes).astype(f32), axis=0)


def swap_core(x):
    return lax.ppermute(x, "c", [(0, 1), (1, 0)])


def project_kernel(tok_ref, gain_ref, wq_ref, wkv_ref, out_ref, normed_ref):
    x = tok_ref[...].reshape(128, D).astype(f32)
    normed = (x * inverse_rms(x) * gain_ref[...]).astype(bf16)
    normed_ref[...] = normed
    for half in range(2):
        q = (dot(normed, wq_ref[half]) * scaling).astype(bf16)
        for k in range(8):
            one = q[:, k * 64 : (k + 1) * 64]
            out_ref[half * 8 + k, 0:64, :] = jnp.concatenate([one[0:64], one[64:128]], axis=1)
    keys = dot(normed, wkv_ref[0]).astype(bf16)
    values = dot(normed, wkv_ref[1]).astype(bf16)
    for n in range(KV_HEADS):
        both = jnp.concatenate(
            [keys[:, n * 64 : (n + 1) * 64], values[:, n * 64 : (n + 1) * 64]], axis=1
        )
        out_ref[2 * n, 64:192, :] = both
        out_ref[2 * n + 1, 64:192, :] = both


def bias_rows(onehot, table):
    return jnp.sum(onehot * table, axis=0, keepdims=True)


def self_kernel(qkv_ref, table_ref, turned_ref, seg_row_ref, seg_col_ref, out_ref, o_ref, p_ref):
    numbers = lax.broadcasted_iota(jnp.int32, (BUCKETS, SEQ), 0)
    onehot = (numbers == turned_ref[...]).astype(f32)
    terms = bias_rows(onehot, table_ref[...])
    bias = pltpu.roll(
        jnp.broadcast_to(terms, (BLOCK, SEQ)), 0, 1, stride=1, stride_axis=0
    )
    row = lax.broadcasted_iota(jnp.int32, (BLOCK, BLOCK), 0)
    col = lax.broadcasted_iota(jnp.int32, (BLOCK, BLOCK), 1)
    blocks = [jnp.where(col <= row, bias[:, 0:BLOCK], masked_score)]
    for k in range(1, 4):
        blocks.append(bias[:, SEQ - k * BLOCK : SEQ - (k - 1) * BLOCK])
    for mb in range(2):
        kv = qkv_ref[:, 64 + 64 * mb : 128 + 64 * mb, :].reshape(SEQ, 128)
        keys, values = kv[:, 0:64], kv[:, 64:128]
        for i in range(4):
            length = (i + 1) * BLOCK
            q = qkv_ref[4 * i : 4 * i + 4, 0:64, :].reshape(BLOCK, 128)
            q = q[:, mb * 64 : (mb + 1) * 64]
            s = dot_nt(q, keys[0:length])
            terms_here = jnp.concatenate([blocks[i - j] for j in range(i + 1)], axis=1)
            seg_q = seg_col_ref[mb, i * BLOCK : (i + 1) * BLOCK, :]
            seg_k = seg_row_ref[mb : mb + 1, 0:length]
            s = jnp.where(seg_q == seg_k, s + terms_here, masked_score)
            top = jnp.max(s, axis=-1, keepdims=True)
            e = jnp.exp(s - top)
            total = jnp.sum(e, axis=-1, keepdims=True)
            p = (e * (1.0 / total)).astype(bf16)
            p_ref[mb, i * BLOCK : (i + 1) * BLOCK, 0:length] = p
            o = dot(p, values[0:length])
            o_ref[i * BLOCK : (i + 1) * BLOCK, mb * 64 : (mb + 1) * 64] = o
            out_ref[4 * i : 4 * i + 4, :, mb * 64 : (mb + 1) * 64] = o.astype(bf16).reshape(
                4, 64, 64
            )


def self_back_kernel(qkv_ref, go_ref, o_ref, p_ref, turned_ref, out_ref, table_ref, diag_ref):
    diag_ref[...] = jnp.zeros_like(diag_ref)
    for mb in range(2):
        lanes = slice(mb * 64, (mb + 1) * 64)
        kv = qkv_ref[:, 64 + 64 * mb : 128 + 64 * mb, :].reshape(SEQ, 128)
        keys, values = kv[:, 0:64], kv[:, 64:128]
        grad_keys = [jnp.zeros((BLOCK, 64), f32) for _ in range(4)]
        grad_values = [jnp.zeros((BLOCK, 64), f32) for _ in range(4)]
        for i in range(4):
            length = (i + 1) * BLOCK
            q = qkv_ref[4 * i : 4 * i + 4, 0:64, :].reshape(BLOCK, 128)[:, lanes]
            go = go_ref[4 * i : 4 * i + 4, :, :].reshape(BLOCK, 128)[:, lanes]
            o = o_ref[i * BLOCK : (i + 1) * BLOCK, lanes]
            centre = jnp.sum(go.astype(f32) * o, axis=-1, keepdims=True)
            p = p_ref[mb, i * BLOCK : (i + 1) * BLOCK, 0:length]
            ds = p.astype(f32) * (dot_nt(go, values[0:length]) - centre)
            for j in range(i + 1):
                diag_ref[i - j] += ds[:, j * BLOCK : (j + 1) * BLOCK]
            ds = ds.astype(bf16)
            gq = (dot(ds, keys[0:length]) * scaling).astype(bf16)
            out_ref[4 * i : 4 * i + 4, 0:64, lanes] = gq.reshape(4, 64, 64)
            for j in range(i + 1):
                part = slice(j * BLOCK, (j + 1) * BLOCK)
                grad_keys[j] += dot_tn(ds[:, part], q)
                grad_values[j] += dot_tn(p[:, part], go)
        for j in range(4):
            both = jnp.concatenate([grad_keys[j], grad_values[j]], axis=1).astype(bf16)
            out_ref[4 * j : 4 * j + 4, 64 + 64 * mb : 128 + 64 * mb, :] = both.reshape(4, 64, 128)
    total = jnp.zeros((8, SEQ), f32)
    for g in range(BLOCK // 8):
        rows = slice(8 * g, 8 * g + 8)
        line = jnp.concatenate(
            [diag_ref[0, rows], diag_ref[3, rows], diag_ref[2, rows], diag_ref[1, rows]], axis=1
        )
        total = total + pltpu.roll(line, (SEQ - 8 * g) % SEQ, 1)
    sums = total[0:1]
    for s in range(1, 8):
        sums = sums + pltpu.roll(total[s : s + 1], SEQ - s, 1)
    numbers = lax.broadcasted_iota(jnp.int32, (BUCKETS, SEQ), 0)
    onehot = (numbers == turned_ref[...]).astype(f32)
    table_ref[...] = jnp.sum(onehot * sums, axis=1, keepdims=True)


def memory_kernel(mem_ref, w_ref, out_ref):
    for mb in range(2):
        rows = mem_ref[:, :, mb].reshape(MEM, D)
        keys = dot(rows, w_ref[0]).astype(bf16)
        values = dot(rows, w_ref[1]).astype(bf16)
        for n in range(KV_HEADS):
            part = slice(n * 64, (n + 1) * 64)
            out_ref[mb, n] = jnp.concatenate([keys[:, part], values[:, part]], axis=1)


def middle_kernel(
    att_ref, tok_ref, gain_cross_ref, gain_ffn_ref, wo_ref, wcq_ref, wco_ref, kv_ref,
    attended_ref, after_self_ref, normed_cross_ref, queries_ref, p_ref, crossed_ref,
    after_cross_ref, normed_ffn_ref,
):
    for h in range(HEADS):
        for mb in range(2):
            attended_ref[mb * 64 : (mb + 1) * 64, h * 64 : (h + 1) * 64] = att_ref[
                h, :, mb * 64 : (mb + 1) * 64
            ]
    attended = attended_ref[...]
    x = tok_ref[...].reshape(128, D).astype(f32)
    branch = jnp.concatenate([dot(attended, wo_ref[0]), dot(attended, wo_ref[1])], axis=1)
    after_self = x + branch
    after_self_ref[...] = after_self
    normed = (after_self * inverse_rms(after_self) * gain_cross_ref[...]).astype(bf16)
    normed_cross_ref[...] = normed
    for half in range(2):
        q = (dot(normed, wcq_ref[half]) * scaling).astype(bf16)
        queries_ref[:, half * HALF : (half + 1) * HALF] = q
    for mb in range(2):
        rows = slice(mb * 64, (mb + 1) * 64)
        for n in range(KV_HEADS):
            first = slice(2 * n * 64, (2 * n + 1) * 64)
            second = slice((2 * n + 1) * 64, (2 * n + 2) * 64)
            q = jnp.concatenate([queries_ref[rows, first], queries_ref[rows, second]], axis=0)
            kv = kv_ref[mb, n]
            s = dot_nt(q, kv[:, 0:64])
            e = jnp.exp(s - jnp.max(s, axis=-1, keepdims=True))
            p = (e * (1.0 / jnp.sum(e, axis=-1, keepdims=True))).astype(bf16)
            p_ref[mb, n] = p
            o = dot(p, kv[:, 64:128]).astype(bf16)
            crossed_ref[rows, first] = o[0:64]
            crossed_ref[rows, second] = o[64:128]
    crossed = crossed_ref[...]
    branch = jnp.concatenate([dot(crossed, wco_ref[0]), dot(crossed, wco_ref[1])], axis=1)
    after_cross = after_self + branch
    after_cross_ref[...] = after_cross
    normed_ffn_ref[...] = (
        after_cross * inverse_rms(after_cross) * gain_ffn_ref[...]
    ).astype(bf16)


def ffn_kernel(
    x_ref, g_ref, w_ref, back_ref, hidden_ref, grad_gate_ref, grad_up_ref, weights_ref
):
    for z in range(4):
        for xl in range(2):
            for xh in range(2):
                t = xl * 4 + z
                for k in range(3):
                    weights_ref[
                        k, xh * 176 : (xh + 1) * 176, t * 128 : (t + 1) * 128
                    ] = w_ref[z, xl, xh, k * 176 : (k + 1) * 176, :]

    def step(i, carry):
        rows = pl.ds(pl.multiple_of(i * 256, 256), 256)
        x, g = x_ref[rows, :], g_ref[rows, :]
        gate = dot_nt(x, weights_ref[0])
        up = dot_nt(x, weights_ref[1])
        grad_hidden = dot_nt(g, weights_ref[2])
        const = 0.7978845608028654
        inner = const * (gate + 0.044715 * gate * gate * gate)
        tanh = jnp.tanh(inner)
        gelu = 0.5 * gate * (1.0 + tanh)
        slope = 0.5 * (1.0 + tanh) + 0.5 * gate * (1.0 - tanh * tanh) * const * (
            1.0 + 3 * 0.044715 * gate * gate
        )
        hidden_ref[rows, :] = (gelu * up).astype(bf16)
        grad_gate = (grad_hidden * up * slope).astype(bf16)
        grad_up = (grad_hidden * gelu).astype(bf16)
        grad_gate_ref[rows, :] = grad_gate
        grad_up_ref[rows, :] = grad_up
        back = dot(grad_gate, weights_ref[0]) + dot(grad_up, weights_ref[1])
        back_ref[rows, :] = back.astype(bf16)
        return carry

    lax.fori_loop(0, 4, step, 0)


def ffn_out_kernel(hidden_ref, w_ref, out_ref):
    def step(i, carry):
        rows = pl.ds(pl.multiple_of(i * 256, 256), 256)
        out_ref[rows, :] = dot(hidden_ref[rows, :], w_ref[...]).astype(bf16)
        return carry

    lax.fori_loop(0, 4, step, 0)


def ffn_weights_kernel(x_ref, g_ref, hidden_ref, grad_gate_ref, grad_up_ref, out_ref):
    for t in range(8):
        xl, z = t // 4, t % 4
        cols = slice(t * 128, (t + 1) * 128)
        x, g = x_ref[:, cols], g_ref[:, cols]
        for k, (left, right) in enumerate(((grad_gate_ref, x), (grad_up_ref, x), (hidden_ref, g))):
            part = dot_tn(left[...], right).astype(bf16)
            for xh in range(2):
                out_ref[z, xl, xh, k * 176 : (k + 1) * 176, :] = part[
                    xh * 176 : (xh + 1) * 176
                ]


def middle_back_kernel(
    e_ref, cot_ref, after_cross_ref, after_self_ref, queries_ref, p_ref, kv_ref,
    gain_cross_ref, gain_ffn_ref, wo_ref, wcq_ref, wco_ref,
    att_ref, cross_branch_ref, grad_queries_ref, self_branch_ref, grad_kv_ref,
    grad_after_self_ref, gains_ref, grad_kv_packed_ref, grad_crossed_ref,
):
    grad_a, grad_gain = norm_back(after_cross_ref[...], gain_ffn_ref[...], e_ref[...])
    gains_ref[1:2, :] = grad_gain
    grad_after_cross = cot_ref[...].reshape(128, D).astype(f32) + grad_a
    branch = grad_after_cross.astype(bf16)
    cross_branch_ref[...] = branch
    grad_crossed_ref[...] = (
        dot_nt(branch[:, 0:HALF], wco_ref[0]) + dot_nt(branch[:, HALF:], wco_ref[1])
    ).astype(bf16)
    for mb in range(2):
        rows = slice(mb * 64, (mb + 1) * 64)
        for n in range(KV_HEADS):
            first = slice(2 * n * 64, (2 * n + 1) * 64)
            second = slice((2 * n + 1) * 64, (2 * n + 2) * 64)
            q = jnp.concatenate([queries_ref[rows, first], queries_ref[rows, second]], axis=0)
            go = jnp.concatenate(
                [grad_crossed_ref[rows, first], grad_crossed_ref[rows, second]], axis=0
            )
            kv = kv_ref[mb, n]
            p = p_ref[mb, n]
            wide = p.astype(f32)
            gp = dot_nt(go, kv[:, 64:128])
            centre = jnp.sum(wide * gp, axis=-1, keepdims=True)
            ds = (wide * (gp - centre)).astype(bf16)
            gq = (dot(ds, kv[:, 0:64]) * scaling).astype(bf16)
            grad_queries_ref[rows, first] = gq[0:64]
            grad_queries_ref[rows, second] = gq[64:128]
            gk = dot_tn(ds, q).astype(bf16)
            gv = dot_tn(p, go).astype(bf16)
            grad_kv_ref[mb, :, n * 64 : (n + 1) * 64] = gk
            grad_kv_ref[mb, :, HALF + n * 64 : HALF + (n + 1) * 64] = gv
    for mb in range(2):
        grad_kv_packed_ref[:, :, mb] = grad_kv_ref[mb].reshape(2, 8, 32, D)
    gq = grad_queries_ref[...]
    e = dot_nt(gq[:, 0:HALF], wcq_ref[0]) + dot_nt(gq[:, HALF:], wcq_ref[1])
    grad_a, grad_gain = norm_back(after_self_ref[...], gain_cross_ref[...], e)
    gains_ref[0:1, :] = grad_gain
    grad_after_self = grad_after_cross + grad_a
    grad_after_self_ref[...] = grad_after_self
    branch = grad_after_self.astype(bf16)
    self_branch_ref[...] = branch
    back = (dot_nt(branch[:, 0:HALF], wo_ref[0]) + dot_nt(branch[:, HALF:], wo_ref[1])).astype(bf16)
    for h in range(HEADS):
        one = back[:, h * 64 : (h + 1) * 64]
        att_ref[h] = jnp.concatenate([one[0:64], one[64:128]], axis=1)


def weights_kernel(
    attended_ref, self_branch_ref, normed_cross_ref, grad_queries_ref, crossed_ref,
    cross_branch_ref, mem_ref, grad_kv_ref, out_ref,
):
    for half in range(2):
        cols = slice(half * HALF, (half + 1) * HALF)
        out_ref[half, 0] = dot_tn(attended_ref[...], self_branch_ref[:, cols]).astype(bf16)
        out_ref[half, 1] = dot_tn(normed_cross_ref[...], grad_queries_ref[:, cols]).astype(bf16)
        out_ref[half, 3] = dot_tn(crossed_ref[...], cross_branch_ref[:, cols]).astype(bf16)
        total = None
        for mb in range(2):
            rows = mem_ref[:, :, mb].reshape(MEM, D)
            part = dot_tn(rows, grad_kv_ref[mb, :, cols])
            total = part if total is None else total + part
        out_ref[half, 2] = total.astype(bf16)


def last_kernel(
    back_ref, tok_ref, normed_ref, grad_after_self_ref, gain_ref, wq_ref, wkv_ref,
    grad_tok_ref, weights_ref, gain_out_ref, gq_ref, gk_ref, gv_ref,
):
    for h in range(HEADS):
        for mb in range(2):
            gq_ref[mb * 64 : (mb + 1) * 64, h * 64 : (h + 1) * 64] = back_ref[
                h, 0:64, mb * 64 : (mb + 1) * 64
            ]
    for n in range(KV_HEADS):
        both = back_ref[2 * n, 64:192, :].astype(f32) + back_ref[2 * n + 1, 64:192, :].astype(f32)
        both = both.astype(bf16)
        gk_ref[:, n * 64 : (n + 1) * 64] = both[:, 0:64]
        gv_ref[:, n * 64 : (n + 1) * 64] = both[:, 64:128]
    gq, gk, gv = gq_ref[...], gk_ref[...], gv_ref[...]
    e = dot_nt(gq[:, 0:HALF], wq_ref[0]) + dot_nt(gq[:, HALF:], wq_ref[1])
    e = e + dot_nt(gk, wkv_ref[0]) + dot_nt(gv, wkv_ref[1])
    x = tok_ref[...].reshape(128, D).astype(f32)
    grad_a, grad_gain = norm_back(x, gain_ref[...], e)
    gain_out_ref[...] = grad_gain
    grad_tok_ref[...] = (grad_after_self_ref[...] + grad_a).reshape(2, 64, D)
    normed = normed_ref[...]
    for half in range(2):
        cols = slice(half * HALF, (half + 1) * HALF)
        weights_ref[half, 0] = dot_tn(normed, gq[:, cols]).astype(bf16)
    weights_ref[0, 1] = dot_tn(normed, gk).astype(bf16)
    weights_ref[1, 1] = dot_tn(normed, gv).astype(bf16)


def on_device(
    tokens,
    memory,
    segment_ids,
    buckets,
    w_query,
    w_keyval,
    w_output,
    w_cross_query,
    w_cross_keyval,
    w_cross_output,
    norm_self,
    norm_cross,
    norm_ffn,
    bias_table,
    w_gate,
    w_up,
    w_down,
    cotangent,
):
    core = lax.axis_index("c")
    head = (lax.axis_index("y") * 2 + lax.axis_index("xh")) * 2 + core

    mem_chips = lax.all_gather(memory, ("y", "xh"), axis=0)
    mem_all = lax.all_gather(mem_chips, "c", axis=0)

    stacked = jnp.stack(
        [w_query, w_keyval, w_output, w_cross_query, w_cross_keyval, w_cross_output]
    )
    halves = jnp.moveaxis(stacked.reshape(6, 8, 2, HALF), 2, 0)
    rows = exchange(halves, "c")
    rows = jnp.moveaxis(rows, 0, 1).reshape(6, 16, HALF)

    ffn_rows = jnp.concatenate([w_gate.T, w_up.T, w_down], axis=0)
    later = jnp.concatenate([rows[2:].reshape(256, 128), ffn_rows], axis=0)
    along_x = to_all(later, ("xl", "xh"))

    small = jnp.concatenate([norm_self, norm_cross, norm_ffn, bias_table])
    small = jnp.pad(small, (0, 8 * HALF - small.shape[0])).reshape(8, HALF)
    first = jnp.concatenate([rows[0], rows[1], small], axis=0)
    first, along_x = lax.optimization_barrier((first, along_x))
    got = to_all(first, CHIPS)
    small = lax.all_gather(got[:, 32, 0:28], "c", axis=1).reshape(128, 28)
    gain_self = small[:, 0:8].reshape(1, D).astype(f32)
    gain_cross = small[:, 8:16].reshape(1, D).astype(f32)
    gain_ffn = small[:, 16:24].reshape(1, D).astype(f32)
    table = small[:, 24:28].reshape(HEADS, BUCKETS)
    table = lax.dynamic_slice_in_dim(table, head, 1, 0).astype(f32).reshape(BUCKETS, 1)
    pair = jnp.stack([got[:, 0:16].reshape(D, HALF), got[:, 16:32].reshape(D, HALF)])
    pair = lax.all_gather(pair, "c", axis=0)
    wq, wkv = pair[:, 0], pair[:, 1]

    other = lax.all_gather(along_x[:, 0:256], ("z", "y"), axis=0)
    other = other.reshape(4, 4, 2, 2, 4, 16, HALF)
    other = other.transpose(4, 2, 0, 1, 3, 5, 6).reshape(4, D, HALF)
    other = lax.all_gather(other, "c", axis=0)
    wo, wcq, wckv, wco = (other[:, k] for k in range(4))

    ffn_w = lax.all_gather(along_x[:, 256:], "z", axis=0).reshape(4, 2, 2, 528, 128)
    cot_all = lax.all_gather(cotangent.reshape(128, D), ("c", "y"), axis=0).reshape(1024, D)

    packed, normed_self = call(
        project_kernel,
        (((16, 192, 128), bf16), ((128, D), bf16)),
        tokens, gain_self, wq, wkv,
    )
    qkv = exchange(packed, FFN)
    turned = jnp.roll(buckets[::-1], 1).reshape(1, SEQ)
    att, o_self, p_self = call(
        self_kernel,
        (((16, 64, 128), bf16), ((SEQ, 128), f32), ((2, SEQ, SEQ), bf16)),
        qkv, table, turned, segment_ids, segment_ids.reshape(2, SEQ, 1),
    )
    att = exchange(att, FFN)

    (kv_mem,) = call(memory_kernel, (((2, 8, MEM, 128), bf16),), mem_all, wckv)
    (
        attended, after_self, normed_cross, queries, p_cross, crossed, after_cross, normed_ffn,
    ) = call(
        middle_kernel,
        (
            ((128, D), bf16), ((128, D), f32), ((128, D), bf16), ((128, D), bf16),
            ((2, 8, 128, MEM), bf16), ((128, D), bf16), ((128, D), f32), ((128, D), bf16),
        ),
        att, tokens, gain_cross, gain_ffn, wo, wcq, wco, kv_mem,
    )

    normed_all = lax.all_gather(to_all(normed_ffn, "y"), "c", axis=0).reshape(1024, D)
    back, hidden, grad_gate, grad_up, ffn_used = call(
        ffn_kernel,
        (
            ((1024, D), bf16), ((1024, 352), bf16), ((1024, 352), bf16), ((1024, 352), bf16),
            ((3, 352, D), bf16),
        ),
        normed_all, cot_all, ffn_w,
    )
    back = back.reshape(2, 4, 128, D)
    mine = lax.dynamic_index_in_dim(back, core, 0, keepdims=False)
    theirs = lax.dynamic_index_in_dim(back, 1 - core, 0, keepdims=False)
    back = (mine.astype(f32) + swap_core(theirs).astype(f32)).astype(bf16)
    grad_normed_ffn = sum_of_all(back, "y")

    (out_part,) = call(ffn_out_kernel, (((1024, D), bf16),), hidden, ffn_used[2])
    out = lax.psum_scatter(out_part, ("c", "y"), scatter_dimension=0, tiled=True)
    output = (after_cross + out.astype(f32)).reshape(2, 64, D)
    (ffn_grads,) = call(
        ffn_weights_kernel,
        (((4, 2, 2, 528, 128), bf16),),
        normed_all, cot_all, hidden, grad_gate, grad_up,
    )
    ffn_grads = lax.psum_scatter(
        ffn_grads.reshape(4 * 2112, 128), "z", scatter_dimension=0, tiled=True
    )

    (
        att, cross_branch, grad_queries, self_branch, grad_kv, grad_after_self, gain_grads,
        grad_kv_packed,
    ) = call(
        middle_back_kernel,
        (
            ((16, 64, 128), bf16), ((128, D), bf16), ((128, D), bf16), ((128, D), bf16),
            ((2, MEM, D), bf16), ((128, D), f32), ((2, D), f32), ((2, 8, 2, 32, D), bf16),
        ),
        grad_normed_ffn, cotangent, after_cross, after_self, queries, p_cross, kv_mem,
        gain_cross, gain_ffn, wo, wcq, wco,
        scratch=[pltpu.VMEM((128, D), bf16)],
    )
    go = exchange(att, FFN)

    back, grad_table = call(
        self_back_kernel,
        (((16, 192, 128), bf16), ((BUCKETS, 1), f32)),
        qkv, go, o_self, p_self, turned,
        scratch=[pltpu.VMEM((4, BLOCK, BLOCK), f32)],
    )
    back = exchange(back, FFN)
    grad_tokens, grads_first, gain_grad_self = call(
        last_kernel,
        (((2, 64, D), f32), ((2, 2, D, HALF), bf16), ((1, D), f32)),
        back, tokens, normed_self, grad_after_self, gain_self, wq, wkv,
        scratch=[pltpu.VMEM((128, D), bf16), pltpu.VMEM((128, HALF), bf16),
                 pltpu.VMEM((128, HALF), bf16)],
    )

    mine = lax.dynamic_index_in_dim(grad_kv_packed, core, 0, keepdims=False)
    theirs = lax.dynamic_index_in_dim(grad_kv_packed, 1 - core, 0, keepdims=False)
    grad_mem = (mine.astype(f32) + swap_core(theirs).astype(f32)).astype(bf16)
    grad_mem = lax.psum_scatter(
        grad_mem.reshape(8 * 64, D), ("y", "xh"), scatter_dimension=0, tiled=True
    )
    grad_memory = dot_nt(grad_mem[:, 0:HALF], wckv[0]) + dot_nt(grad_mem[:, HALF:], wckv[1])
    grad_memory = grad_memory.reshape(2, 32, D)

    (grads_other,) = call(
        weights_kernel,
        (((2, 4, D, HALF), bf16),),
        attended, self_branch, normed_cross, grad_queries, crossed, cross_branch, mem_all, grad_kv,
    )
    mine = lax.dynamic_index_in_dim(grads_other, core, 0, keepdims=False)
    theirs = lax.dynamic_index_in_dim(grads_other, 1 - core, 0, keepdims=False)
    both = (mine.astype(f32) + swap_core(theirs).astype(f32)).astype(bf16)
    both = both.reshape(4, 2, 4, 4, 2, 16, HALF)
    both = both.transpose(2, 3, 1, 4, 0, 5, 6).reshape(16 * 256, HALF)
    both = lax.psum_scatter(both, ("z", "y"), scatter_dimension=0, tiled=True)

    tail_x = jnp.concatenate(
        [both.reshape(4, 256, 128), ffn_grads.reshape(4, 528, 128)], axis=1
    )
    tail_x = sum_of_all(tail_x, ("xl", "xh"))
    rows_other = tail_x[0:256].reshape(4, 16, HALF)
    ffn_final = tail_x[256:]

    mine = lax.dynamic_index_in_dim(grads_first, core, 0, keepdims=False)
    theirs = lax.dynamic_index_in_dim(grads_first, 1 - core, 0, keepdims=False)
    both = (mine.astype(f32) + swap_core(theirs).astype(f32)).astype(bf16)
    both = both.reshape(2, 64, 16, HALF).transpose(1, 0, 2, 3).reshape(64, 32, HALF)
    table_all = jnp.where(
        jnp.arange(HEADS)[:, None] == head, grad_table.reshape(1, BUCKETS), 0.0
    ).reshape(64, 8)
    gains = jnp.concatenate([gain_grad_self, gain_grads], axis=0)
    gains = gains.reshape(3, 64, 16).transpose(1, 0, 2).reshape(64, 48)
    small = jnp.concatenate([gains, table_all], axis=1)
    small = small + swap_core(small)
    small = jnp.pad(small.astype(bf16), ((0, 0), (0, 8 * HALF - 56))).reshape(64, 8, HALF)
    first = sum_of_all(jnp.concatenate([both, small], axis=1), CHIPS)
    rows_first = first[0:32].reshape(2, 16, HALF)
    small = first[32, 0:56]

    rows = jnp.concatenate([rows_first, rows_other], axis=0)
    rows = exchange(jnp.moveaxis(rows.reshape(6, 2, 8, HALF), 1, 0), "c")
    rows = jnp.moveaxis(rows, 0, 2).reshape(6, 8, D)

    gains = small[0:48].reshape(3, 2, 8)
    gains = lax.dynamic_index_in_dim(gains, core, 1, keepdims=False)
    table_grad = lax.dynamic_index_in_dim(small[48:56].reshape(2, 4), core, 0, keepdims=False)
    return (
        output,
        grad_tokens,
        grad_memory,
        rows[0],
        rows[1],
        rows[2],
        rows[3],
        rows[4],
        rows[5],
        gains[0],
        gains[1],
        gains[2],
        table_grad,
        ffn_final[0:176].T,
        ffn_final[176:352].T,
        ffn_final[352:528],
    )


def solution(mesh):
    names = Mesh(mesh.devices.reshape(2, 4, 4, 2, 2), EVERY)
    tok, ffn, both = ("xl", "z"), FFN, EVERY
    big, mat, vec = P(None, both, None), P(both, None), P(both)
    fn = jax.shard_map(
        on_device,
        mesh=names,
        in_specs=(
            big, big, P(None, tok), P(), mat, mat, mat, mat, mat, mat, vec, vec, vec, vec,
            P(tok, ffn), P(tok, ffn), P(ffn, tok), big,
        ),
        out_specs=(
            big, big, big, mat, mat, mat, mat, mat, mat, vec, vec, vec, vec,
            P(tok, ffn), P(tok, ffn), P(ffn, tok),
        ),
        check_vma=False,
    )
    return fn
```

```python
import jax
import jax.numpy as jnp
from jax import lax
from jax.experimental import pallas as pl
from jax.experimental.pallas import tpu as pltpu
from jax.sharding import Mesh, PartitionSpec as P

HEADS = 16
HEAD_DIM = 64
BUCKETS = 32
KV_HEADS = 8
D = 1024
HALF = 512
SEQ = 1024
MEM = 512
BLOCK = 256

epsilon = 1e-06
masked_score = -1e30
scaling = HEAD_DIM ** (-0.5)

bf16 = jnp.bfloat16
f32 = jnp.float32

FFN = ("y", "xh", "c")
CHIPS = ("xl", "z", "y", "xh")
EVERY = ("xl", "z", "y", "xh", "c")


def dot(a, b):
    return lax.dot_general(a, b, (((1,), (0,)), ((), ())), preferred_element_type=f32)


def dot_nt(a, b):
    return lax.dot_general(a, b, (((1,), (1,)), ((), ())), preferred_element_type=f32)


def dot_tn(a, b):
    return lax.dot_general(a, b, (((0,), (0,)), ((), ())), preferred_element_type=f32)


def inverse_rms(a):
    return lax.rsqrt(jnp.mean(a * a, axis=-1, keepdims=True) + epsilon)


def norm_back(a, gain, e):
    n = inverse_rms(a)
    weighted = e * gain
    centre = jnp.mean(weighted * a, axis=-1, keepdims=True)
    grad_a = n * weighted - a * (n * n * n * centre)
    grad_gain = jnp.sum(e * a * n, axis=0, keepdims=True)
    return grad_a, grad_gain


class Mover:
    def __init__(self, arrived):
        self.arrived, self.copies, self.waited = arrived, [], []

    def start(self, source, target):
        number = len(self.copies)
        self.copies.append(pltpu.make_async_copy(source, target, self.arrived.at[number]))
        self.waited.append(False)
        self.copies[number].start()
        return number

    def wait(self, number):
        if not self.waited[number]:
            self.copies[number].wait()
            self.waited[number] = True

    def finish(self):
        for number in range(len(self.copies)):
            self.wait(number)


class Near:
    def __init__(self, mover, source, target):
        self.mover, self.target = mover, target
        self.number = mover.start(source, target)

    def here(self):
        self.mover.wait(self.number)
        return self.target


COPIES = 64


def call(kernel, outs, *args, raw=(), small=(), scratch=(), us=5, core=None, after=(), raw_outs=()):
    far, near = pl.BlockSpec(memory_space=pltpu.HBM), pl.BlockSpec(memory_space=pltpu.VMEM)
    operands = [*after, *args, *raw, *small]
    specs = [far] * (len(after) + len(args) + len(raw)) + [near] * len(small)
    leading = 0
    if core is not None:
        leading = 1
        operands = [core, *operands]
        specs = [pl.BlockSpec(memory_space=pltpu.SMEM), *specs]
    buffers = [pltpu.VMEM(x.shape, x.dtype) for x in args]
    buffers += [pltpu.VMEM(shape, dtype) for shape, dtype in outs]

    def body(*refs):
        refs = list(refs)
        take = lambda count: [refs.pop(0) for _ in range(count)]
        places = take(leading)
        take(len(after))
        sources, raws, smalls = take(len(args)), take(len(raw)), take(len(small))
        results, raw_results = take(len(outs)), take(len(raw_outs))
        own = take(len(scratch))
        targets, leaving = take(len(args)), take(len(outs))
        mover = Mover(refs.pop(0))
        sent = {}

        def send(number):
            if number not in sent:
                sent[number] = mover.start(leaving[number], results[number])

        mover.send = send
        nears = [Near(mover, *pair) for pair in zip(sources, targets)]
        kernel(mover, *places, *nears, *raws, *smalls, *leaving, *raw_results, *own)
        for number in range(len(outs)):
            send(number)
        mover.finish()

    return pl.pallas_call(
        body,
        out_shape=tuple(jax.ShapeDtypeStruct(s, t) for s, t in (*outs, *raw_outs)),
        in_specs=specs,
        out_specs=tuple([far] * (len(outs) + len(raw_outs))),
        scratch_shapes=[*scratch, *buffers, pltpu.SemaphoreType.DMA((COPIES,))],
        cost_estimate=pl.CostEstimate(
            flops=us * 400_000_000, bytes_accessed=us * 3_000_000, transcendentals=0
        ),
        compiler_params=pltpu.CompilerParams(vmem_limit_bytes=60 * 1024 * 1024),
    )(*operands)


def to_all(x, axes):
    n = lax.axis_size(axes)
    return lax.all_to_all(jnp.broadcast_to(x[None], (n, *x.shape)), axes, 0, 0, tiled=True)


def exchange(x, axes):
    return lax.all_to_all(x, axes, 0, 0, tiled=True)


def sum_of_all(x, axes):
    return jnp.sum(exchange(x, axes).astype(f32), axis=0)


def swap_core(x):
    return lax.ppermute(x, "c", [(0, 1), (1, 0)])


def flips_x(parts):
    flip_high = lax.ppermute(parts[0], "xh", [(0, 1), (1, 0)])
    flip_low = lax.ppermute(parts[1], "xl", [(0, 1), (1, 0)])
    flip_both = lax.ppermute(parts[2], ("xl", "xh"), [(0, 3), (1, 2), (2, 1), (3, 0)])
    return flip_high, flip_low, flip_both


def at_place(x, place):
    return lax.dynamic_index_in_dim(x, place, 0, keepdims=False)


def sum_over_x(x, x_at):
    found = flips_x([at_place(x, x_at ^ k) for k in range(1, 4)])
    total = at_place(x, x_at).astype(f32)
    for part in found:
        total = total + part.astype(f32)
    return total


def prepare_kernel(mover, core_ref, *refs):
    inputs, (kept_ref, given_ref, ffn_ref) = refs[0:9], refs[9:12]
    inputs = [x.here() for x in inputs]
    first = core_ref[0] == 0
    for k in range(6):
        left, right = inputs[k][:, 0:HALF], inputs[k][:, HALF:]
        kept_ref[k] = jnp.where(first, left, right)
        given_ref[k] = jnp.where(first, right, left)
    for k in range(3):
        ffn_ref[:, k * 128 : (k + 1) * 128] = inputs[6 + k][...]
    ffn_ref[:, 384:] = jnp.zeros((176, 128), bf16)


def arrange_kernel(mover, core_ref, kept, given, small, ffn, later_ref, first_ref, row_ref):
    is_first = core_ref[0] == 0
    kept_ref, given_ref = kept.here(), given.here()
    for k in range(6):
        pair = [kept_ref[k].astype(f32), given_ref[k].astype(f32)]
        pair = jnp.where(
            is_first, jnp.concatenate(pair, axis=0), jnp.concatenate(pair[::-1], axis=0)
        ).astype(bf16)
        if k < 2:
            row_ref[16 * k : 16 * k + 16, 0:HALF] = pair
        else:
            later_ref[16 * (k - 2) : 16 * (k - 2) + 16, :] = pair
    row_ref[:, HALF:] = jnp.broadcast_to(small.here()[0:1, :], (32, 128))
    for p in range(16):
        mover.start(row_ref, first_ref.at[p])
    later_ref[64:240, :] = ffn.here()[...]


def spread_kernel(mover, core_ref, own, high, low, both, memory, other_ref, ffn_ref, memory_8_ref):
    x_at = core_ref[2]
    refs = [x.here() for x in (own, high, low, both)]
    for k, ref in enumerate(refs):
        other_ref[x_at ^ k] = ref[0:64, :]
        ffn_ref[x_at ^ k] = ref[64:240, 0:384]
    mover.send(0)
    mover.send(1)
    memory_ref = memory.here()
    for p in range(8):
        mover.start(memory_ref, memory_8_ref.at[p])


def start_place(mover, core, mine_ref, theirs_ref, weights_ref, which):
    numbers = []
    for at, k in enumerate(which):
        numbers.append([])
        for x in range(4):
            xl, xh = x // 2, x % 2
            rows = pl.ds(16 * k, 16)
            for half, ref in ((core, mine_ref), (1 - core, theirs_ref)):
                numbers[-1].append(
                    mover.start(ref.at[:, x, rows, :], weights_ref.at[half, at, xl, :, xh])
                )
    return numbers


def start_place_first(mover, core, x_at, mine_refs, theirs_refs, weights_ref):
    numbers = []
    for at in range(2):
        numbers.append([])
        rows = pl.ds(16 * at, 16)
        for flip in range(4):
            x = x_at ^ flip
            for half, refs in ((core, mine_refs), (1 - core, theirs_refs)):
                target = weights_ref.at[half, at, x // 2, :, x % 2]
                source = refs[flip].at[:, rows, pl.ds(0, HALF)]
                numbers[-1].append(mover.start(source, target))
    return numbers


def placed_halves(mover, weights_ref, at, numbers):
    for number in numbers[at]:
        mover.wait(number)
    return [half_of(weights_ref, at, half) for half in range(2)]


def half_of(weights_ref, at, half):
    return weights_ref[half, at].reshape(D, HALF)


def iotas(rows, cols):
    return [lax.broadcasted_iota(jnp.int32, (rows, cols), k) for k in range(2)]


def one_hot(condition):
    return condition.astype(f32).astype(bf16)


def lanes_of(core, k):
    d, lane = iotas(D, 128)
    return one_hot((lane == 8 * k + d % 8) & ((d // 8) % 2 == core))


def chip_of():
    p, d = iotas(64, D)
    return d // 16 == p


def chip_along(p):
    x, zy = p // 16, p % 16
    return (x // 2) * 32 + zy * 2 + x % 2


def project_kernel(mover, core_ref, tok, *refs):
    mine_refs, theirs_refs = refs[0:4], refs[4:8]
    out_ref, normed_ref, gains_ref, table_ref, weights_ref, small_ref = refs[8:]
    core, head, x_at = (core_ref[k] for k in range(3))
    arrivals = []
    for c, sources in enumerate((mine_refs, theirs_refs)):
        for flip in range(4):
            source = sources[flip].at[:, pl.ds(0, 16), pl.ds(HALF, 128)]
            arrivals.append(mover.start(source, small_ref.at[c, x_at ^ flip]))
    numbers = start_place_first(mover, core, x_at, mine_refs, theirs_refs, weights_ref)
    for number in arrivals:
        mover.wait(number)
    smalls = [(core, small_ref[0, :, :, 0:1, :]), (1 - core, small_ref[1, :, :, 0:1, :])]
    smalls = [(c, small.reshape(64, 128)) for c, small in smalls]
    p, d = iotas(64, D)
    own_chip = d // 16 == chip_along(p)
    gains = []
    for k in range(3):
        spread = sum(dot_nt(small, lanes_of(c, k)) for c, small in smalls)
        gains.append(jnp.sum(jnp.where(own_chip, spread, 0.0), axis=0, keepdims=True))
        gains_ref[k : k + 1, :] = gains[-1]
    b, p = iotas(BUCKETS, 64)
    chips = one_hot(chip_along(p) == head * 4 + b // 8)
    b, lane = iotas(BUCKETS, 128)
    column = jnp.zeros((BUCKETS, 1), f32)
    for c, small in smalls:
        hit = (lane == 24 + b % 4) & ((b // 4) % 2 == c)
        found = jnp.where(hit, dot(chips, small), 0.0)
        column = column + jnp.sum(found, axis=1, keepdims=True)
    table_ref[...] = jnp.broadcast_to(column, (BUCKETS, 128))
    mover.send(2)
    mover.send(3)

    x = tok.here()[...].reshape(128, D).astype(f32)
    normed = (x * inverse_rms(x) * gains[0]).astype(bf16)
    normed_ref[...] = normed
    mover.send(1)
    wq = placed_halves(mover, weights_ref, 0, numbers)
    for half in range(2):
        q = (dot(normed, wq[half]) * scaling).astype(bf16)
        for k in range(8):
            one = q[:, k * 64 : (k + 1) * 64]
            out_ref[half * 8 + k, 0:64, :] = jnp.concatenate([one[0:64], one[64:128]], axis=1)
    wkv = placed_halves(mover, weights_ref, 1, numbers)
    keys = dot(normed, wkv[0]).astype(bf16)
    values = dot(normed, wkv[1]).astype(bf16)
    for n in range(KV_HEADS):
        both = jnp.concatenate(
            [keys[:, n * 64 : (n + 1) * 64], values[:, n * 64 : (n + 1) * 64]], axis=1
        )
        out_ref[2 * n, 64:192, :] = both
        out_ref[2 * n + 1, 64:192, :] = both


def bias_rows(onehot, table):
    return jnp.sum(onehot * table, axis=0, keepdims=True)


def self_kernel(
    mover, qkv, table, other, turned_ref, seg_ref, out_ref, o_ref, p_ref, other_out_ref
):
    numbers = lax.broadcasted_iota(jnp.int32, (BUCKETS, SEQ), 0)
    onehot = (numbers == turned_ref[...]).astype(f32)
    terms = bias_rows(onehot, table.here()[:, 0:1])
    bias = pltpu.roll(
        jnp.broadcast_to(terms, (BLOCK, SEQ)), 0, 1, stride=1, stride_axis=0
    )
    row = lax.broadcasted_iota(jnp.int32, (BLOCK, BLOCK), 0)
    col = lax.broadcasted_iota(jnp.int32, (BLOCK, BLOCK), 1)
    blocks = [jnp.where(col <= row, bias[:, 0:BLOCK], masked_score)]
    for k in range(1, 4):
        blocks.append(bias[:, SEQ - k * BLOCK : SEQ - (k - 1) * BLOCK])
    same_place = row == col
    qkv_ref = qkv.here()
    for mb in range(2):
        kv = qkv_ref[:, 64 + 64 * mb : 128 + 64 * mb, :].reshape(SEQ, 128)
        keys, values = kv[:, 0:64], kv[:, 64:128]
        segments = seg_ref[mb : mb + 1, :].astype(f32)
        for i in range(4):
            length = (i + 1) * BLOCK
            q = qkv_ref[4 * i : 4 * i + 4, 0:64, :].reshape(BLOCK, 128)
            q = q[:, mb * 64 : (mb + 1) * 64]
            s = dot_nt(q, keys[0:length])
            terms_here = jnp.concatenate([blocks[i - j] for j in range(i + 1)], axis=1)
            seg_q = jnp.where(same_place, segments[:, i * BLOCK : (i + 1) * BLOCK], 0.0)
            seg_q = jnp.sum(seg_q, axis=1, keepdims=True)
            s = jnp.where(seg_q == segments[:, 0:length], s + terms_here, masked_score)
            top = jnp.max(s, axis=-1, keepdims=True)
            e = jnp.exp(s - top)
            total = jnp.sum(e, axis=-1, keepdims=True)
            p = (e * (1.0 / total)).astype(bf16)
            p_ref[mb, i * BLOCK : (i + 1) * BLOCK, 0:length] = p
            o = dot(p, values[0:length])
            o_ref[i * BLOCK : (i + 1) * BLOCK, mb * 64 : (mb + 1) * 64] = o
            out_ref[4 * i : 4 * i + 4, :, mb * 64 : (mb + 1) * 64] = o.astype(bf16).reshape(
                4, 64, 64
            )
        if mb == 0:
            mover.start(other.here(), other_out_ref)


def self_back_kernel(
    mover, go, qkv, o, p_all, turned_ref, out_ref, table_ref, diag_ref
):
    diag_ref[...] = jnp.zeros_like(diag_ref)
    qkv_ref, go_ref, o_ref, p_ref = qkv.here(), go.here(), o.here(), p_all.here()
    for mb in range(2):
        lanes = slice(mb * 64, (mb + 1) * 64)
        kv = qkv_ref[:, 64 + 64 * mb : 128 + 64 * mb, :].reshape(SEQ, 128)
        keys, values = kv[:, 0:64], kv[:, 64:128]
        grad_keys = [jnp.zeros((BLOCK, 64), f32) for _ in range(4)]
        grad_values = [jnp.zeros((BLOCK, 64), f32) for _ in range(4)]
        for i in range(4):
            length = (i + 1) * BLOCK
            q = qkv_ref[4 * i : 4 * i + 4, 0:64, :].reshape(BLOCK, 128)[:, lanes]
            go = go_ref[4 * i : 4 * i + 4, :, :].reshape(BLOCK, 128)[:, lanes]
            o = o_ref[i * BLOCK : (i + 1) * BLOCK, lanes]
            centre = jnp.sum(go.astype(f32) * o, axis=-1, keepdims=True)
            p = p_ref[mb, i * BLOCK : (i + 1) * BLOCK, 0:length]
            ds = p.astype(f32) * (dot_nt(go, values[0:length]) - centre)
            for j in range(i + 1):
                diag_ref[i - j] += ds[:, j * BLOCK : (j + 1) * BLOCK]
            ds = ds.astype(bf16)
            gq = (dot(ds, keys[0:length]) * scaling).astype(bf16)
            out_ref[4 * i : 4 * i + 4, 0:64, lanes] = gq.reshape(4, 64, 64)
            for j in range(i + 1):
                part = slice(j * BLOCK, (j + 1) * BLOCK)
                grad_keys[j] += dot_tn(ds[:, part], q)
                grad_values[j] += dot_tn(p[:, part], go)
        for j in range(4):
            both = jnp.concatenate([grad_keys[j], grad_values[j]], axis=1).astype(bf16)
            out_ref[4 * j : 4 * j + 4, 64 + 64 * mb : 128 + 64 * mb, :] = both.reshape(4, 64, 128)
    mover.send(0)
    total = jnp.zeros((8, SEQ), f32)
    for g in range(BLOCK // 8):
        rows = slice(8 * g, 8 * g + 8)
        line = jnp.concatenate(
            [diag_ref[0, rows], diag_ref[3, rows], diag_ref[2, rows], diag_ref[1, rows]], axis=1
        )
        total = total + pltpu.roll(line, (SEQ - 8 * g) % SEQ, 1)
    sums = total[0:1]
    for s in range(1, 8):
        sums = sums + pltpu.roll(total[s : s + 1], SEQ - s, 1)
    numbers = lax.broadcasted_iota(jnp.int32, (BUCKETS, SEQ), 0)
    onehot = (numbers == turned_ref[...]).astype(f32)
    sums = jnp.sum(onehot * sums, axis=1, keepdims=True)
    table_ref[...] = jnp.broadcast_to(sums, (BUCKETS, 128))


def memory_kernel(mover, core_ref, mem, mem2, mine_ref, theirs_ref, out_ref, weights_ref):
    numbers = start_place(mover, core_ref[0], mine_ref, theirs_ref, weights_ref, (2,))
    mem_ref, mem2_ref = mem.here(), mem2.here()
    wckv = placed_halves(mover, weights_ref, 0, numbers)
    for mb in range(2):
        rows = jnp.concatenate(
            [mem_ref[:, mb].reshape(256, D), mem2_ref[:, mb].reshape(256, D)], axis=0
        )
        keys = dot(rows, wckv[0]).astype(bf16)
        values = dot(rows, wckv[1]).astype(bf16)
        for n in range(KV_HEADS):
            part = slice(n * 64, (n + 1) * 64)
            out_ref[mb, n] = jnp.concatenate([keys[:, part], values[:, part]], axis=1)


def middle_kernel(
    mover, core_ref, att, tok, gains, kv_all, mine_ref, theirs_ref,
    lefts_ref, after_self_ref, queries_ref, p_ref, after_cross_ref, normed_ffn_ref,
    weights_ref, normed_row_ref,
):
    numbers = start_place(mover, core_ref[0], mine_ref, theirs_ref, weights_ref, (0, 1, 3))
    attended_ref, normed_cross_ref, crossed_ref = (lefts_ref.at[k] for k in range(3))
    att_ref, tok_ref, gains_ref = att.here(), tok.here(), gains.here()
    for h in range(HEADS):
        for mb in range(2):
            attended_ref[mb * 64 : (mb + 1) * 64, h * 64 : (h + 1) * 64] = att_ref[
                h, :, mb * 64 : (mb + 1) * 64
            ]
    attended = attended_ref[...]
    x = tok_ref[...].reshape(128, D).astype(f32)
    wo = placed_halves(mover, weights_ref, 0, numbers)
    after_self = x + jnp.concatenate([dot(attended, wo[0]), dot(attended, wo[1])], axis=1)
    after_self_ref[...] = after_self
    mover.send(1)
    normed = (after_self * inverse_rms(after_self) * gains_ref[1:2, :]).astype(bf16)
    normed_cross_ref[...] = normed
    wcq = placed_halves(mover, weights_ref, 1, numbers)
    for half in range(2):
        q = (dot(normed, wcq[half]) * scaling).astype(bf16)
        queries_ref[:, half * HALF : (half + 1) * HALF] = q
    mover.send(2)
    kv_ref = kv_all.here()
    for mb in range(2):
        rows = slice(mb * 64, (mb + 1) * 64)
        for n in range(KV_HEADS):
            first = slice(2 * n * 64, (2 * n + 1) * 64)
            second = slice((2 * n + 1) * 64, (2 * n + 2) * 64)
            q = jnp.concatenate([queries_ref[rows, first], queries_ref[rows, second]], axis=0)
            kv = kv_ref[mb, n]
            s = dot_nt(q, kv[:, 0:64])
            e = jnp.exp(s - jnp.max(s, axis=-1, keepdims=True))
            p = (e * (1.0 / jnp.sum(e, axis=-1, keepdims=True))).astype(bf16)
            p_ref[mb, n] = p
            o = dot(p, kv[:, 64:128]).astype(bf16)
            crossed_ref[rows, first] = o[0:64]
            crossed_ref[rows, second] = o[64:128]
    mover.send(3)
    mover.send(0)
    crossed = crossed_ref[...]
    wco = placed_halves(mover, weights_ref, 2, numbers)
    after_cross = after_self + jnp.concatenate([dot(crossed, wco[0]), dot(crossed, wco[1])], axis=1)
    after_cross_ref[...] = after_cross
    mover.send(4)
    normed = after_cross * inverse_rms(after_cross) * gains_ref[2:3, :]
    normed_row_ref[...] = normed.astype(bf16)
    for k in range(4):
        mover.start(normed_row_ref, normed_ffn_ref.at[k])


def ffn_kernel(
    mover, w, g, g2, x, x2,
    back_ref, back2_ref, hidden_ref, grad_gate_ref, grad_up_ref, weights_ref,
):
    w_ref = w.here()
    for z in range(4):
        for along in range(4):
            t = (along // 2) * 4 + z
            rows = slice((along % 2) * 176, (along % 2) * 176 + 176)
            for k in range(3):
                weights_ref[k, rows, t * 128 : (t + 1) * 128] = w_ref[
                    z, along, :, k * 128 : (k + 1) * 128
                ]

    def tokens(at, x, g, rows, back_ref):
        gate = dot_nt(x, weights_ref[0])
        up = dot_nt(x, weights_ref[1])
        grad_hidden = dot_nt(g, weights_ref[2])
        const = 0.7978845608028654
        inner = const * (gate + 0.044715 * gate * gate * gate)
        tanh = jnp.tanh(inner)
        gelu = 0.5 * gate * (1.0 + tanh)
        slope = 0.5 * (1.0 + tanh) + 0.5 * gate * (1.0 - tanh * tanh) * const * (
            1.0 + 3 * 0.044715 * gate * gate
        )
        hidden_ref[at, rows, :] = (gelu * up).astype(bf16)
        grad_gate = (grad_hidden * up * slope).astype(bf16)
        grad_up = (grad_hidden * gelu).astype(bf16)
        grad_gate_ref[at, rows, :] = grad_gate
        grad_up_ref[at, rows, :] = grad_up
        back = dot(grad_gate, weights_ref[0]) + dot(grad_up, weights_ref[1])
        back_ref[rows, :] = back.astype(bf16)

    mover.send(5)
    sides = ((x2, g2, back2_ref, 1), (x, g, back_ref, 0))
    for x, g, back, at in sides:
        x, g = x.here(), g.here()

        def step(i, carry, at=at, x=x, g=g, back=back):
            rows = pl.ds(pl.multiple_of(i * 256, 256), 256)
            tokens(at, x[rows, :], g[rows, :], rows, back)
            return carry

        lax.fori_loop(0, 2, step, 0)
        mover.send(at)


def ffn_rest_kernel(
    mover, hidden, weights, x, x2, g, g2, grad_gate, grad_up, out2_ref, out_ref, grads_ref
):
    hidden_ref, weights_ref = hidden.here(), weights.here()
    for at, ref in ((1, out2_ref), (0, out_ref)):
        ref[...] = dot(hidden_ref[at], weights_ref[2]).astype(bf16)
        mover.send(1 - at)
    x_ref, x2_ref, g_ref, g2_ref = (ref.here() for ref in (x, x2, g, g2))
    grad_gate_ref, grad_up_ref = grad_gate.here(), grad_up.here()
    for t in range(8):
        xl, z = t // 4, t % 4
        cols = slice(t * 128, (t + 1) * 128)
        sides = ((grad_gate_ref, x_ref, x2_ref), (grad_up_ref, x_ref, x2_ref),
                 (hidden_ref, g_ref, g2_ref))
        for k, (left, right, right2) in enumerate(sides):
            part = dot_tn(left[0], right[:, cols]) + dot_tn(left[1], right2[:, cols])
            part = part.astype(bf16)
            for xh in range(2):
                grads_ref[z, xl * 2 + xh, :, k * 128 : (k + 1) * 128] = part[
                    xh * 176 : (xh + 1) * 176
                ]


def middle_back_kernel(
    mover, core_ref, parts, cot, after_cross, gains, kv_all, queries, p_all, after_self,
    mine_ref, theirs_ref,
    att_ref, rights_ref, grad_kv_ref, grad_after_self_ref, grad_gains_ref,
    grad_crossed_ref, weights_ref,
):
    numbers = start_place(mover, core_ref[0], mine_ref, theirs_ref, weights_ref, (3, 1, 0))
    self_branch_ref, grad_queries_ref, cross_branch_ref = (rights_ref.at[k] for k in range(3))
    parts_ref, gains_ref = parts.here(), gains.here()
    e = parts_ref[0].astype(f32)
    for k in range(1, 4):
        e = e + parts_ref[k].astype(f32)
    grad_a, grad_gain = norm_back(after_cross.here()[...], gains_ref[2:3, :], e)
    grad_gains_ref[1:2, :] = grad_gain
    grad_after_cross = cot.here()[...].reshape(128, D).astype(f32) + grad_a
    branch = grad_after_cross.astype(bf16)
    cross_branch_ref[...] = branch
    wco = placed_halves(mover, weights_ref, 0, numbers)
    grad_crossed_ref[...] = (
        dot_nt(branch[:, 0:HALF], wco[0]) + dot_nt(branch[:, HALF:], wco[1])
    ).astype(bf16)
    queries_ref, p_ref, kv_ref = queries.here(), p_all.here(), kv_all.here()
    for mb in range(2):
        rows = slice(mb * 64, (mb + 1) * 64)
        for n in range(KV_HEADS):
            first = slice(2 * n * 64, (2 * n + 1) * 64)
            second = slice((2 * n + 1) * 64, (2 * n + 2) * 64)
            q = jnp.concatenate([queries_ref[rows, first], queries_ref[rows, second]], axis=0)
            go = jnp.concatenate(
                [grad_crossed_ref[rows, first], grad_crossed_ref[rows, second]], axis=0
            )
            kv = kv_ref[mb, n]
            p = p_ref[mb, n]
            wide = p.astype(f32)
            gp = dot_nt(go, kv[:, 64:128])
            centre = jnp.sum(wide * gp, axis=-1, keepdims=True)
            ds = (wide * (gp - centre)).astype(bf16)
            gq = (dot(ds, kv[:, 0:64]) * scaling).astype(bf16)
            grad_queries_ref[rows, first] = gq[0:64]
            grad_queries_ref[rows, second] = gq[64:128]
            gk = dot_tn(ds, q).astype(bf16).reshape(2, 8, 32, 64)
            gv = dot_tn(p, go).astype(bf16).reshape(2, 8, 32, 64)
            grad_kv_ref[:, :, mb, :, n * 64 : (n + 1) * 64] = gk
            grad_kv_ref[:, :, mb, :, HALF + n * 64 : HALF + (n + 1) * 64] = gv
    mover.send(2)
    gq = grad_queries_ref[...]
    wcq = placed_halves(mover, weights_ref, 1, numbers)
    e = dot_nt(gq[:, 0:HALF], wcq[0]) + dot_nt(gq[:, HALF:], wcq[1])
    grad_a, grad_gain = norm_back(after_self.here()[...], gains_ref[1:2, :], e)
    grad_gains_ref[0:1, :] = grad_gain
    grad_after_self = grad_after_cross + grad_a
    grad_after_self_ref[...] = grad_after_self
    mover.send(3)
    branch = grad_after_self.astype(bf16)
    self_branch_ref[...] = branch
    mover.send(1)
    wo = placed_halves(mover, weights_ref, 2, numbers)
    back = (dot_nt(branch[:, 0:HALF], wo[0]) + dot_nt(branch[:, HALF:], wo[1])).astype(bf16)
    for h in range(HEADS):
        one = back[:, h * 64 : (h + 1) * 64]
        att_ref[h] = jnp.concatenate([one[0:64], one[64:128]], axis=1)


def half_columns(core, x):
    return jnp.where(core == 0, x[:, 0:HALF], x[:, HALF:])


def weights_kernel(
    mover, core_ref, lefts, lefts2, rights, rights2, mem, mem2, grad_kv, grad_kv2,
    out_ref,
):
    core = core_ref[0]
    rights_ref, rights2_ref = rights.here(), rights2.here()
    lefts_ref, lefts2_ref = lefts.here(), lefts2.here()

    def put(k, whole):
        whole = whole.astype(bf16).reshape(2, 16, 2, 16, HALF)
        for x in range(4):
            out_ref[:, x, 16 * k : 16 * k + 16, :] = whole[x // 2, :, x % 2]

    for k, at in enumerate((0, 1, 3)):
        left = jnp.concatenate([lefts_ref[k], lefts2_ref[k]], axis=0)
        right = jnp.concatenate(
            [half_columns(core, rights_ref[k]), half_columns(core, rights2_ref[k])], axis=0
        )
        put(at, dot_tn(left, right))
    total = jnp.zeros((D, HALF), f32)
    kv_ref, kv2_ref = grad_kv.here(), grad_kv2.here()
    for at, mem_ref in enumerate((mem.here(), mem2.here())):
        own = half_columns(core, kv_ref[at].reshape(512, D)).astype(f32)
        both = own + half_columns(core, kv2_ref[1 - at].reshape(512, D)).astype(f32)
        total = total + dot_tn(mem_ref[...].reshape(512, D), both.astype(bf16))
    put(2, total)


def memory_back_kernel(mover, core_ref, parts, mine_ref, theirs_ref, out_ref, weights_ref):
    numbers = start_place(mover, core_ref[0], mine_ref, theirs_ref, weights_ref, (2,))
    parts_ref = parts.here()
    grad = parts_ref[0].astype(f32)
    for k in range(1, 8):
        grad = grad + parts_ref[k].astype(f32)
    grad = grad.reshape(64, D).astype(bf16)
    wckv = placed_halves(mover, weights_ref, 0, numbers)
    whole = dot_nt(grad[:, 0:HALF], wckv[0]) + dot_nt(grad[:, HALF:], wckv[1])
    out_ref[...] = whole.reshape(2, 32, D)


def unpack(back_ref, out_ref):
    for h in range(HEADS):
        for mb in range(2):
            out_ref[0, mb * 64 : (mb + 1) * 64, h * 64 : (h + 1) * 64] = back_ref[
                h, 0:64, mb * 64 : (mb + 1) * 64
            ]
    for n in range(KV_HEADS):
        both = back_ref[2 * n, 64:192, :].astype(f32) + back_ref[2 * n + 1, 64:192, :].astype(f32)
        both = both.astype(bf16)
        out_ref[1, :, n * 64 : (n + 1) * 64] = both[:, 0:64]
        out_ref[1, :, HALF + n * 64 : HALF + (n + 1) * 64] = both[:, 64:128]


def last_kernel(mover, core_ref, back, tok, grad_after_self, gains, *refs):
    mine_refs, theirs_refs = refs[0:4], refs[4:8]
    rights_ref, grad_tok_ref, gain_out_ref, weights_ref = refs[8:]
    numbers = start_place_first(
        mover, core_ref[0], core_ref[2], mine_refs, theirs_refs, weights_ref
    )
    unpack(back.here(), rights_ref)
    mover.send(0)
    gq, gkv = rights_ref[0], rights_ref[1]
    wq = placed_halves(mover, weights_ref, 0, numbers)
    e = dot_nt(gq[:, 0:HALF], wq[0]) + dot_nt(gq[:, HALF:], wq[1])
    wkv = placed_halves(mover, weights_ref, 1, numbers)
    e = e + dot_nt(gkv[:, 0:HALF], wkv[0]) + dot_nt(gkv[:, HALF:], wkv[1])
    x = tok.here()[...].reshape(128, D).astype(f32)
    grad_a, grad_gain = norm_back(x, gains.here()[0:1, :], e)
    gain_out_ref[0:1, :] = grad_gain
    grad_tok_ref[...] = (grad_after_self.here()[...] + grad_a).reshape(2, 64, D)


def first_grads_kernel(
    mover, core_ref, rights, back2, normed, normed2, gain_self, gain_others, table, out_ref,
    rights2_ref,
):
    core, head = core_ref[0], core_ref[1]
    unpack(back2.here(), rights2_ref)
    left = jnp.concatenate([normed.here()[...], normed2.here()[...]], axis=0)
    rights_ref = rights.here()
    for k in range(2):
        right = jnp.concatenate(
            [half_columns(core, rights_ref[k]), half_columns(core, rights2_ref[k])], axis=0
        )
        whole = dot_tn(left, right).astype(bf16)
        out_ref[:, 16 * k : 16 * k + 16, 0:HALF] = whole.reshape(64, 16, HALF)
    grad_gains = (gain_self.here()[0:1, :], gain_others.here()[0:1, :], gain_others.here()[1:2, :])
    small = jnp.zeros((64, 128), f32)
    for k, gain in enumerate(grad_gains):
        spread = jnp.where(chip_of(), gain, 0.0).astype(bf16)
        d, lane = iotas(D, 128)
        small = small + dot(spread, one_hot(lane == 32 * ((d // 8) % 2) + 8 * k + d % 8))
    b, p = iotas(BUCKETS, 64)
    spread = jnp.where(p == head * 4 + b // 8, table.here()[:, 0:1], 0.0).astype(bf16)
    b, lane = iotas(BUCKETS, 128)
    small = small + dot_tn(spread, one_hot(lane == 32 * ((b // 4) % 2) + 24 + b % 4))
    out_ref[:, :, HALF:] = jnp.broadcast_to(small.astype(bf16)[:, None, :], (64, 32, 128))


def add_kernel(mover, a, b, out_ref):
    out_ref[...] = (a.here()[...].astype(f32) + b.here()[...].astype(f32)).astype(bf16)


def memory_add_kernel(mover, a_ref, b_ref, out_ref, left_ref, right_ref):
    left, right = mover.start(a_ref.at[0], left_ref), mover.start(b_ref.at[1], right_ref)
    mover.wait(left)
    mover.wait(right)
    out_ref[...] = (left_ref[...].astype(f32) + right_ref[...].astype(f32)).astype(bf16)


def on_device(
    tokens,
    memory,
    segment_ids,
    buckets,
    w_query,
    w_keyval,
    w_output,
    w_cross_query,
    w_cross_keyval,
    w_cross_output,
    norm_self,
    norm_cross,
    norm_ffn,
    bias_table,
    w_gate,
    w_up,
    w_down,
    cotangent,
):
    core = lax.axis_index("c")
    head = (lax.axis_index("y") * 2 + lax.axis_index("xh")) * 2 + core
    x_at = lax.axis_index("xl") * 2 + lax.axis_index("xh")
    places = jnp.stack([core, head, x_at]).astype(jnp.int32)
    placed_1, placed_2, placed_3 = (
        pltpu.VMEM((2, k, 2, 16, 2, 16, HALF), bf16) for k in (1, 2, 3)
    )

    kept, given, ffn_rows = call(
        prepare_kernel,
        (((6, 8, HALF), bf16), ((6, 8, HALF), bf16), ((176, HALF), bf16)),
        w_query, w_keyval, w_output, w_cross_query, w_cross_keyval, w_cross_output,
        w_gate.T, w_up.T, w_down, us=2, core=places,
    )
    small = jnp.concatenate([norm_self, norm_cross, norm_ffn, bias_table])
    small = jnp.broadcast_to(jnp.pad(small, (0, 128 - small.shape[0]))[None], (8, 128))
    later, first = call(
        arrange_kernel,
        (((240, HALF), bf16),),
        kept, swap_core(given), small, ffn_rows, us=2, core=places,
        raw_outs=(((16, 32, 640), bf16),), scratch=[pltpu.VMEM((32, 640), bf16)],
    )
    cot_mine = lax.all_gather(cotangent.reshape(128, D), "y", axis=0, tiled=True)
    along_x = flips_x([later, later, later])
    first = exchange(first, ("z", "y"))
    mine_first = (first, *flips_x([first, first, first]))
    theirs_first = tuple(swap_core(x) for x in mine_first)
    other, ffn_part, memory_8 = call(
        spread_kernel,
        (((4, 64, HALF), bf16), ((4, 176, 384), bf16)),
        later, *along_x, memory, us=2, core=places, raw_outs=(((8, 2, 32, D), bf16),),
        after=(cot_mine,),
    )

    mine_other = lax.all_gather(other, ("z", "y"), axis=0)
    ffn_w = lax.all_gather(ffn_part, "z", axis=0)
    mem_mine = exchange(memory_8, ("y", "xh"))
    mem_theirs = swap_core(mem_mine)

    packed, normed_self, gains, table = call(
        project_kernel,
        (((16, 192, 128), bf16), ((128, D), bf16), ((8, D), f32), ((BUCKETS, 128), f32)),
        tokens, raw=(*mine_first, *theirs_first),
        scratch=[placed_2, pltpu.VMEM((2, 4, 16, 16, 128), bf16)], us=5, core=places,
        after=(mem_mine,),
    )
    qkv = exchange(packed, FFN)
    turned = jnp.roll(buckets[::-1], 1).reshape(1, SEQ)
    att, o_self, p_self, mine_other = call(
        self_kernel,
        (((16, 64, 128), bf16), ((SEQ, 128), f32), ((2, SEQ, SEQ), bf16)),
        qkv, table, mine_other, small=(turned, segment_ids), us=8,
        raw_outs=(((16, 4, 64, HALF), bf16),),
    )
    att = exchange(att, FFN)
    theirs_other = swap_core(mine_other)

    cot_theirs = swap_core(cot_mine)
    (kv_mem,) = call(
        memory_kernel,
        (((2, 8, MEM, 128), bf16),),
        mem_mine, mem_theirs, raw=(mine_other, theirs_other),
        scratch=[placed_1], us=5, core=places,
    )
    lefts, after_self, queries, p_cross, after_cross, normed_ffn = call(
        middle_kernel,
        (
            ((3, 128, D), bf16), ((128, D), f32), ((128, D), bf16), ((2, 8, 128, MEM), bf16),
            ((128, D), f32),
        ),
        att, tokens, gains, kv_mem, raw=(mine_other, theirs_other),
        raw_outs=(((4, 128, D), bf16),),
        scratch=[placed_3, pltpu.VMEM((128, D), bf16)], us=12, core=places,
    )

    x_mine = exchange(normed_ffn, "y").reshape(512, D)
    x_theirs = swap_core(x_mine)
    back, back2, hidden, grad_gate, grad_up, ffn_used = call(
        ffn_kernel,
        (
            ((512, D), bf16), ((512, D), bf16), ((2, 512, 352), bf16), ((2, 512, 352), bf16),
            ((2, 512, 352), bf16), ((3, 352, D), bf16),
        ),
        ffn_w, cot_mine, cot_theirs, x_mine, x_theirs, us=10,
    )
    back = (back.astype(f32) + swap_core(back2).astype(f32)).astype(bf16)
    grad_normed_ffn = exchange(back.reshape(4, 128, D), "y")

    out2, out, ffn_grads = call(
        ffn_rest_kernel,
        (((512, D), bf16), ((512, D), bf16), ((4, 4, 176, 384), bf16)),
        hidden, ffn_used, x_mine, x_theirs, cot_mine, cot_theirs, grad_gate, grad_up, us=11,
        after=(back,),
    )
    (out,) = call(add_kernel, (((512, D), bf16),), out, swap_core(out2), us=1)
    out_here = lax.psum_scatter(out, "y", scatter_dimension=0, tiled=True)
    output = (after_cross + out_here.astype(f32)).reshape(2, 64, D)
    ffn_grads = lax.psum_scatter(
        ffn_grads.reshape(4 * 704, 384), "z", scatter_dimension=0, tiled=True
    )

    att, rights, grad_kv, grad_after_self, gain_grads = call(
        middle_back_kernel,
        (
            ((16, 64, 128), bf16), ((3, 128, D), bf16), ((2, 8, 2, 32, D), bf16),
            ((128, D), f32), ((8, D), f32),
        ),
        grad_normed_ffn, cotangent, after_cross, gains, kv_mem, queries, p_cross, after_self,
        raw=(mine_other, theirs_other),
        scratch=[pltpu.VMEM((128, D), bf16), placed_3],
        us=15, core=places, after=(out,),
    )
    go = exchange(att, FFN)

    grad_kv2 = swap_core(grad_kv)
    (grad_mem,) = call(
        memory_add_kernel, (((8, 2, 32, D), bf16),), raw=(grad_kv, grad_kv2), us=1, after=(go,),
        scratch=[pltpu.VMEM((8, 2, 32, D), bf16)] * 2,
    )
    grad_mem = exchange(grad_mem, ("y", "xh"))

    back, grad_table = call(
        self_back_kernel,
        (((16, 192, 128), bf16), ((BUCKETS, 128), f32)),
        go, qkv, o_self, p_self, small=(turned,),
        scratch=[pltpu.VMEM((4, BLOCK, BLOCK), f32)], us=7, after=(ffn_grads,),
    )

    (grads_other,) = call(
        weights_kernel,
        (((16, 4, 64, HALF), bf16),),
        lefts, swap_core(lefts), rights, swap_core(rights), mem_mine, mem_theirs, grad_kv,
        grad_kv2, us=9, core=places, after=(back,),
    )
    rows_other = lax.psum_scatter(
        grads_other.reshape(16 * 256, HALF), "z", scatter_dimension=0, tiled=True
    )
    rows_other = lax.psum_scatter(rows_other, "y", scatter_dimension=0, tiled=True)

    back = exchange(back, FFN)
    (grad_memory,) = call(
        memory_back_kernel,
        (((2, 32, D), f32),),
        grad_mem, raw=(mine_other, theirs_other), scratch=[placed_1], us=3, core=places,
    )
    rights_first, grad_tokens, gain_self = call(
        last_kernel,
        (((2, 128, D), bf16), ((2, 64, D), f32), ((8, D), f32)),
        back, tokens, grad_after_self, gains, raw=(*mine_first, *theirs_first),
        scratch=[placed_2], us=5, core=places, after=(grads_other, out_here),
    )

    (first,) = call(
        first_grads_kernel,
        (((64, 32, 640), bf16),),
        rights_first, swap_core(back), normed_self, swap_core(normed_self), gain_self,
        gain_grads, grad_table,
        scratch=[pltpu.VMEM((2, 128, D), bf16)], us=4, core=places,
    )
    first = sum_of_all(first, CHIPS)
    small = first[0, HALF : HALF + 64].reshape(2, 32)

    tail_x = jnp.concatenate(
        [
            rows_other.reshape(4, 64, HALF),
            jnp.pad(ffn_grads.reshape(4, 176, 384), ((0, 0), (0, 0), (0, 128))),
        ],
        axis=1,
    )
    tail_x = sum_over_x(tail_x, x_at)
    ffn_final = tail_x[64:]

    def own_rows(rows):
        kept = jnp.where(core == 0, rows[:, 0:8], rows[:, 8:16])
        given = swap_core(jnp.where(core == 0, rows[:, 8:16], rows[:, 0:8]))
        return jnp.where(
            core == 0,
            jnp.concatenate([kept, given], axis=2),
            jnp.concatenate([given, kept], axis=2),
        )

    others = own_rows(tail_x[0:64].reshape(4, 16, HALF))
    firsts = own_rows(first[:, 0:HALF].reshape(2, 16, HALF))
    small = at_place(small, core) + swap_core(at_place(small, 1 - core))
    return (
        output,
        grad_tokens,
        grad_memory,
        firsts[0],
        firsts[1],
        others[0],
        others[1],
        others[2],
        others[3],
        small[0:8],
        small[8:16],
        small[16:24],
        small[24:28],
        ffn_final[:, 0:128].T,
        ffn_final[:, 128:256].T,
        ffn_final[:, 256:384],
    )


def solution(mesh):
    names = Mesh(mesh.devices.reshape(2, 4, 4, 2, 2), EVERY)
    tok, ffn, both = ("xl", "z"), FFN, EVERY
    big, mat, vec = P(None, both, None), P(both, None), P(both)
    fn = jax.shard_map(
        on_device,
        mesh=names,
        in_specs=(
            big, big, P(None, tok), P(), mat, mat, mat, mat, mat, mat, vec, vec, vec, vec,
            P(tok, ffn), P(tok, ffn), P(ffn, tok), big,
        ),
        out_specs=(
            big, big, big, mat, mat, mat, mat, mat, mat, vec, vec, vec, vec,
            P(tok, ffn), P(tok, ffn), P(ffn, tok),
        ),
        check_vma=False,
    )
    return fn
```

```python
import jax
import jax.numpy as jnp
from jax import lax
from jax.experimental import pallas as pl
from jax.experimental.pallas import tpu as pltpu
from jax.sharding import Mesh, PartitionSpec as P

HEADS = 16
HEAD_DIM = 64
BUCKETS = 32
KV_HEADS = 8
D = 1024
HALF = 512
SEQ = 1024
MEM = 512
BLOCK = 256

epsilon = 1e-06
masked_score = -1e30
scaling = HEAD_DIM ** (-0.5)

bf16 = jnp.bfloat16
f32 = jnp.float32

FFN = ("y", "xh", "c")
CHIPS = ("xl", "z", "y", "xh")
EVERY = ("xl", "z", "y", "xh", "c")


def dot(a, b):
    return lax.dot_general(a, b, (((1,), (0,)), ((), ())), preferred_element_type=f32)


def dot_nt(a, b):
    return lax.dot_general(a, b, (((1,), (1,)), ((), ())), preferred_element_type=f32)


def dot_tn(a, b):
    return lax.dot_general(a, b, (((0,), (0,)), ((), ())), preferred_element_type=f32)


def inverse_rms(a):
    return lax.rsqrt(jnp.mean(a * a, axis=-1, keepdims=True) + epsilon)


def norm_back(a, gain, e):
    n = inverse_rms(a)
    weighted = e * gain
    centre = jnp.mean(weighted * a, axis=-1, keepdims=True)
    grad_a = n * weighted - a * (n * n * n * centre)
    grad_gain = jnp.sum(e * a * n, axis=0, keepdims=True)
    return grad_a, grad_gain


class Mover:
    def __init__(self, arrived):
        self.arrived, self.copies, self.waited = arrived, [], []

    def start(self, source, target):
        number = len(self.copies)
        self.copies.append(pltpu.make_async_copy(source, target, self.arrived.at[number]))
        self.waited.append(False)
        self.copies[number].start()
        return number

    def wait(self, number):
        if not self.waited[number]:
            self.copies[number].wait()
            self.waited[number] = True

    def finish(self):
        for number in range(len(self.copies)):
            self.wait(number)


class Near:
    def __init__(self, mover, source, target):
        self.mover, self.target = mover, target
        self.number = mover.start(source, target)

    def here(self):
        self.mover.wait(self.number)
        return self.target


COPIES = 64


def call(kernel, outs, *args, raw=(), small=(), scratch=(), us=5, core=None, after=(), raw_outs=()):
    far, near = pl.BlockSpec(memory_space=pltpu.HBM), pl.BlockSpec(memory_space=pltpu.VMEM)
    operands = [*after, *args, *raw, *small]
    specs = [far] * (len(after) + len(args) + len(raw)) + [near] * len(small)
    leading = 0
    if core is not None:
        leading = 1
        operands = [core, *operands]
        specs = [pl.BlockSpec(memory_space=pltpu.SMEM), *specs]
    buffers = [pltpu.VMEM(x.shape, x.dtype) for x in args]
    buffers += [pltpu.VMEM(shape, dtype) for shape, dtype in outs]

    def body(*refs):
        refs = list(refs)
        take = lambda count: [refs.pop(0) for _ in range(count)]
        places = take(leading)
        take(len(after))
        sources, raws, smalls = take(len(args)), take(len(raw)), take(len(small))
        results, raw_results = take(len(outs)), take(len(raw_outs))
        own = take(len(scratch))
        targets, leaving = take(len(args)), take(len(outs))
        mover = Mover(refs.pop(0))
        sent = {}

        def send(number):
            if number not in sent:
                sent[number] = mover.start(leaving[number], results[number])

        mover.send = send
        nears = [Near(mover, *pair) for pair in zip(sources, targets)]
        kernel(mover, *places, *nears, *raws, *smalls, *leaving, *raw_results, *own)
        for number in range(len(outs)):
            send(number)
        mover.finish()

    return pl.pallas_call(
        body,
        out_shape=tuple(jax.ShapeDtypeStruct(s, t) for s, t in (*outs, *raw_outs)),
        in_specs=specs,
        out_specs=tuple([far] * (len(outs) + len(raw_outs))),
        scratch_shapes=[*scratch, *buffers, pltpu.SemaphoreType.DMA((COPIES,))],
        cost_estimate=pl.CostEstimate(
            flops=us * 2_000_000_000, bytes_accessed=us * 10_000_000, transcendentals=0
        ),
        compiler_params=pltpu.CompilerParams(vmem_limit_bytes=60 * 1024 * 1024),
    )(*operands)


def to_all(x, axes):
    n = lax.axis_size(axes)
    return lax.all_to_all(jnp.broadcast_to(x[None], (n, *x.shape)), axes, 0, 0, tiled=True)


def exchange(x, axes):
    return lax.all_to_all(x, axes, 0, 0, tiled=True)


def sum_of_all(x, axes):
    return jnp.sum(exchange(x, axes).astype(f32), axis=0)


def swap_core(x):
    return lax.ppermute(x, "c", [(0, 1), (1, 0)])


def flips_x(parts):
    flip_high = lax.ppermute(parts[0], "xh", [(0, 1), (1, 0)])
    flip_low = lax.ppermute(parts[1], "xl", [(0, 1), (1, 0)])
    flip_both = lax.ppermute(parts[2], ("xl", "xh"), [(0, 3), (1, 2), (2, 1), (3, 0)])
    return flip_high, flip_low, flip_both


def at_place(x, place):
    return lax.dynamic_index_in_dim(x, place, 0, keepdims=False)


def sum_over_x(x, x_at):
    found = flips_x([at_place(x, x_at ^ k) for k in range(1, 4)])
    total = at_place(x, x_at).astype(f32)
    for part in found:
        total = total + part.astype(f32)
    return total


def both_rows(core_ref, own, other):
    first = core_ref[0] == 0
    pair = [ref.here()[...].astype(f32) for ref in (own, other)]
    pair = [jnp.where(first, rows[:, 0:HALF], rows[:, HALF:]) for rows in pair]
    return jnp.where(
        first, jnp.concatenate(pair, axis=0), jnp.concatenate(pair[::-1], axis=0)
    ).astype(bf16)


def later_kernel(mover, core_ref, *refs):
    owns, others, ffns, out_ref = refs[0:4], refs[4:8], refs[8:11], refs[11]
    for k in range(4):
        out_ref[16 * k : 16 * k + 16, :] = both_rows(core_ref, owns[k], others[k])
    for k in range(3):
        out_ref[64:240, k * 128 : (k + 1) * 128] = ffns[k].here()[...]
    out_ref[64:240, 384:] = jnp.zeros((176, 128), bf16)


def first_kernel(mover, core_ref, own, own2, other, other2, small, first_ref, row_ref):
    row_ref[0:16, 0:HALF] = both_rows(core_ref, own, other)
    row_ref[16:32, 0:HALF] = both_rows(core_ref, own2, other2)
    row_ref[:, HALF:] = jnp.broadcast_to(small.here()[0:1, :], (32, 128))
    for p in range(16):
        mover.start(row_ref, first_ref.at[p])


def spread_kernel(mover, core_ref, own, high, low, both, memory, other_ref, ffn_ref, memory_8_ref):
    x_at = core_ref[2]
    refs = [x.here() for x in (own, high, low, both)]
    for k, ref in enumerate(refs):
        other_ref[x_at ^ k] = ref[0:64, :]
        ffn_ref[x_at ^ k] = ref[64:240, 0:384]
    mover.send(0)
    mover.send(1)
    memory_ref = memory.here()
    for p in range(8):
        mover.start(memory_ref, memory_8_ref.at[p])


def start_place(mover, core, mine_ref, theirs_ref, weights_ref, which):
    numbers = []
    for at, k in enumerate(which):
        numbers.append([])
        for x in range(4):
            xl, xh = x // 2, x % 2
            rows = pl.ds(16 * k, 16)
            for half, ref in ((core, mine_ref), (1 - core, theirs_ref)):
                numbers[-1].append(
                    mover.start(ref.at[:, x, rows, :], weights_ref.at[half, at, xl, :, xh])
                )
    return numbers


def start_place_first(mover, core, x_at, mine_refs, theirs_refs, weights_ref):
    numbers = []
    for at in range(2):
        numbers.append([])
        rows = pl.ds(16 * at, 16)
        for flip in range(4):
            x = x_at ^ flip
            for half, refs in ((core, mine_refs), (1 - core, theirs_refs)):
                target = weights_ref.at[half, at, x // 2, :, x % 2]
                source = refs[flip].at[:, rows, pl.ds(0, HALF)]
                numbers[-1].append(mover.start(source, target))
    return numbers


def placed_halves(mover, weights_ref, at, numbers):
    for number in numbers[at]:
        mover.wait(number)
    return [half_of(weights_ref, at, half) for half in range(2)]


def half_of(weights_ref, at, half):
    return weights_ref[half, at].reshape(D, HALF)


def iotas(rows, cols):
    return [lax.broadcasted_iota(jnp.int32, (rows, cols), k) for k in range(2)]


def one_hot(condition):
    return condition.astype(f32).astype(bf16)


def lanes_of(core, k):
    d, lane = iotas(D, 128)
    return one_hot((lane == 8 * k + d % 8) & ((d // 8) % 2 == core))


def chip_of():
    p, d = iotas(64, D)
    return d // 16 == p


def chip_along(p):
    x, zy = p // 16, p % 16
    return (x // 2) * 32 + zy * 2 + x % 2


def project_kernel(mover, core_ref, tok, *refs):
    mine_refs, theirs_refs, rows_ref = refs[0:4], refs[4:8], refs[8]
    out_ref, gains_ref, table_ref, tokens_ref, weights_ref, small_ref, stage_ref = refs[9:]
    core, head, x_at = (core_ref[k] for k in range(3))
    staged = mover.start(rows_ref.at[:, pl.ds(128, 128), :], stage_ref)
    arrivals = []
    for c, sources in enumerate((mine_refs, theirs_refs)):
        for flip in range(4):
            source = sources[flip].at[:, pl.ds(0, 16), pl.ds(HALF, 128)]
            arrivals.append(mover.start(source, small_ref.at[c, x_at ^ flip]))
    numbers = start_place_first(mover, core, x_at, mine_refs, theirs_refs, weights_ref)
    for number in arrivals:
        mover.wait(number)
    smalls = [(core, small_ref[0, :, :, 0:1, :]), (1 - core, small_ref[1, :, :, 0:1, :])]
    smalls = [(c, small.reshape(64, 128)) for c, small in smalls]
    p, d = iotas(64, D)
    own_chip = d // 16 == chip_along(p)
    gains = []
    for k in range(3):
        spread = sum(dot_nt(small, lanes_of(c, k)) for c, small in smalls)
        gains.append(jnp.sum(jnp.where(own_chip, spread, 0.0), axis=0, keepdims=True))
        gains_ref[k : k + 1, :] = gains[-1]
    b, p = iotas(BUCKETS, 64)
    chips = one_hot(chip_along(p) == head * 4 + b // 8)
    b, lane = iotas(BUCKETS, 128)
    column = jnp.zeros((BUCKETS, 1), f32)
    for c, small in smalls:
        hit = (lane == 24 + b % 4) & ((b // 4) % 2 == c)
        found = jnp.where(hit, dot(chips, small), 0.0)
        column = column + jnp.sum(found, axis=1, keepdims=True)
    table_ref[...] = jnp.broadcast_to(column, (BUCKETS, 128))
    mover.send(1)
    mover.send(2)

    x = tok.here()[...].reshape(128, D).astype(f32)
    normed = (x * inverse_rms(x) * gains[0]).astype(bf16)
    mover.wait(staged)
    mover.start(stage_ref, tokens_ref)
    wq = placed_halves(mover, weights_ref, 0, numbers)
    for half in range(2):
        q = (dot(normed, wq[half]) * scaling).astype(bf16)
        for k in range(8):
            one = q[:, k * 64 : (k + 1) * 64]
            out_ref[half * 8 + k, 0:64, :] = jnp.concatenate([one[0:64], one[64:128]], axis=1)
    wkv = placed_halves(mover, weights_ref, 1, numbers)
    keys = dot(normed, wkv[0]).astype(bf16)
    values = dot(normed, wkv[1]).astype(bf16)
    for n in range(KV_HEADS):
        both = jnp.concatenate(
            [keys[:, n * 64 : (n + 1) * 64], values[:, n * 64 : (n + 1) * 64]], axis=1
        )
        out_ref[2 * n, 64:192, :] = both
        out_ref[2 * n + 1, 64:192, :] = both


def bias_rows(onehot, table):
    return jnp.sum(onehot * table, axis=0, keepdims=True)


def self_kernel(
    mover, qkv, table, other, turned_ref, seg_ref, out_ref, o_ref, p_ref, other_out_ref
):
    numbers = lax.broadcasted_iota(jnp.int32, (BUCKETS, SEQ), 0)
    onehot = (numbers == turned_ref[...]).astype(f32)
    terms = bias_rows(onehot, table.here()[:, 0:1])
    bias = pltpu.roll(
        jnp.broadcast_to(terms, (BLOCK, SEQ)), 0, 1, stride=1, stride_axis=0
    )
    row = lax.broadcasted_iota(jnp.int32, (BLOCK, BLOCK), 0)
    col = lax.broadcasted_iota(jnp.int32, (BLOCK, BLOCK), 1)
    blocks = [jnp.where(col <= row, bias[:, 0:BLOCK], masked_score)]
    for k in range(1, 4):
        blocks.append(bias[:, SEQ - k * BLOCK : SEQ - (k - 1) * BLOCK])
    same_place = row == col
    qkv_ref = qkv.here()
    for mb in range(2):
        kv = qkv_ref[:, 64 + 64 * mb : 128 + 64 * mb, :].reshape(SEQ, 128)
        keys, values = kv[:, 0:64], kv[:, 64:128]
        segments = seg_ref[mb : mb + 1, :].astype(f32)
        for i in range(4):
            length = (i + 1) * BLOCK
            q = qkv_ref[4 * i : 4 * i + 4, 0:64, :].reshape(BLOCK, 128)
            q = q[:, mb * 64 : (mb + 1) * 64]
            s = dot_nt(q, keys[0:length])
            terms_here = jnp.concatenate([blocks[i - j] for j in range(i + 1)], axis=1)
            seg_q = jnp.where(same_place, segments[:, i * BLOCK : (i + 1) * BLOCK], 0.0)
            seg_q = jnp.sum(seg_q, axis=1, keepdims=True)
            s = jnp.where(seg_q == segments[:, 0:length], s + terms_here, masked_score)
            top = jnp.max(s, axis=-1, keepdims=True)
            e = jnp.exp(s - top)
            total = jnp.sum(e, axis=-1, keepdims=True)
            p = (e * (1.0 / total)).astype(bf16)
            p_ref[mb, i * BLOCK : (i + 1) * BLOCK, 0:length] = p
            o = dot(p, values[0:length])
            o_ref[i * BLOCK : (i + 1) * BLOCK, mb * 64 : (mb + 1) * 64] = o
            out_ref[4 * i : 4 * i + 4, :, mb * 64 : (mb + 1) * 64] = o.astype(bf16).reshape(
                4, 64, 64
            )
        if mb == 0:
            mover.start(other.here(), other_out_ref)


def self_back_kernel(
    mover, go, qkv, o, p_all, turned_ref, out_ref, table_ref, diag_ref
):
    diag_ref[...] = jnp.zeros_like(diag_ref)
    qkv_ref, go_ref, o_ref, p_ref = qkv.here(), go.here(), o.here(), p_all.here()
    for mb in range(2):
        lanes = slice(mb * 64, (mb + 1) * 64)
        kv = qkv_ref[:, 64 + 64 * mb : 128 + 64 * mb, :].reshape(SEQ, 128)
        keys, values = kv[:, 0:64], kv[:, 64:128]
        grad_keys = [jnp.zeros((BLOCK, 64), f32) for _ in range(4)]
        grad_values = [jnp.zeros((BLOCK, 64), f32) for _ in range(4)]
        for i in range(4):
            length = (i + 1) * BLOCK
            q = qkv_ref[4 * i : 4 * i + 4, 0:64, :].reshape(BLOCK, 128)[:, lanes]
            go = go_ref[4 * i : 4 * i + 4, :, :].reshape(BLOCK, 128)[:, lanes]
            o = o_ref[i * BLOCK : (i + 1) * BLOCK, lanes]
            centre = jnp.sum(go.astype(f32) * o, axis=-1, keepdims=True)
            p = p_ref[mb, i * BLOCK : (i + 1) * BLOCK, 0:length]
            ds = p.astype(f32) * (dot_nt(go, values[0:length]) - centre)
            for j in range(i + 1):
                diag_ref[i - j] += ds[:, j * BLOCK : (j + 1) * BLOCK]
            ds = ds.astype(bf16)
            gq = (dot(ds, keys[0:length]) * scaling).astype(bf16)
            out_ref[4 * i : 4 * i + 4, 0:64, lanes] = gq.reshape(4, 64, 64)
            for j in range(i + 1):
                part = slice(j * BLOCK, (j + 1) * BLOCK)
                grad_keys[j] += dot_tn(ds[:, part], q)
                grad_values[j] += dot_tn(p[:, part], go)
        for j in range(4):
            both = jnp.concatenate([grad_keys[j], grad_values[j]], axis=1).astype(bf16)
            out_ref[4 * j : 4 * j + 4, 64 + 64 * mb : 128 + 64 * mb, :] = both.reshape(4, 64, 128)
    mover.send(0)
    total = jnp.zeros((8, SEQ), f32)
    for g in range(BLOCK // 8):
        rows = slice(8 * g, 8 * g + 8)
        line = jnp.concatenate(
            [diag_ref[0, rows], diag_ref[3, rows], diag_ref[2, rows], diag_ref[1, rows]], axis=1
        )
        total = total + pltpu.roll(line, (SEQ - 8 * g) % SEQ, 1)
    sums = total[0:1]
    for s in range(1, 8):
        sums = sums + pltpu.roll(total[s : s + 1], SEQ - s, 1)
    numbers = lax.broadcasted_iota(jnp.int32, (BUCKETS, SEQ), 0)
    onehot = (numbers == turned_ref[...]).astype(f32)
    sums = jnp.sum(onehot * sums, axis=1, keepdims=True)
    table_ref[...] = jnp.broadcast_to(sums, (BUCKETS, 128))


def memory_kernel(mover, core_ref, mem, mem2, mine_ref, theirs_ref, out_ref, weights_ref):
    numbers = start_place(mover, core_ref[0], mine_ref, theirs_ref, weights_ref, (2,))
    mem_ref, mem2_ref = mem.here(), mem2.here()
    wckv = placed_halves(mover, weights_ref, 0, numbers)
    for mb in range(2):
        rows = jnp.concatenate(
            [mem_ref[:, mb].reshape(256, D), mem2_ref[:, mb].reshape(256, D)], axis=0
        )
        keys = dot(rows, wckv[0]).astype(bf16)
        values = dot(rows, wckv[1]).astype(bf16)
        for n in range(KV_HEADS):
            part = slice(n * 64, (n + 1) * 64)
            out_ref[mb, n] = jnp.concatenate([keys[:, part], values[:, part]], axis=1)


def middle_kernel(
    mover, core_ref, att, tok, gains, kv_all, mine_ref, theirs_ref,
    lefts_ref, after_self_ref, queries_ref, p_ref, after_cross_ref, normed_ffn_ref,
    weights_ref, normed_row_ref,
):
    numbers = start_place(mover, core_ref[0], mine_ref, theirs_ref, weights_ref, (0, 1, 3))
    attended_ref, normed_cross_ref, crossed_ref = (lefts_ref.at[k] for k in range(3))
    att_ref, tok_ref, gains_ref = att.here(), tok.here(), gains.here()
    for h in range(HEADS):
        for mb in range(2):
            attended_ref[mb * 64 : (mb + 1) * 64, h * 64 : (h + 1) * 64] = att_ref[
                h, :, mb * 64 : (mb + 1) * 64
            ]
    attended = attended_ref[...]
    x = tok_ref[...].reshape(128, D).astype(f32)
    wo = placed_halves(mover, weights_ref, 0, numbers)
    after_self = x + jnp.concatenate([dot(attended, wo[0]), dot(attended, wo[1])], axis=1)
    after_self_ref[...] = after_self
    mover.send(1)
    normed = (after_self * inverse_rms(after_self) * gains_ref[1:2, :]).astype(bf16)
    normed_cross_ref[...] = normed
    wcq = placed_halves(mover, weights_ref, 1, numbers)
    for half in range(2):
        q = (dot(normed, wcq[half]) * scaling).astype(bf16)
        queries_ref[:, half * HALF : (half + 1) * HALF] = q
    mover.send(2)
    kv_ref = kv_all.here()
    for mb in range(2):
        rows = slice(mb * 64, (mb + 1) * 64)
        for n in range(KV_HEADS):
            first = slice(2 * n * 64, (2 * n + 1) * 64)
            second = slice((2 * n + 1) * 64, (2 * n + 2) * 64)
            q = jnp.concatenate([queries_ref[rows, first], queries_ref[rows, second]], axis=0)
            kv = kv_ref[mb, n]
            s = dot_nt(q, kv[:, 0:64])
            e = jnp.exp(s - jnp.max(s, axis=-1, keepdims=True))
            p = (e * (1.0 / jnp.sum(e, axis=-1, keepdims=True))).astype(bf16)
            p_ref[mb, n] = p
            o = dot(p, kv[:, 64:128]).astype(bf16)
            crossed_ref[rows, first] = o[0:64]
            crossed_ref[rows, second] = o[64:128]
    mover.send(3)
    mover.send(0)
    crossed = crossed_ref[...]
    wco = placed_halves(mover, weights_ref, 2, numbers)
    after_cross = after_self + jnp.concatenate([dot(crossed, wco[0]), dot(crossed, wco[1])], axis=1)
    after_cross_ref[...] = after_cross
    mover.send(4)
    normed = after_cross * inverse_rms(after_cross) * gains_ref[2:3, :]
    normed_row_ref[...] = normed.astype(bf16)
    for k in range(4):
        mover.start(normed_row_ref, normed_ffn_ref.at[k])


def start_cotangents(mover, sources, targets):
    return [
        mover.start(source.at[:, pl.ds(0, 128), :], target)
        for source, target in zip(sources, targets)
    ]


def ffn_kernel(
    mover, w, x, x2, rows_ref, rows2_ref,
    back_ref, back2_ref, hidden_ref, grad_gate_ref, grad_up_ref, weights_ref, g_ref, g2_ref,
):
    arrivals = start_cotangents(mover, (rows_ref, rows2_ref), (g_ref, g2_ref))
    w_ref = w.here()
    for z in range(4):
        for along in range(4):
            t = (along // 2) * 4 + z
            rows = slice((along % 2) * 176, (along % 2) * 176 + 176)
            for k in range(3):
                weights_ref[k, rows, t * 128 : (t + 1) * 128] = w_ref[
                    z, along, :, k * 128 : (k + 1) * 128
                ]

    def tokens(at, x, g, rows, back_ref):
        gate = dot_nt(x, weights_ref[0])
        up = dot_nt(x, weights_ref[1])
        grad_hidden = dot_nt(g, weights_ref[2])
        const = 0.7978845608028654
        inner = const * (gate + 0.044715 * gate * gate * gate)
        tanh = jnp.tanh(inner)
        gelu = 0.5 * gate * (1.0 + tanh)
        slope = 0.5 * (1.0 + tanh) + 0.5 * gate * (1.0 - tanh * tanh) * const * (
            1.0 + 3 * 0.044715 * gate * gate
        )
        hidden_ref[at, rows, :] = (gelu * up).astype(bf16)
        grad_gate = (grad_hidden * up * slope).astype(bf16)
        grad_up = (grad_hidden * gelu).astype(bf16)
        grad_gate_ref[at, rows, :] = grad_gate
        grad_up_ref[at, rows, :] = grad_up
        back = dot(grad_gate, weights_ref[0]) + dot(grad_up, weights_ref[1])
        back_ref[rows, :] = back.astype(bf16)

    mover.send(5)
    sides = ((x2, g2_ref, back2_ref, 1), (x, g_ref, back_ref, 0))
    for x, g, back, at in sides:
        x = x.here()
        mover.wait(arrivals[at])

        def step(i, carry, at=at, x=x, g=g, back=back):
            rows = pl.ds(pl.multiple_of(i * 256, 256), 256)
            two = g[pl.ds(2 * i, 2)].reshape(256, D)
            tokens(at, x[rows, :], two, rows, back)
            return carry

        lax.fori_loop(0, 2, step, 0)
        mover.send(at)


def ffn_rest_kernel(
    mover, hidden, weights, x, x2, grad_gate, grad_up, rows_ref, rows2_ref,
    out2_ref, out_ref, grads_ref, g_ref, g2_ref,
):
    arrivals = start_cotangents(mover, (rows_ref, rows2_ref), (g_ref, g2_ref))
    hidden_ref, weights_ref = hidden.here(), weights.here()
    for at, ref in ((1, out2_ref), (0, out_ref)):
        ref[...] = dot(hidden_ref[at], weights_ref[2]).astype(bf16)
        mover.send(1 - at)
    x_ref, x2_ref = x.here(), x2.here()
    for number in arrivals:
        mover.wait(number)
    grad_gate_ref, grad_up_ref = grad_gate.here(), grad_up.here()
    for t in range(8):
        xl, z = t // 4, t % 4
        cols = slice(t * 128, (t + 1) * 128)
        x_cols = (x_ref[:, cols], x2_ref[:, cols])
        g_cols = (g_ref[:, :, cols].reshape(512, 128), g2_ref[:, :, cols].reshape(512, 128))
        sides = ((grad_gate_ref, x_cols), (grad_up_ref, x_cols), (hidden_ref, g_cols))
        for k, (left, right) in enumerate(sides):
            part = (dot_tn(left[0], right[0]) + dot_tn(left[1], right[1])).astype(bf16)
            for xh in range(2):
                grads_ref[z, xl * 2 + xh, :, k * 128 : (k + 1) * 128] = part[
                    xh * 176 : (xh + 1) * 176
                ]


def middle_back_kernel(
    mover, core_ref, parts, cot, after_cross, gains, kv_all, queries, p_all, after_self,
    mine_ref, theirs_ref,
    att_ref, rights_ref, grad_kv_ref, grad_after_self_ref, grad_gains_ref,
    grad_crossed_ref, weights_ref,
):
    numbers = start_place(mover, core_ref[0], mine_ref, theirs_ref, weights_ref, (3, 1, 0))
    self_branch_ref, grad_queries_ref, cross_branch_ref = (rights_ref.at[k] for k in range(3))
    parts_ref, gains_ref = parts.here(), gains.here()
    e = parts_ref[0].astype(f32)
    for k in range(1, 4):
        e = e + parts_ref[k].astype(f32)
    grad_a, grad_gain = norm_back(after_cross.here()[...], gains_ref[2:3, :], e)
    grad_gains_ref[1:2, :] = grad_gain
    grad_after_cross = cot.here()[...].reshape(128, D).astype(f32) + grad_a
    branch = grad_after_cross.astype(bf16)
    cross_branch_ref[...] = branch
    wco = placed_halves(mover, weights_ref, 0, numbers)
    grad_crossed_ref[...] = (
        dot_nt(branch[:, 0:HALF], wco[0]) + dot_nt(branch[:, HALF:], wco[1])
    ).astype(bf16)
    queries_ref, p_ref, kv_ref = queries.here(), p_all.here(), kv_all.here()
    for mb in range(2):
        rows = slice(mb * 64, (mb + 1) * 64)
        for n in range(KV_HEADS):
            first = slice(2 * n * 64, (2 * n + 1) * 64)
            second = slice((2 * n + 1) * 64, (2 * n + 2) * 64)
            q = jnp.concatenate([queries_ref[rows, first], queries_ref[rows, second]], axis=0)
            go = jnp.concatenate(
                [grad_crossed_ref[rows, first], grad_crossed_ref[rows, second]], axis=0
            )
            kv = kv_ref[mb, n]
            p = p_ref[mb, n]
            wide = p.astype(f32)
            gp = dot_nt(go, kv[:, 64:128])
            centre = jnp.sum(wide * gp, axis=-1, keepdims=True)
            ds = (wide * (gp - centre)).astype(bf16)
            gq = (dot(ds, kv[:, 0:64]) * scaling).astype(bf16)
            grad_queries_ref[rows, first] = gq[0:64]
            grad_queries_ref[rows, second] = gq[64:128]
            gk = dot_tn(ds, q).astype(bf16).reshape(2, 8, 32, 64)
            gv = dot_tn(p, go).astype(bf16).reshape(2, 8, 32, 64)
            grad_kv_ref[:, :, mb, :, n * 64 : (n + 1) * 64] = gk
            grad_kv_ref[:, :, mb, :, HALF + n * 64 : HALF + (n + 1) * 64] = gv
    mover.send(2)
    gq = grad_queries_ref[...]
    wcq = placed_halves(mover, weights_ref, 1, numbers)
    e = dot_nt(gq[:, 0:HALF], wcq[0]) + dot_nt(gq[:, HALF:], wcq[1])
    grad_a, grad_gain = norm_back(after_self.here()[...], gains_ref[1:2, :], e)
    grad_gains_ref[0:1, :] = grad_gain
    grad_after_self = grad_after_cross + grad_a
    grad_after_self_ref[...] = grad_after_self
    mover.send(3)
    branch = grad_after_self.astype(bf16)
    self_branch_ref[...] = branch
    mover.send(1)
    wo = placed_halves(mover, weights_ref, 2, numbers)
    back = (dot_nt(branch[:, 0:HALF], wo[0]) + dot_nt(branch[:, HALF:], wo[1])).astype(bf16)
    for h in range(HEADS):
        one = back[:, h * 64 : (h + 1) * 64]
        att_ref[h] = jnp.concatenate([one[0:64], one[64:128]], axis=1)


def half_columns(core, x):
    return jnp.where(core == 0, x[:, 0:HALF], x[:, HALF:])


def weights_kernel(
    mover, core_ref, lefts, lefts2, rights, rights2, mem, mem2, grad_kv, grad_kv2, part, part2,
    out_ref, whole_ref,
):
    core = core_ref[0]
    rights_ref, rights2_ref = rights.here(), rights2.here()
    lefts_ref, lefts2_ref = lefts.here(), lefts2.here()

    def put(k, whole):
        whole = whole.astype(bf16).reshape(2, 4, 8, 16, HALF)
        for xl in range(2):
            out_ref[:, 8 * xl : 8 * xl + 8, 16 * k : 16 * k + 16, :] = whole[xl]

    for k in range(3):
        left = jnp.concatenate([lefts_ref[k], lefts2_ref[k]], axis=0)
        right = jnp.concatenate(
            [half_columns(core, rights_ref[k]), half_columns(core, rights2_ref[k])], axis=0
        )
        put((0, 1, 3)[k], dot_tn(left, right))
    total = jnp.zeros((D, HALF), f32)
    kv_ref, kv2_ref = grad_kv.here(), grad_kv2.here()
    for at, mem_ref in enumerate((mem.here(), mem2.here())):
        own = half_columns(core, kv_ref[at].reshape(512, D)).astype(f32)
        both = own + half_columns(core, kv2_ref[1 - at].reshape(512, D)).astype(f32)
        total = total + dot_tn(mem_ref[...].reshape(512, D), both.astype(bf16))
    put(2, total)
    whole_ref[...] = (part.here()[...].astype(f32) + part2.here()[...].astype(f32)).astype(bf16)


def memory_back_kernel(mover, core_ref, parts, mine_ref, theirs_ref, out_ref, weights_ref):
    numbers = start_place(mover, core_ref[0], mine_ref, theirs_ref, weights_ref, (2,))
    parts_ref = parts.here()
    grad = parts_ref[0].astype(f32)
    for k in range(1, 8):
        grad = grad + parts_ref[k].astype(f32)
    grad = grad.reshape(64, D).astype(bf16)
    wckv = placed_halves(mover, weights_ref, 0, numbers)
    whole = dot_nt(grad[:, 0:HALF], wckv[0]) + dot_nt(grad[:, HALF:], wckv[1])
    out_ref[...] = whole.reshape(2, 32, D)


def unpack(back_ref, out_ref):
    for h in range(HEADS):
        for mb in range(2):
            out_ref[0, mb * 64 : (mb + 1) * 64, h * 64 : (h + 1) * 64] = back_ref[
                h, 0:64, mb * 64 : (mb + 1) * 64
            ]
    for n in range(KV_HEADS):
        both = back_ref[2 * n, 64:192, :].astype(f32) + back_ref[2 * n + 1, 64:192, :].astype(f32)
        both = both.astype(bf16)
        out_ref[1, :, n * 64 : (n + 1) * 64] = both[:, 0:64]
        out_ref[1, :, HALF + n * 64 : HALF + (n + 1) * 64] = both[:, 64:128]


def head_grads_kernel(
    mover, core_ref, back, gains, rows_ref, rows2_ref, far_ref, far2_ref, out_ref, *tokens_refs
):
    core, xh = core_ref[0], core_ref[2] % 2
    near = pl.ds(128, 128)
    sources = (rows_ref.at[:, near, :], rows2_ref.at[:, near, :], far_ref, far2_ref)
    numbers = [mover.start(*pair) for pair in zip(sources, tokens_refs)]
    back_ref = back.here()
    gain = gains.here()[0:1, :]
    total = jnp.zeros((D, 192), f32)
    for k in range(4):
        mover.wait(numbers[k])
        x = tokens_refs[k][...].reshape(512, D).astype(f32)
        normed = (x * inverse_rms(x) * gain).astype(bf16)
        parts = []
        for y in range(4):
            block = back_ref[(y * 2 + (xh ^ (k // 2))) * 2 + (core ^ (k % 2))]
            for mb in range(2):
                lanes = slice(mb * 64, (mb + 1) * 64)
                keyvals = block[64 + 64 * mb : 128 + 64 * mb]
                parts.append(jnp.concatenate([block[0:64, lanes], keyvals], axis=1))
        total = total + dot_tn(normed, jnp.concatenate(parts, axis=0))
    out_ref[...] = total.astype(bf16)


def last_kernel(mover, core_ref, back, tok, grad_after_self, gains, head_grads, gain_others,
                table, *refs):
    mine_refs, theirs_refs = refs[0:4], refs[4:8]
    grad_tok_ref, sums_ref, rights_ref, weights_ref = refs[8:]
    head = core_ref[1]
    numbers = start_place_first(
        mover, core_ref[0], core_ref[2], mine_refs, theirs_refs, weights_ref
    )
    unpack(back.here(), rights_ref)
    sums_ref[:, 0:192] = head_grads.here()[...]
    gq, gkv = rights_ref[0], rights_ref[1]
    wq = placed_halves(mover, weights_ref, 0, numbers)
    e = dot_nt(gq[:, 0:HALF], wq[0]) + dot_nt(gq[:, HALF:], wq[1])
    wkv = placed_halves(mover, weights_ref, 1, numbers)
    e = e + dot_nt(gkv[:, 0:HALF], wkv[0]) + dot_nt(gkv[:, HALF:], wkv[1])
    x = tok.here()[...].reshape(128, D).astype(f32)
    grad_a, grad_gain = norm_back(x, gains.here()[0:1, :], e)
    grad_tok_ref[...] = (grad_after_self.here()[...] + grad_a).reshape(2, 64, D)
    others_ref = gain_others.here()
    lines = [grad_gain, others_ref[0:1, :], others_ref[1:2, :], jnp.zeros((5, D), f32)]
    lines = jnp.concatenate(lines, axis=0).astype(bf16)
    number, lane = iotas(8, 64)
    extra = dot_tn(lines, one_hot(number == lane))
    d, b = iotas(D, BUCKETS)
    entry = (d // 128) * 64 + ((d // 8) % 16) * 4 + d % 8
    found = one_hot((d % 8 < 4) & (entry == head * BUCKETS + b))
    b, lane = iotas(BUCKETS, 64)
    column = jnp.where(lane == 3, table.here()[:, 0:64], 0.0).astype(bf16)
    sums_ref[:, 192:256] = (extra + dot(found, column)).astype(bf16)


def finish_kernel(mover, parts, query_ref, keyval_ref, small_ref):
    parts_ref = parts.here()
    total = parts_ref[0:128, :].astype(f32)
    for t in range(1, 8):
        total = total + parts_ref[128 * t : 128 * t + 128, :].astype(f32)
    heads = [total[8 * h : 8 * h + 8] for h in range(HEADS)]
    small_ref[...] = sum(heads)[:, 128:256]
    for h in range(HEADS):
        query_ref[:, h * 64 : (h + 1) * 64] = heads[h][:, 0:64]
    for n in range(KV_HEADS):
        both = heads[2 * n][:, 64:192] + heads[2 * n + 1][:, 64:192]
        keyval_ref[:, n * 64 : (n + 1) * 64] = both[:, 0:64]
        keyval_ref[:, HALF + n * 64 : HALF + (n + 1) * 64] = both[:, 64:128]


def memory_add_kernel(mover, a_ref, b_ref, out_ref, left_ref, right_ref):
    left, right = mover.start(a_ref.at[0], left_ref), mover.start(b_ref.at[1], right_ref)
    mover.wait(left)
    mover.wait(right)
    out_ref[...] = (left_ref[...].astype(f32) + right_ref[...].astype(f32)).astype(bf16)


def pass_kernel(mover, source, target_ref):
    target_ref[...] = source.here()[...]


def on_device(
    tokens,
    memory,
    segment_ids,
    buckets,
    w_query,
    w_keyval,
    w_output,
    w_cross_query,
    w_cross_keyval,
    w_cross_output,
    norm_self,
    norm_cross,
    norm_ffn,
    bias_table,
    w_gate,
    w_up,
    w_down,
    cotangent,
):
    core = lax.axis_index("c")
    head = (lax.axis_index("y") * 2 + lax.axis_index("xh")) * 2 + core
    x_at = lax.axis_index("xl") * 2 + lax.axis_index("xh")
    places = jnp.stack([core, head, x_at]).astype(jnp.int32)
    placed_1, placed_2, placed_3 = (
        pltpu.VMEM((2, k, 2, 16, 2, 16, HALF), bf16) for k in (1, 2, 3)
    )

    owns = [w_query, w_keyval, w_output, w_cross_query, w_cross_keyval, w_cross_output]
    others = [swap_core(w) for w in owns]
    (later,) = call(
        later_kernel, (((240, HALF), bf16),), *owns[2:], *others[2:], w_gate.T, w_up.T, w_down,
        us=1, core=places,
    )
    small = jnp.concatenate([norm_self, norm_cross, norm_ffn, bias_table])
    small = jnp.broadcast_to(jnp.pad(small, (0, 128 - small.shape[0]))[None], (8, 128))
    (first,) = call(
        first_kernel, (), *owns[:2], *others[:2], small, us=2, core=places, after=(later,),
        raw_outs=(((16, 32, 640), bf16),), scratch=[pltpu.VMEM((32, 640), bf16)],
    )
    rows = jnp.concatenate([cotangent.reshape(128, D), tokens.reshape(128, D)], axis=0)
    rows_mine = lax.all_gather(rows, "y", axis=0)
    along_x = flips_x([later, later, later])
    first = exchange(first, ("z", "y"))
    mine_first = (first, *flips_x([first, first, first]))
    theirs_first = tuple(swap_core(x) for x in mine_first)
    other, ffn_part, memory_8 = call(
        spread_kernel,
        (((4, 64, HALF), bf16), ((4, 176, 384), bf16)),
        later, *along_x, memory, us=2, core=places, raw_outs=(((8, 2, 32, D), bf16),),
        after=(first,),
    )

    mine_other = lax.all_gather(other, ("z", "y"), axis=0)
    ffn_w = lax.all_gather(ffn_part, "z", axis=0)
    mem_mine = exchange(memory_8, ("y", "xh"))
    mem_theirs = swap_core(mem_mine)

    packed, gains, table, tok_mine = call(
        project_kernel,
        (((16, 192, 128), bf16), ((8, D), f32), ((BUCKETS, 128), f32)),
        tokens, raw=(*mine_first, *theirs_first, rows_mine),
        raw_outs=(((4, 128, D), bf16),),
        scratch=[placed_2, pltpu.VMEM((2, 4, 16, 16, 128), bf16), pltpu.VMEM((4, 128, D), bf16)],
        us=5, core=places, after=(mem_mine,),
    )
    qkv = exchange(packed, FFN)
    turned = jnp.roll(buckets[::-1], 1).reshape(1, SEQ)
    att, o_self, p_self, mine_other = call(
        self_kernel,
        (((16, 64, 128), bf16), ((SEQ, 128), f32), ((2, SEQ, SEQ), bf16)),
        qkv, table, mine_other, small=(turned, segment_ids), us=8,
        raw_outs=(((16, 4, 64, HALF), bf16),),
    )
    att = exchange(att, FFN)
    theirs_other = swap_core(mine_other)

    rows_theirs = swap_core(rows_mine)
    far_mine = lax.ppermute(tok_mine, "xh", [(0, 1), (1, 0)])
    far_theirs = swap_core(far_mine)
    (kv_mem,) = call(
        memory_kernel,
        (((2, 8, MEM, 128), bf16),),
        mem_mine, mem_theirs, raw=(mine_other, theirs_other),
        scratch=[placed_1], us=5, core=places,
    )
    lefts, after_self, queries, p_cross, after_cross, normed_ffn = call(
        middle_kernel,
        (
            ((3, 128, D), bf16), ((128, D), f32), ((128, D), bf16), ((2, 8, 128, MEM), bf16),
            ((128, D), f32),
        ),
        att, tokens, gains, kv_mem, raw=(mine_other, theirs_other),
        raw_outs=(((4, 128, D), bf16),),
        scratch=[placed_3, pltpu.VMEM((128, D), bf16)], us=12, core=places,
    )

    x_mine = exchange(normed_ffn, "y").reshape(512, D)
    x_theirs = swap_core(x_mine)
    back, back2, hidden, grad_gate, grad_up, ffn_used = call(
        ffn_kernel,
        (
            ((512, D), bf16), ((512, D), bf16), ((2, 512, 352), bf16), ((2, 512, 352), bf16),
            ((2, 512, 352), bf16), ((3, 352, D), bf16),
        ),
        ffn_w, x_mine, x_theirs, raw=(rows_mine, rows_theirs),
        scratch=[pltpu.VMEM((4, 128, D), bf16)] * 2, us=10,
    )
    back = (back.astype(f32) + swap_core(back2).astype(f32)).astype(bf16)
    grad_normed_ffn = exchange(back.reshape(4, 128, D), "y")

    out2, out, ffn_grads = call(
        ffn_rest_kernel,
        (((512, D), bf16), ((512, D), bf16), ((4, 4, 176, 384), bf16)),
        hidden, ffn_used, x_mine, x_theirs, grad_gate, grad_up, raw=(rows_mine, rows_theirs),
        scratch=[pltpu.VMEM((4, 128, D), bf16)] * 2, us=11, after=(back,),
    )
    ffn_rows = lax.psum_scatter(
        ffn_grads.reshape(4 * 704, 384), "z", scatter_dimension=0, tiled=True
    )

    att, rights, grad_kv, grad_after_self, gain_grads = call(
        middle_back_kernel,
        (
            ((16, 64, 128), bf16), ((3, 128, D), bf16), ((2, 8, 2, 32, D), bf16),
            ((128, D), f32), ((8, D), f32),
        ),
        grad_normed_ffn, cotangent, after_cross, gains, kv_mem, queries, p_cross, after_self,
        raw=(mine_other, theirs_other),
        scratch=[pltpu.VMEM((128, D), bf16), placed_3],
        us=15, core=places, after=(ffn_grads, far_mine),
    )
    go = exchange(att, FFN)
    grad_kv2 = swap_core(grad_kv)
    (grad_mem,) = call(
        memory_add_kernel, (((8, 2, 32, D), bf16),), raw=(grad_kv, grad_kv2), us=1,
        scratch=[pltpu.VMEM((8, 2, 32, D), bf16)] * 2,
    )
    grad_mem = exchange(grad_mem, ("y", "xh"))

    back, grad_table = call(
        self_back_kernel,
        (((16, 192, 128), bf16), ((BUCKETS, 128), f32)),
        go, qkv, o_self, p_self, small=(turned,),
        scratch=[pltpu.VMEM((4, BLOCK, BLOCK), f32)], us=7,
    )


    (back,) = call(pass_kernel, (((16, 192, 128), bf16),), back, us=1, after=(grad_mem,))
    grads_other, out = call(
        weights_kernel,
        (((4, 16, 64, HALF), bf16), ((512, D), bf16)),
        lefts, swap_core(lefts), rights, swap_core(rights), mem_mine, mem_theirs, grad_kv,
        grad_kv2, out, swap_core(out2), us=9, core=places, after=(go, ffn_rows),
    )
    out_here = lax.psum_scatter(out, "y", scatter_dimension=0, tiled=True)
    output = (after_cross + out_here.astype(f32)).reshape(2, 64, D)

    rows_other = lax.psum_scatter(
        grads_other.reshape(16 * 256, HALF), "z", scatter_dimension=0, tiled=True
    )

    (head_grads,) = call(
        head_grads_kernel,
        (((D, 192), bf16),),
        back, gains, raw=(rows_mine, rows_theirs, far_mine, far_theirs),
        scratch=[pltpu.VMEM((4, 128, D), bf16)] * 4, us=4, core=places,
    )
    back = exchange(back, FFN)
    (grad_memory,) = call(
        memory_back_kernel,
        (((2, 32, D), f32),),
        grad_mem, raw=(mine_other, theirs_other), scratch=[placed_1], us=3, core=places,
    )
    grad_tokens, sums = call(
        last_kernel,
        (((2, 64, D), f32), ((D, 256), bf16)),
        back, tokens, grad_after_self, gains, head_grads, gain_grads, grad_table,
        raw=(*mine_first, *theirs_first), scratch=[pltpu.VMEM((2, 128, D), bf16), placed_2],
        us=6, core=places, after=(rows_other,),
    )

    grad_query, grad_keyval, small = call(
        finish_kernel,
        (((8, D), f32), ((8, D), f32), ((8, 128), f32)),
        exchange(sums, EVERY), us=1,
    )

    others = sum_of_all(rows_other.reshape(16, 64, HALF), ("xl", "y", "xh"))
    ffn_final = sum_over_x(ffn_rows.reshape(4, 176, 384), x_at)

    def own_rows(rows):
        kept = jnp.where(core == 0, rows[:, 0:8], rows[:, 8:16])
        given = swap_core(jnp.where(core == 0, rows[:, 8:16], rows[:, 0:8]))
        return jnp.where(
            core == 0,
            jnp.concatenate([kept, given], axis=2),
            jnp.concatenate([given, kept], axis=2),
        )

    others = own_rows(others.reshape(4, 16, HALF))
    return (
        output,
        grad_tokens,
        grad_memory,
        grad_query,
        grad_keyval,
        others[0],
        others[1],
        others[2],
        others[3],
        small[:, 64],
        small[:, 65],
        small[:, 66],
        small[0:4, 67],
        ffn_final[:, 0:128].T,
        ffn_final[:, 128:256].T,
        ffn_final[:, 256:384],
    )


def solution(mesh):
    names = Mesh(mesh.devices.reshape(2, 4, 4, 2, 2), EVERY)
    tok, ffn, both = ("xl", "z"), FFN, EVERY
    big, mat, vec = P(None, both, None), P(both, None), P(both)
    fn = jax.shard_map(
        on_device,
        mesh=names,
        in_specs=(
            big, big, P(None, tok), P(), mat, mat, mat, mat, mat, mat, vec, vec, vec, vec,
            P(tok, ffn), P(tok, ffn), P(ffn, tok), big,
        ),
        out_specs=(
            big, big, big, mat, mat, mat, mat, mat, mat, vec, vec, vec, vec,
            P(tok, ffn), P(tok, ffn), P(ffn, tok),
        ),
        check_vma=False,
    )
    return fn
```

```python
import jax
import jax.numpy as jnp
from jax import lax
from jax.experimental import pallas as pl
from jax.experimental.pallas import tpu as pltpu
from jax.sharding import Mesh, PartitionSpec as P

HEADS = 16
HEAD_DIM = 64
BUCKETS = 32
KV_HEADS = 8
D = 1024
HALF = 512
SEQ = 1024
MEM = 512
BLOCK = 256

epsilon = 1e-06
masked_score = -1e30
scaling = HEAD_DIM ** (-0.5)

bf16 = jnp.bfloat16
f32 = jnp.float32

FFN = ("y", "xh", "c")
CHIPS = ("xl", "z", "y", "xh")
EVERY = ("xl", "z", "y", "xh", "c")


def dot(a, b):
    return lax.dot_general(a, b, (((1,), (0,)), ((), ())), preferred_element_type=f32)


def dot_nt(a, b):
    return lax.dot_general(a, b, (((1,), (1,)), ((), ())), preferred_element_type=f32)


def dot_tn(a, b):
    return lax.dot_general(a, b, (((0,), (0,)), ((), ())), preferred_element_type=f32)


def inverse_rms(a):
    return lax.rsqrt(jnp.mean(a * a, axis=-1, keepdims=True) + epsilon)


def norm_back(a, gain, e):
    n = inverse_rms(a)
    weighted = e * gain
    centre = jnp.mean(weighted * a, axis=-1, keepdims=True)
    grad_a = n * weighted - a * (n * n * n * centre)
    grad_gain = jnp.sum(e * a * n, axis=0, keepdims=True)
    return grad_a, grad_gain


class Mover:
    def __init__(self, arrived):
        self.arrived, self.copies, self.waited = arrived, [], []

    def start(self, source, target):
        number = len(self.copies)
        self.copies.append(pltpu.make_async_copy(source, target, self.arrived.at[number]))
        self.waited.append(False)
        self.copies[number].start()
        return number

    def wait(self, number):
        if not self.waited[number]:
            self.copies[number].wait()
            self.waited[number] = True

    def finish(self):
        for number in range(len(self.copies)):
            self.wait(number)


class Near:
    def __init__(self, mover, source, target):
        self.mover, self.target = mover, target
        self.number = mover.start(source, target)

    def here(self):
        self.mover.wait(self.number)
        return self.target


COPIES = 64


def call(kernel, outs, *args, raw=(), small=(), scratch=(), us=5, core=None, after=(), raw_outs=()):
    far, near = pl.BlockSpec(memory_space=pltpu.HBM), pl.BlockSpec(memory_space=pltpu.VMEM)
    operands = [*after, *args, *raw, *small]
    specs = [far] * (len(after) + len(args) + len(raw)) + [near] * len(small)
    leading = 0
    if core is not None:
        leading = 1
        operands = [core, *operands]
        specs = [pl.BlockSpec(memory_space=pltpu.SMEM), *specs]
    buffers = [pltpu.VMEM(x.shape, x.dtype) for x in args]
    buffers += [pltpu.VMEM(shape, dtype) for shape, dtype in outs]

    def body(*refs):
        refs = list(refs)
        take = lambda count: [refs.pop(0) for _ in range(count)]
        places = take(leading)
        take(len(after))
        sources, raws, smalls = take(len(args)), take(len(raw)), take(len(small))
        results, raw_results = take(len(outs)), take(len(raw_outs))
        own = take(len(scratch))
        targets, leaving = take(len(args)), take(len(outs))
        mover = Mover(refs.pop(0))
        sent = {}

        def send(number):
            if number not in sent:
                sent[number] = mover.start(leaving[number], results[number])

        mover.send = send
        nears = [Near(mover, *pair) for pair in zip(sources, targets)]
        kernel(mover, *places, *nears, *raws, *smalls, *leaving, *raw_results, *own)
        for number in range(len(outs)):
            send(number)
        mover.finish()

    return pl.pallas_call(
        body,
        out_shape=tuple(jax.ShapeDtypeStruct(s, t) for s, t in (*outs, *raw_outs)),
        in_specs=specs,
        out_specs=tuple([far] * (len(outs) + len(raw_outs))),
        scratch_shapes=[*scratch, *buffers, pltpu.SemaphoreType.DMA((COPIES,))],
        cost_estimate=pl.CostEstimate(
            flops=us * 2_000_000_000, bytes_accessed=us * 10_000_000, transcendentals=0
        ),
        compiler_params=pltpu.CompilerParams(vmem_limit_bytes=60 * 1024 * 1024),
    )(*operands)


def to_all(x, axes):
    n = lax.axis_size(axes)
    return lax.all_to_all(jnp.broadcast_to(x[None], (n, *x.shape)), axes, 0, 0, tiled=True)


def exchange(x, axes):
    return lax.all_to_all(x, axes, 0, 0, tiled=True)


def sum_of_all(x, axes):
    return jnp.sum(exchange(x, axes).astype(f32), axis=0)


def swap_core(x):
    return lax.ppermute(x, "c", [(0, 1), (1, 0)])


def flips_x(parts):
    flip_high = lax.ppermute(parts[0], "xh", [(0, 1), (1, 0)])
    flip_low = lax.ppermute(parts[1], "xl", [(0, 1), (1, 0)])
    flip_both = lax.ppermute(parts[2], ("xl", "xh"), [(0, 3), (1, 2), (2, 1), (3, 0)])
    return flip_high, flip_low, flip_both


def at_place(x, place):
    return lax.dynamic_index_in_dim(x, place, 0, keepdims=False)


def sum_over_x(x, x_at):
    found = flips_x([at_place(x, x_at ^ k) for k in range(1, 4)])
    total = at_place(x, x_at).astype(f32)
    for part in found:
        total = total + part.astype(f32)
    return total


def both_rows(core_ref, own, other):
    first = core_ref[0] == 0
    pair = [ref.here()[...].astype(f32) for ref in (own, other)]
    pair = [jnp.where(first, rows[:, 0:HALF], rows[:, HALF:]) for rows in pair]
    return jnp.where(
        first, jnp.concatenate(pair, axis=0), jnp.concatenate(pair[::-1], axis=0)
    ).astype(bf16)


def arrange_kernel(mover, core_ref, *refs):
    owns, others, ffns, small = refs[0:6], refs[6:12], refs[12:15], refs[15]
    out_ref, first_ref, row_ref = refs[16:]
    for k in range(4):
        out_ref[16 * k : 16 * k + 16, :] = both_rows(core_ref, owns[k + 2], others[k + 2])
    for k in range(3):
        out_ref[64:240, k * 128 : (k + 1) * 128] = ffns[k].here()[...]
    out_ref[64:240, 384:] = jnp.zeros((176, 128), bf16)
    mover.send(0)
    for k in range(2):
        row_ref[16 * k : 16 * k + 16, 0:HALF] = both_rows(core_ref, owns[k], others[k])
    row_ref[:, HALF:] = jnp.broadcast_to(small.here()[0:1, :], (32, 128))
    for p in range(16):
        mover.start(row_ref, first_ref.at[p])


def spread_kernel(
    mover, core_ref, own, high, low, both, memory, memory2, other_ref, ffn_ref, memory_4_ref
):
    x_at = core_ref[2]
    refs = [x.here() for x in (own, high, low, both)]
    for k, ref in enumerate(refs):
        other_ref[x_at ^ k] = ref[0:64, :]
        ffn_ref[x_at ^ k] = ref[64:240, 0:384]
    mover.send(0)
    mover.send(1)
    for k, ref in enumerate((memory.here(), memory2.here())):
        for p in range(4):
            mover.start(ref, memory_4_ref.at[p, pl.ds(64 * k, 64), :])


def start_place(mover, core, mine_ref, theirs_ref, weights_ref, which):
    numbers = []
    for at, k in enumerate(which):
        numbers.append([])
        for x in range(4):
            xl, xh = x // 2, x % 2
            rows = pl.ds(16 * k, 16)
            for half, ref in ((core, mine_ref), (1 - core, theirs_ref)):
                numbers[-1].append(
                    mover.start(ref.at[:, x, rows, :], weights_ref.at[half, at, xl, :, xh])
                )
    return numbers


def start_place_first(mover, core, x_at, mine_refs, theirs_refs, weights_ref):
    numbers = []
    for at in range(2):
        numbers.append([])
        rows = pl.ds(16 * at, 16)
        for flip in range(4):
            x = x_at ^ flip
            for half, refs in ((core, mine_refs), (1 - core, theirs_refs)):
                target = weights_ref.at[half, at, x // 2, :, x % 2]
                source = refs[flip].at[:, rows, pl.ds(0, HALF)]
                numbers[-1].append(mover.start(source, target))
    return numbers


def placed_halves(mover, weights_ref, at, numbers):
    for number in numbers[at]:
        mover.wait(number)
    return [half_of(weights_ref, at, half) for half in range(2)]


def half_of(weights_ref, at, half):
    return weights_ref[half, at].reshape(D, HALF)


def iotas(rows, cols):
    return [lax.broadcasted_iota(jnp.int32, (rows, cols), k) for k in range(2)]


def one_hot(condition):
    return condition.astype(f32).astype(bf16)


def lanes_of(core, k):
    d, lane = iotas(D, 128)
    return one_hot((lane == 8 * k + d % 8) & ((d // 8) % 2 == core))


def chip_of():
    p, d = iotas(64, D)
    return d // 16 == p


def chip_along(p):
    x, zy = p // 16, p % 16
    return (x // 2) * 32 + zy * 2 + x % 2


def project_kernel(mover, core_ref, tok, *refs):
    mine_refs, theirs_refs, rows_ref = refs[0:4], refs[4:8], refs[8]
    out_ref, gains_ref, table_ref, tokens_ref, weights_ref, small_ref, stage_ref = refs[9:]
    core, head, x_at = (core_ref[k] for k in range(3))
    staged = mover.start(rows_ref.at[:, pl.ds(128, 128), :], stage_ref)
    arrivals = []
    for c, sources in enumerate((mine_refs, theirs_refs)):
        for flip in range(4):
            source = sources[flip].at[:, pl.ds(0, 16), pl.ds(HALF, 128)]
            arrivals.append(mover.start(source, small_ref.at[c, x_at ^ flip]))
    numbers = start_place_first(mover, core, x_at, mine_refs, theirs_refs, weights_ref)
    for number in arrivals:
        mover.wait(number)
    smalls = [(core, small_ref[0, :, :, 0:1, :]), (1 - core, small_ref[1, :, :, 0:1, :])]
    smalls = [(c, small.reshape(64, 128)) for c, small in smalls]
    p, d = iotas(64, D)
    own_chip = d // 16 == chip_along(p)
    gains = []
    for k in range(3):
        spread = sum(dot_nt(small, lanes_of(c, k)) for c, small in smalls)
        gains.append(jnp.sum(jnp.where(own_chip, spread, 0.0), axis=0, keepdims=True))
        gains_ref[k : k + 1, :] = gains[-1]
    b, p = iotas(BUCKETS, 64)
    chips = one_hot(chip_along(p) == head * 4 + b // 8)
    b, lane = iotas(BUCKETS, 128)
    column = jnp.zeros((BUCKETS, 1), f32)
    for c, small in smalls:
        hit = (lane == 24 + b % 4) & ((b // 4) % 2 == c)
        found = jnp.where(hit, dot(chips, small), 0.0)
        column = column + jnp.sum(found, axis=1, keepdims=True)
    table_ref[...] = jnp.broadcast_to(column, (BUCKETS, 128))
    mover.send(1)
    mover.send(2)

    x = tok.here()[...].reshape(128, D).astype(f32)
    normed = (x * inverse_rms(x) * gains[0]).astype(bf16)
    mover.wait(staged)
    mover.start(stage_ref, tokens_ref)
    wq = placed_halves(mover, weights_ref, 0, numbers)
    for half in range(2):
        q = (dot(normed, wq[half]) * scaling).astype(bf16)
        for k in range(8):
            one = q[:, k * 64 : (k + 1) * 64]
            out_ref[half * 8 + k, 0:64, :] = jnp.concatenate([one[0:64], one[64:128]], axis=1)
    wkv = placed_halves(mover, weights_ref, 1, numbers)
    keys = dot(normed, wkv[0]).astype(bf16)
    values = dot(normed, wkv[1]).astype(bf16)
    for n in range(KV_HEADS):
        both = jnp.concatenate(
            [keys[:, n * 64 : (n + 1) * 64], values[:, n * 64 : (n + 1) * 64]], axis=1
        )
        out_ref[2 * n, 64:192, :] = both
        out_ref[2 * n + 1, 64:192, :] = both


def bias_rows(onehot, table):
    return jnp.sum(onehot * table, axis=0, keepdims=True)


def self_kernel(
    mover, qkv, table, other, turned_ref, seg_ref,
    out_ref, o_ref, other_out_ref, p_out_ref, p_ref,
):
    numbers = lax.broadcasted_iota(jnp.int32, (BUCKETS, SEQ), 0)
    onehot = (numbers == turned_ref[...]).astype(f32)
    terms = bias_rows(onehot, table.here()[:, 0:1])
    bias = pltpu.roll(
        jnp.broadcast_to(terms, (BLOCK, SEQ)), 0, 1, stride=1, stride_axis=0
    )
    row = lax.broadcasted_iota(jnp.int32, (BLOCK, BLOCK), 0)
    col = lax.broadcasted_iota(jnp.int32, (BLOCK, BLOCK), 1)
    blocks = [jnp.where(col <= row, bias[:, 0:BLOCK], masked_score)]
    for k in range(1, 4):
        blocks.append(bias[:, SEQ - k * BLOCK : SEQ - (k - 1) * BLOCK])
    same_place = row == col
    qkv_ref = qkv.here()
    for mb in range(2):
        kv = qkv_ref[:, 64 + 64 * mb : 128 + 64 * mb, :].reshape(SEQ, 128)
        keys, values = kv[:, 0:64], kv[:, 64:128]
        segments = seg_ref[mb : mb + 1, :].astype(f32)
        for i in range(4):
            length = (i + 1) * BLOCK
            q = qkv_ref[4 * i : 4 * i + 4, 0:64, :].reshape(BLOCK, 128)
            q = q[:, mb * 64 : (mb + 1) * 64]
            s = dot_nt(q, keys[0:length])
            terms_here = jnp.concatenate([blocks[i - j] for j in range(i + 1)], axis=1)
            seg_q = jnp.where(same_place, segments[:, i * BLOCK : (i + 1) * BLOCK], 0.0)
            seg_q = jnp.sum(seg_q, axis=1, keepdims=True)
            s = jnp.where(seg_q == segments[:, 0:length], s + terms_here, masked_score)
            top = jnp.max(s, axis=-1, keepdims=True)
            e = jnp.exp(s - top)
            total = jnp.sum(e, axis=-1, keepdims=True)
            p = (e * (1.0 / total)).astype(bf16)
            p_ref[mb, i * BLOCK : (i + 1) * BLOCK, 0:length] = p
            o = dot(p, values[0:length])
            o_ref[i * BLOCK : (i + 1) * BLOCK, mb * 64 : (mb + 1) * 64] = o
            out_ref[4 * i : 4 * i + 4, :, mb * 64 : (mb + 1) * 64] = o.astype(bf16).reshape(
                4, 64, 64
            )
        mover.start(p_ref.at[mb], p_out_ref.at[mb])
        if mb == 0:
            mover.start(other.here(), other_out_ref)


def self_back_kernel(
    mover, go, qkv, o, p_all, turned_ref, out_ref, table_ref, diag_ref
):
    diag_ref[...] = jnp.zeros_like(diag_ref)
    qkv_ref, go_ref, o_ref, p_ref = qkv.here(), go.here(), o.here(), p_all.here()
    for mb in range(2):
        lanes = slice(mb * 64, (mb + 1) * 64)
        kv = qkv_ref[:, 64 + 64 * mb : 128 + 64 * mb, :].reshape(SEQ, 128)
        keys, values = kv[:, 0:64], kv[:, 64:128]
        grad_keys = [jnp.zeros((BLOCK, 64), f32) for _ in range(4)]
        grad_values = [jnp.zeros((BLOCK, 64), f32) for _ in range(4)]
        for i in range(4):
            length = (i + 1) * BLOCK
            q = qkv_ref[4 * i : 4 * i + 4, 0:64, :].reshape(BLOCK, 128)[:, lanes]
            go = go_ref[4 * i : 4 * i + 4, :, :].reshape(BLOCK, 128)[:, lanes]
            o = o_ref[i * BLOCK : (i + 1) * BLOCK, lanes]
            centre = jnp.sum(go.astype(f32) * o, axis=-1, keepdims=True)
            p = p_ref[mb, i * BLOCK : (i + 1) * BLOCK, 0:length]
            ds = p.astype(f32) * (dot_nt(go, values[0:length]) - centre)
            for j in range(i + 1):
                diag_ref[i - j] += ds[:, j * BLOCK : (j + 1) * BLOCK]
            ds = ds.astype(bf16)
            gq = (dot(ds, keys[0:length]) * scaling).astype(bf16)
            out_ref[4 * i : 4 * i + 4, 0:64, lanes] = gq.reshape(4, 64, 64)
            for j in range(i + 1):
                part = slice(j * BLOCK, (j + 1) * BLOCK)
                grad_keys[j] += dot_tn(ds[:, part], q)
                grad_values[j] += dot_tn(p[:, part], go)
        for j in range(4):
            both = jnp.concatenate([grad_keys[j], grad_values[j]], axis=1).astype(bf16)
            out_ref[4 * j : 4 * j + 4, 64 + 64 * mb : 128 + 64 * mb, :] = both.reshape(4, 64, 128)
    mover.send(0)
    total = jnp.zeros((8, SEQ), f32)
    for g in range(BLOCK // 8):
        rows = slice(8 * g, 8 * g + 8)
        line = jnp.concatenate(
            [diag_ref[0, rows], diag_ref[3, rows], diag_ref[2, rows], diag_ref[1, rows]], axis=1
        )
        total = total + pltpu.roll(line, (SEQ - 8 * g) % SEQ, 1)
    sums = total[0:1]
    for s in range(1, 8):
        sums = sums + pltpu.roll(total[s : s + 1], SEQ - s, 1)
    numbers = lax.broadcasted_iota(jnp.int32, (BUCKETS, SEQ), 0)
    onehot = (numbers == turned_ref[...]).astype(f32)
    sums = jnp.sum(onehot * sums, axis=1, keepdims=True)
    table_ref[...] = jnp.broadcast_to(sums, (BUCKETS, 128))


def start_memory(mover, mem_ref, mem2_ref, pieces_ref):
    return [
        mover.start(ref.at[:, pl.ds(64 * x, 64), :], pieces_ref.at[c, x])
        for c, ref in enumerate((mem_ref, mem2_ref))
        for x in range(2)
    ]


def memory_kernel(
    mover, core_ref, mem_ref, mem2_ref, mine_ref, theirs_ref, out_ref, weights_ref, pieces_ref
):
    arrivals = start_memory(mover, mem_ref, mem2_ref, pieces_ref)
    numbers = start_place(mover, core_ref[0], mine_ref, theirs_ref, weights_ref, (2,))
    for number in arrivals:
        mover.wait(number)
    wckv = placed_halves(mover, weights_ref, 0, numbers)
    for mb in range(2):
        rows = pieces_ref[:, :, :, 32 * mb : 32 * mb + 32, :].reshape(MEM, D)
        keys = dot(rows, wckv[0]).astype(bf16)
        values = dot(rows, wckv[1]).astype(bf16)
        for n in range(KV_HEADS):
            part = slice(n * 64, (n + 1) * 64)
            out_ref[mb, n] = jnp.concatenate([keys[:, part], values[:, part]], axis=1)


def middle_kernel(
    mover, core_ref, att, tok, gains, kv_all, mine_ref, theirs_ref,
    lefts_ref, after_self_ref, queries_ref, p_ref, after_cross_ref, normed_ffn_ref,
    weights_ref, normed_row_ref,
):
    numbers = start_place(mover, core_ref[0], mine_ref, theirs_ref, weights_ref, (0, 1, 3))
    attended_ref, normed_cross_ref, crossed_ref = (lefts_ref.at[k] for k in range(3))
    att_ref, tok_ref, gains_ref = att.here(), tok.here(), gains.here()
    for h in range(HEADS):
        for mb in range(2):
            attended_ref[mb * 64 : (mb + 1) * 64, h * 64 : (h + 1) * 64] = att_ref[
                h, :, mb * 64 : (mb + 1) * 64
            ]
    attended = attended_ref[...]
    x = tok_ref[...].reshape(128, D).astype(f32)
    wo = placed_halves(mover, weights_ref, 0, numbers)
    after_self = x + jnp.concatenate([dot(attended, wo[0]), dot(attended, wo[1])], axis=1)
    after_self_ref[...] = after_self
    mover.send(1)
    normed = (after_self * inverse_rms(after_self) * gains_ref[1:2, :]).astype(bf16)
    normed_cross_ref[...] = normed
    wcq = placed_halves(mover, weights_ref, 1, numbers)
    for half in range(2):
        q = (dot(normed, wcq[half]) * scaling).astype(bf16)
        queries_ref[:, half * HALF : (half + 1) * HALF] = q
    mover.send(2)
    kv_ref = kv_all.here()
    for mb in range(2):
        rows = slice(mb * 64, (mb + 1) * 64)
        for n in range(KV_HEADS):
            first = slice(2 * n * 64, (2 * n + 1) * 64)
            second = slice((2 * n + 1) * 64, (2 * n + 2) * 64)
            q = jnp.concatenate([queries_ref[rows, first], queries_ref[rows, second]], axis=0)
            kv = kv_ref[mb, n]
            s = dot_nt(q, kv[:, 0:64])
            e = jnp.exp(s - jnp.max(s, axis=-1, keepdims=True))
            p = (e * (1.0 / jnp.sum(e, axis=-1, keepdims=True))).astype(bf16)
            p_ref[mb, n] = p
            o = dot(p, kv[:, 64:128]).astype(bf16)
            crossed_ref[rows, first] = o[0:64]
            crossed_ref[rows, second] = o[64:128]
    mover.send(3)
    mover.send(0)
    crossed = crossed_ref[...]
    wco = placed_halves(mover, weights_ref, 2, numbers)
    after_cross = after_self + jnp.concatenate([dot(crossed, wco[0]), dot(crossed, wco[1])], axis=1)
    after_cross_ref[...] = after_cross
    mover.send(4)
    normed = after_cross * inverse_rms(after_cross) * gains_ref[2:3, :]
    normed_row_ref[...] = normed.astype(bf16)
    for k in range(4):
        mover.start(normed_row_ref, normed_ffn_ref.at[k])


def start_cotangents(mover, sources, targets):
    return [
        mover.start(source.at[:, pl.ds(0, 128), :], target)
        for source, target in zip(sources, targets)
    ]


def ffn_kernel(
    mover, w, x, x2, rows_ref, rows2_ref,
    back_ref, back2_ref, hidden_ref, grad_gate_ref, grad_up_ref, weights_ref, g_ref, g2_ref,
):
    arrivals = start_cotangents(mover, (rows_ref, rows2_ref), (g_ref, g2_ref))
    w_ref = w.here()
    for z in range(4):
        for along in range(4):
            t = (along // 2) * 4 + z
            rows = slice((along % 2) * 176, (along % 2) * 176 + 176)
            for k in range(3):
                weights_ref[k, rows, t * 128 : (t + 1) * 128] = w_ref[
                    z, along, :, k * 128 : (k + 1) * 128
                ]

    def tokens(at, x, g, rows, back_ref):
        gate = dot_nt(x, weights_ref[0])
        up = dot_nt(x, weights_ref[1])
        grad_hidden = dot_nt(g, weights_ref[2])
        const = 0.7978845608028654
        inner = const * (gate + 0.044715 * gate * gate * gate)
        tanh = jnp.tanh(inner)
        gelu = 0.5 * gate * (1.0 + tanh)
        slope = 0.5 * (1.0 + tanh) + 0.5 * gate * (1.0 - tanh * tanh) * const * (
            1.0 + 3 * 0.044715 * gate * gate
        )
        hidden_ref[at, rows, :] = (gelu * up).astype(bf16)
        grad_gate = (grad_hidden * up * slope).astype(bf16)
        grad_up = (grad_hidden * gelu).astype(bf16)
        grad_gate_ref[at, rows, :] = grad_gate
        grad_up_ref[at, rows, :] = grad_up
        back = dot(grad_gate, weights_ref[0]) + dot(grad_up, weights_ref[1])
        back_ref[rows, :] = back.astype(bf16)

    mover.send(5)
    sides = ((x2, g2_ref, back2_ref, 1), (x, g_ref, back_ref, 0))
    for x, g, back, at in sides:
        x = x.here()
        mover.wait(arrivals[at])

        def step(i, carry, at=at, x=x, g=g, back=back):
            rows = pl.ds(pl.multiple_of(i * 256, 256), 256)
            two = g[pl.ds(2 * i, 2)].reshape(256, D)
            tokens(at, x[rows, :], two, rows, back)
            return carry

        lax.fori_loop(0, 2, step, 0)
        mover.send(at)


def ffn_rest_kernel(
    mover, hidden, weights, x, x2, grad_gate, grad_up, rows_ref, rows2_ref,
    out2_ref, out_ref, grads_ref, g_ref, g2_ref,
):
    arrivals = start_cotangents(mover, (rows_ref, rows2_ref), (g_ref, g2_ref))
    hidden_ref, weights_ref = hidden.here(), weights.here()
    for at, ref in ((1, out2_ref), (0, out_ref)):
        ref[...] = dot(hidden_ref[at], weights_ref[2]).astype(bf16)
        mover.send(1 - at)
    x_ref, x2_ref = x.here(), x2.here()
    for number in arrivals:
        mover.wait(number)
    grad_gate_ref, grad_up_ref = grad_gate.here(), grad_up.here()
    for t in range(8):
        xl, z = t // 4, t % 4
        cols = slice(t * 128, (t + 1) * 128)
        x_cols = (x_ref[:, cols], x2_ref[:, cols])
        g_cols = (g_ref[:, :, cols].reshape(512, 128), g2_ref[:, :, cols].reshape(512, 128))
        sides = ((grad_gate_ref, x_cols), (grad_up_ref, x_cols), (hidden_ref, g_cols))
        for k, (left, right) in enumerate(sides):
            part = (dot_tn(left[0], right[0]) + dot_tn(left[1], right[1])).astype(bf16)
            for xh in range(2):
                grads_ref[z, xl * 2 + xh, :, k * 128 : (k + 1) * 128] = part[
                    xh * 176 : (xh + 1) * 176
                ]


def middle_back_kernel(
    mover, core_ref, parts, cot, after_cross, gains, queries, after_self,
    mine_ref, theirs_ref, kv_all_ref, p_all_ref,
    att_ref, rights_ref, grad_kv_ref, grad_after_self_ref, grad_gains_ref,
    grad_crossed_ref, weights_ref, kv_ref, p_ref,
):
    xh = core_ref[2] % 2
    numbers = start_place(mover, core_ref[0], mine_ref, theirs_ref, weights_ref, (3,))
    arrivals = [mover.start(kv_all_ref, kv_ref), mover.start(p_all_ref, p_ref)]
    later = weights_ref.at[:, pl.ds(1, 2)]
    numbers += start_place(mover, core_ref[0], mine_ref, theirs_ref, later, (1, 0))
    self_branch_ref, grad_queries_ref, cross_branch_ref = (rights_ref.at[k] for k in range(3))
    parts_ref, gains_ref = parts.here(), gains.here()
    e = parts_ref[0].astype(f32)
    for k in range(1, 4):
        e = e + parts_ref[k].astype(f32)
    grad_a, grad_gain = norm_back(after_cross.here()[...], gains_ref[2:3, :], e)
    grad_gains_ref[1:2, :] = grad_gain
    grad_after_cross = cot.here()[...].reshape(128, D).astype(f32) + grad_a
    branch = grad_after_cross.astype(bf16)
    cross_branch_ref[...] = branch
    wco = placed_halves(mover, weights_ref, 0, numbers)
    grad_crossed_ref[...] = (
        dot_nt(branch[:, 0:HALF], wco[0]) + dot_nt(branch[:, HALF:], wco[1])
    ).astype(bf16)
    queries_ref = queries.here()
    for number in arrivals:
        mover.wait(number)
    for mb in range(2):
        rows = slice(mb * 64, (mb + 1) * 64)
        for n in range(KV_HEADS):
            first = slice(2 * n * 64, (2 * n + 1) * 64)
            second = slice((2 * n + 1) * 64, (2 * n + 2) * 64)
            q = jnp.concatenate([queries_ref[rows, first], queries_ref[rows, second]], axis=0)
            go = jnp.concatenate(
                [grad_crossed_ref[rows, first], grad_crossed_ref[rows, second]], axis=0
            )
            kv = kv_ref[mb, n]
            p = p_ref[mb, n]
            wide = p.astype(f32)
            gp = dot_nt(go, kv[:, 64:128])
            centre = jnp.sum(wide * gp, axis=-1, keepdims=True)
            ds = (wide * (gp - centre)).astype(bf16)
            gq = (dot(ds, kv[:, 0:64]) * scaling).astype(bf16)
            grad_queries_ref[rows, first] = gq[0:64]
            grad_queries_ref[rows, second] = gq[64:128]
            gk = dot_tn(ds, q).astype(bf16).reshape(2, 2, 4, 32, 64)
            gv = dot_tn(p, go).astype(bf16).reshape(2, 2, 4, 32, 64)
            for x in range(2):
                at = xh ^ x
                grad_kv_ref[:, :, at, mb, :, n * 64 : (n + 1) * 64] = gk[:, x]
                grad_kv_ref[:, :, at, mb, :, HALF + n * 64 : HALF + (n + 1) * 64] = gv[:, x]
    mover.send(2)
    gq = grad_queries_ref[...]
    wcq = placed_halves(mover, weights_ref, 1, numbers)
    e = dot_nt(gq[:, 0:HALF], wcq[0]) + dot_nt(gq[:, HALF:], wcq[1])
    grad_a, grad_gain = norm_back(after_self.here()[...], gains_ref[1:2, :], e)
    grad_gains_ref[0:1, :] = grad_gain
    grad_after_self = grad_after_cross + grad_a
    grad_after_self_ref[...] = grad_after_self
    mover.send(3)
    branch = grad_after_self.astype(bf16)
    self_branch_ref[...] = branch
    mover.send(1)
    wo = placed_halves(mover, weights_ref, 2, numbers)
    back = (dot_nt(branch[:, 0:HALF], wo[0]) + dot_nt(branch[:, HALF:], wo[1])).astype(bf16)
    for h in range(HEADS):
        one = back[:, h * 64 : (h + 1) * 64]
        att_ref[h] = jnp.concatenate([one[0:64], one[64:128]], axis=1)


def half_columns(core, x):
    return jnp.where(core == 0, x[:, 0:HALF], x[:, HALF:])


def weights_kernel(
    mover, core_ref, lefts, lefts2, rights, rights2, grad_kv, grad_kv2, part, part2,
    mem_ref, mem2_ref, out_ref, whole_ref, grad_mem_ref, pieces_ref,
):
    core, xh = core_ref[0], core_ref[2] % 2
    arrivals = start_memory(mover, mem_ref, mem2_ref, pieces_ref)
    rights_ref, rights2_ref = rights.here(), rights2.here()
    lefts_ref, lefts2_ref = lefts.here(), lefts2.here()

    def put(k, whole):
        whole = whole.astype(bf16).reshape(2, 4, 8, 16, HALF)
        for xl in range(2):
            out_ref[:, 8 * xl : 8 * xl + 8, 16 * k : 16 * k + 16, :] = whole[xl]

    for k in range(3):
        left = jnp.concatenate([lefts_ref[k], lefts2_ref[k]], axis=0)
        right = jnp.concatenate(
            [half_columns(core, rights_ref[k]), half_columns(core, rights2_ref[k])], axis=0
        )
        put((0, 1, 3)[k], dot_tn(left, right))
    total = jnp.zeros((D, HALF), f32)
    kv_ref, kv2_ref = grad_kv.here(), grad_kv2.here()
    grad_mem_ref[...] = (kv_ref[0].astype(f32) + kv2_ref[1].astype(f32)).astype(bf16)
    mover.send(2)
    for number in arrivals:
        mover.wait(number)
    for c in range(2):
        for x in range(2):
            at = xh ^ x
            own = half_columns(core, kv_ref[c, :, at].reshape(256, D)).astype(f32)
            both = own + half_columns(core, kv2_ref[1 - c, :, at].reshape(256, D)).astype(f32)
            total = total + dot_tn(pieces_ref[c, x].reshape(256, D), both.astype(bf16))
    put(2, total)
    whole_ref[...] = (part.here()[...].astype(f32) + part2.here()[...].astype(f32)).astype(bf16)


def memory_back_kernel(mover, core_ref, parts, mine_ref, theirs_ref, out_ref, weights_ref):
    numbers = start_place(mover, core_ref[0], mine_ref, theirs_ref, weights_ref, (2,))
    parts_ref = parts.here()
    grad = parts_ref[0].astype(f32)
    for k in range(1, 8):
        grad = grad + parts_ref[k].astype(f32)
    grad = grad.reshape(64, D).astype(bf16)
    wckv = placed_halves(mover, weights_ref, 0, numbers)
    whole = dot_nt(grad[:, 0:HALF], wckv[0]) + dot_nt(grad[:, HALF:], wckv[1])
    out_ref[...] = whole.reshape(2, 32, D)


def unpack(back_ref, out_ref):
    for h in range(HEADS):
        for mb in range(2):
            out_ref[0, mb * 64 : (mb + 1) * 64, h * 64 : (h + 1) * 64] = back_ref[
                h, 0:64, mb * 64 : (mb + 1) * 64
            ]
    for n in range(KV_HEADS):
        both = back_ref[2 * n, 64:192, :].astype(f32) + back_ref[2 * n + 1, 64:192, :].astype(f32)
        both = both.astype(bf16)
        out_ref[1, :, n * 64 : (n + 1) * 64] = both[:, 0:64]
        out_ref[1, :, HALF + n * 64 : HALF + (n + 1) * 64] = both[:, 64:128]


def head_grads_kernel(
    mover, core_ref, back, gains, rows_ref, rows2_ref, far_ref, far2_ref, out_ref, *tokens_refs
):
    core, xh = core_ref[0], core_ref[2] % 2
    near = pl.ds(128, 128)
    sources = (rows_ref.at[:, near, :], rows2_ref.at[:, near, :], far_ref, far2_ref)
    numbers = [mover.start(*pair) for pair in zip(sources, tokens_refs)]
    back_ref = back.here()
    gain = gains.here()[0:1, :]
    total = jnp.zeros((D, 192), f32)
    for k in range(4):
        mover.wait(numbers[k])
        x = tokens_refs[k][...].reshape(512, D).astype(f32)
        normed = (x * inverse_rms(x) * gain).astype(bf16)
        parts = []
        for y in range(4):
            block = back_ref[(y * 2 + (xh ^ (k // 2))) * 2 + (core ^ (k % 2))]
            for mb in range(2):
                lanes = slice(mb * 64, (mb + 1) * 64)
                keyvals = block[64 + 64 * mb : 128 + 64 * mb]
                parts.append(jnp.concatenate([block[0:64, lanes], keyvals], axis=1))
        total = total + dot_tn(normed, jnp.concatenate(parts, axis=0))
    out_ref[...] = total.astype(bf16)


def last_kernel(mover, core_ref, back, tok, grad_after_self, gains, head_grads, gain_others,
                table, *refs):
    mine_refs, theirs_refs = refs[0:4], refs[4:8]
    grad_tok_ref, sums_ref, rights_ref, weights_ref = refs[8:]
    head = core_ref[1]
    numbers = start_place_first(
        mover, core_ref[0], core_ref[2], mine_refs, theirs_refs, weights_ref
    )
    unpack(back.here(), rights_ref)
    sums_ref[:, 0:192] = head_grads.here()[...]
    gq, gkv = rights_ref[0], rights_ref[1]
    wq = placed_halves(mover, weights_ref, 0, numbers)
    e = dot_nt(gq[:, 0:HALF], wq[0]) + dot_nt(gq[:, HALF:], wq[1])
    wkv = placed_halves(mover, weights_ref, 1, numbers)
    e = e + dot_nt(gkv[:, 0:HALF], wkv[0]) + dot_nt(gkv[:, HALF:], wkv[1])
    x = tok.here()[...].reshape(128, D).astype(f32)
    grad_a, grad_gain = norm_back(x, gains.here()[0:1, :], e)
    grad_tok_ref[...] = (grad_after_self.here()[...] + grad_a).reshape(2, 64, D)
    others_ref = gain_others.here()
    lines = [grad_gain, others_ref[0:1, :], others_ref[1:2, :], jnp.zeros((5, D), f32)]
    lines = jnp.concatenate(lines, axis=0).astype(bf16)
    number, lane = iotas(8, 64)
    extra = dot_tn(lines, one_hot(number == lane))
    d, b = iotas(D, BUCKETS)
    entry = (d // 128) * 64 + ((d // 8) % 16) * 4 + d % 8
    found = one_hot((d % 8 < 4) & (entry == head * BUCKETS + b))
    b, lane = iotas(BUCKETS, 64)
    column = jnp.where(lane == 3, table.here()[:, 0:64], 0.0).astype(bf16)
    sums_ref[:, 192:256] = (extra + dot(found, column)).astype(bf16)


def finish_kernel(mover, parts, query_ref, keyval_ref, small_ref):
    parts_ref = parts.here()
    total = parts_ref[0:128, :].astype(f32)
    for t in range(1, 8):
        total = total + parts_ref[128 * t : 128 * t + 128, :].astype(f32)
    heads = [total[8 * h : 8 * h + 8] for h in range(HEADS)]
    small_ref[...] = sum(heads)[:, 128:256]
    for h in range(HEADS):
        query_ref[:, h * 64 : (h + 1) * 64] = heads[h][:, 0:64]
    for n in range(KV_HEADS):
        both = heads[2 * n][:, 64:192] + heads[2 * n + 1][:, 64:192]
        keyval_ref[:, n * 64 : (n + 1) * 64] = both[:, 0:64]
        keyval_ref[:, HALF + n * 64 : HALF + (n + 1) * 64] = both[:, 64:128]


def pass_kernel(mover, source, target_ref):
    target_ref[...] = source.here()[...]


def on_device(
    tokens,
    memory,
    segment_ids,
    buckets,
    w_query,
    w_keyval,
    w_output,
    w_cross_query,
    w_cross_keyval,
    w_cross_output,
    norm_self,
    norm_cross,
    norm_ffn,
    bias_table,
    w_gate,
    w_up,
    w_down,
    cotangent,
):
    core = lax.axis_index("c")
    head = (lax.axis_index("y") * 2 + lax.axis_index("xh")) * 2 + core
    x_at = lax.axis_index("xl") * 2 + lax.axis_index("xh")
    places = jnp.stack([core, head, x_at]).astype(jnp.int32)
    placed_1, placed_2, placed_3 = (
        pltpu.VMEM((2, k, 2, 16, 2, 16, HALF), bf16) for k in (1, 2, 3)
    )

    owns = [w_query, w_keyval, w_output, w_cross_query, w_cross_keyval, w_cross_output]
    others = [swap_core(w) for w in owns]
    small = jnp.concatenate([norm_self, norm_cross, norm_ffn, bias_table])
    small = jnp.broadcast_to(jnp.pad(small, (0, 128 - small.shape[0]))[None], (8, 128))
    memory = memory.reshape(64, D)
    memory_far = lax.ppermute(memory, "xh", [(0, 1), (1, 0)])
    later, first = call(
        arrange_kernel,
        (((240, HALF), bf16),),
        *owns, *others, w_gate.T, w_up.T, w_down, small, us=3, core=places,
        raw_outs=(((16, 32, 640), bf16),), scratch=[pltpu.VMEM((32, 640), bf16)],
        after=(memory_far,),
    )
    rows = jnp.concatenate([cotangent.reshape(128, D), tokens.reshape(128, D)], axis=0)
    rows_mine = lax.all_gather(rows, "y", axis=0)
    along_x = flips_x([later, later, later])
    first = exchange(first, ("z", "y"))
    mine_first = (first, *flips_x([first, first, first]))
    theirs_first = tuple(swap_core(x) for x in mine_first)
    other, ffn_part, memory_4 = call(
        spread_kernel,
        (((4, 64, HALF), bf16), ((4, 176, 384), bf16)),
        later, *along_x, memory, memory_far, us=2, core=places,
        raw_outs=(((4, 128, D), bf16),),
        after=(first,),
    )

    mine_other = lax.all_gather(other, ("z", "y"), axis=0)
    ffn_w = lax.all_gather(ffn_part, "z", axis=0)
    mem_mine = exchange(memory_4, "y")
    mem_theirs = swap_core(mem_mine)

    packed, gains, table, tok_mine = call(
        project_kernel,
        (((16, 192, 128), bf16), ((8, D), f32), ((BUCKETS, 128), f32)),
        tokens, raw=(*mine_first, *theirs_first, rows_mine),
        raw_outs=(((4, 128, D), bf16),),
        scratch=[placed_2, pltpu.VMEM((2, 4, 16, 16, 128), bf16), pltpu.VMEM((4, 128, D), bf16)],
        us=5, core=places, after=(mem_mine,),
    )
    qkv = exchange(packed, FFN)
    turned = jnp.roll(buckets[::-1], 1).reshape(1, SEQ)
    att, o_self, mine_other, p_self = call(
        self_kernel,
        (((16, 64, 128), bf16), ((SEQ, 128), f32)),
        qkv, table, mine_other, small=(turned, segment_ids), us=8,
        raw_outs=(((16, 4, 64, HALF), bf16), ((2, SEQ, SEQ), bf16)),
        scratch=[pltpu.VMEM((2, SEQ, SEQ), bf16)],
    )
    att = exchange(att, FFN)
    theirs_other = swap_core(mine_other)

    rows_theirs = swap_core(rows_mine)
    far_mine = lax.ppermute(tok_mine, "xh", [(0, 1), (1, 0)])
    far_theirs = swap_core(far_mine)
    (kv_mem,) = call(
        memory_kernel,
        (((2, 8, MEM, 128), bf16),),
        raw=(mem_mine, mem_theirs, mine_other, theirs_other),
        scratch=[placed_1, pltpu.VMEM((2, 2, 4, 64, D), bf16)], us=5, core=places,
    )
    lefts, after_self, queries, p_cross, after_cross, normed_ffn = call(
        middle_kernel,
        (
            ((3, 128, D), bf16), ((128, D), f32), ((128, D), bf16), ((2, 8, 128, MEM), bf16),
            ((128, D), f32),
        ),
        att, tokens, gains, kv_mem, raw=(mine_other, theirs_other),
        raw_outs=(((4, 128, D), bf16),),
        scratch=[placed_3, pltpu.VMEM((128, D), bf16)], us=12, core=places,
    )

    x_mine = exchange(normed_ffn, "y").reshape(512, D)
    x_theirs = swap_core(x_mine)
    back, back2, hidden, grad_gate, grad_up, ffn_used = call(
        ffn_kernel,
        (
            ((512, D), bf16), ((512, D), bf16), ((2, 512, 352), bf16), ((2, 512, 352), bf16),
            ((2, 512, 352), bf16), ((3, 352, D), bf16),
        ),
        ffn_w, x_mine, x_theirs, raw=(rows_mine, rows_theirs),
        scratch=[pltpu.VMEM((4, 128, D), bf16)] * 2, us=10,
    )
    back = (back.astype(f32) + swap_core(back2).astype(f32)).astype(bf16)
    grad_normed_ffn = exchange(back.reshape(4, 128, D), "y")

    out2, out, ffn_grads = call(
        ffn_rest_kernel,
        (((512, D), bf16), ((512, D), bf16), ((4, 4, 176, 384), bf16)),
        hidden, ffn_used, x_mine, x_theirs, grad_gate, grad_up, raw=(rows_mine, rows_theirs),
        scratch=[pltpu.VMEM((4, 128, D), bf16)] * 2, us=11, after=(back,),
    )
    ffn_rows = lax.psum_scatter(
        ffn_grads.reshape(4 * 704, 384), "z", scatter_dimension=0, tiled=True
    )

    att, rights, grad_kv, grad_after_self, gain_grads = call(
        middle_back_kernel,
        (
            ((16, 64, 128), bf16), ((3, 128, D), bf16), ((2, 4, 2, 2, 32, D), bf16),
            ((128, D), f32), ((8, D), f32),
        ),
        grad_normed_ffn, cotangent, after_cross, gains, queries, after_self,
        raw=(mine_other, theirs_other, kv_mem, p_cross),
        scratch=[pltpu.VMEM((128, D), bf16), placed_3, pltpu.VMEM((2, 8, MEM, 128), bf16),
                 pltpu.VMEM((2, 8, 128, MEM), bf16)],
        us=15, core=places, after=(ffn_grads, far_mine),
    )
    go = exchange(att, FFN)
    grad_kv2 = swap_core(grad_kv)

    grads_other, out, grad_mem = call(
        weights_kernel,
        (((4, 16, 64, HALF), bf16), ((512, D), bf16), ((4, 2, 2, 32, D), bf16)),
        lefts, swap_core(lefts), rights, swap_core(rights), grad_kv, grad_kv2, out,
        swap_core(out2), raw=(mem_mine, mem_theirs),
        scratch=[pltpu.VMEM((2, 2, 4, 64, D), bf16)],
        us=9, core=places, after=(go, ffn_rows),
    )
    grad_mem = exchange(grad_mem.reshape(8, 2, 32, D), ("y", "xh"))

    back, grad_table = call(
        self_back_kernel,
        (((16, 192, 128), bf16), ((BUCKETS, 128), f32)),
        go, qkv, o_self, p_self, small=(turned,),
        scratch=[pltpu.VMEM((4, BLOCK, BLOCK), f32)], us=7,
    )


    (back,) = call(pass_kernel, (((16, 192, 128), bf16),), back, us=1, after=(grad_mem,))
    out_here = lax.psum_scatter(out, "y", scatter_dimension=0, tiled=True)
    output = (after_cross + out_here.astype(f32)).reshape(2, 64, D)

    rows_other = lax.psum_scatter(
        grads_other.reshape(16 * 256, HALF), "z", scatter_dimension=0, tiled=True
    )

    (head_grads,) = call(
        head_grads_kernel,
        (((D, 192), bf16),),
        back, gains, raw=(rows_mine, rows_theirs, far_mine, far_theirs),
        scratch=[pltpu.VMEM((4, 128, D), bf16)] * 4, us=4, core=places,
    )
    back = exchange(back, FFN)
    (grad_memory,) = call(
        memory_back_kernel,
        (((2, 32, D), f32),),
        grad_mem, raw=(mine_other, theirs_other), scratch=[placed_1], us=3, core=places,
    )
    grad_tokens, sums = call(
        last_kernel,
        (((2, 64, D), f32), ((D, 256), bf16)),
        back, tokens, grad_after_self, gains, head_grads, gain_grads, grad_table,
        raw=(*mine_first, *theirs_first), scratch=[pltpu.VMEM((2, 128, D), bf16), placed_2],
        us=6, core=places, after=(rows_other,),
    )

    grad_query, grad_keyval, small = call(
        finish_kernel,
        (((8, D), f32), ((8, D), f32), ((8, 128), f32)),
        exchange(sums, EVERY), us=1,
    )

    others = sum_of_all(rows_other.reshape(16, 64, HALF), ("xl", "y", "xh"))
    ffn_final = sum_over_x(ffn_rows.reshape(4, 176, 384), x_at)

    def own_rows(rows):
        kept = jnp.where(core == 0, rows[:, 0:8], rows[:, 8:16])
        given = swap_core(jnp.where(core == 0, rows[:, 8:16], rows[:, 0:8]))
        return jnp.where(
            core == 0,
            jnp.concatenate([kept, given], axis=2),
            jnp.concatenate([given, kept], axis=2),
        )

    others = own_rows(others.reshape(4, 16, HALF))
    return (
        output,
        grad_tokens,
        grad_memory,
        grad_query,
        grad_keyval,
        others[0],
        others[1],
        others[2],
        others[3],
        small[:, 64],
        small[:, 65],
        small[:, 66],
        small[0:4, 67],
        ffn_final[:, 0:128].T,
        ffn_final[:, 128:256].T,
        ffn_final[:, 256:384],
    )


def solution(mesh):
    names = Mesh(mesh.devices.reshape(2, 4, 4, 2, 2), EVERY)
    tok, ffn, both = ("xl", "z"), FFN, EVERY
    big, mat, vec = P(None, both, None), P(both, None), P(both)
    fn = jax.shard_map(
        on_device,
        mesh=names,
        in_specs=(
            big, big, P(None, tok), P(), mat, mat, mat, mat, mat, mat, vec, vec, vec, vec,
            P(tok, ffn), P(tok, ffn), P(ffn, tok), big,
        ),
        out_specs=(
            big, big, big, mat, mat, mat, mat, mat, mat, vec, vec, vec, vec,
            P(tok, ffn), P(tok, ffn), P(ffn, tok),
        ),
        check_vma=False,
    )
    return fn
```

```python
import jax
import jax.numpy as jnp
from jax import lax
from jax.experimental import pallas as pl
from jax.experimental.pallas import tpu as pltpu
from jax.sharding import Mesh, PartitionSpec as P

HEADS = 16
HEAD_DIM = 64
BUCKETS = 32
KV_HEADS = 8
D = 1024
HALF = 512
SEQ = 1024
MEM = 512
BLOCK = 256

epsilon = 1e-06
masked_score = -1e30
scaling = HEAD_DIM ** (-0.5)

bf16 = jnp.bfloat16
f32 = jnp.float32

FFN = ("y", "xh", "c")
CHIPS = ("xl", "z", "y", "xh")
EVERY = ("xl", "z", "y", "xh", "c")


def dot(a, b):
    return lax.dot_general(a, b, (((1,), (0,)), ((), ())), preferred_element_type=f32)


def dot_nt(a, b):
    return lax.dot_general(a, b, (((1,), (1,)), ((), ())), preferred_element_type=f32)


def dot_tn(a, b):
    return lax.dot_general(a, b, (((0,), (0,)), ((), ())), preferred_element_type=f32)


def inverse_rms(a):
    return lax.rsqrt(jnp.mean(a * a, axis=-1, keepdims=True) + epsilon)


def norm_back(a, gain, e):
    n = inverse_rms(a)
    weighted = e * gain
    centre = jnp.mean(weighted * a, axis=-1, keepdims=True)
    grad_a = n * weighted - a * (n * n * n * centre)
    grad_gain = jnp.sum(e * a * n, axis=0, keepdims=True)
    return grad_a, grad_gain


class Mover:
    def __init__(self, arrived):
        self.arrived, self.copies, self.waited = arrived, [], []

    def start(self, source, target):
        number = len(self.copies)
        self.copies.append(pltpu.make_async_copy(source, target, self.arrived.at[number]))
        self.waited.append(False)
        self.copies[number].start()
        return number

    def wait(self, number):
        if not self.waited[number]:
            self.copies[number].wait()
            self.waited[number] = True

    def finish(self):
        for number in range(len(self.copies)):
            self.wait(number)


class Near:
    def __init__(self, mover, source, target):
        self.mover, self.target = mover, target
        self.number = mover.start(source, target)

    def here(self):
        self.mover.wait(self.number)
        return self.target


COPIES = 64


def call(kernel, outs, *args, raw=(), small=(), scratch=(), us=5, core=None, after=(), raw_outs=()):
    far, near = pl.BlockSpec(memory_space=pltpu.HBM), pl.BlockSpec(memory_space=pltpu.VMEM)
    operands = [*after, *args, *raw, *small]
    specs = [far] * (len(after) + len(args) + len(raw)) + [near] * len(small)
    leading = 0
    if core is not None:
        leading = 1
        operands = [core, *operands]
        specs = [pl.BlockSpec(memory_space=pltpu.SMEM), *specs]
    buffers = [pltpu.VMEM(x.shape, x.dtype) for x in args]
    buffers += [pltpu.VMEM(shape, dtype) for shape, dtype in outs]

    def body(*refs):
        refs = list(refs)
        take = lambda count: [refs.pop(0) for _ in range(count)]
        places = take(leading)
        take(len(after))
        sources, raws, smalls = take(len(args)), take(len(raw)), take(len(small))
        results, raw_results = take(len(outs)), take(len(raw_outs))
        own = take(len(scratch))
        targets, leaving = take(len(args)), take(len(outs))
        mover = Mover(refs.pop(0))
        sent = {}

        def send(number):
            if number not in sent:
                sent[number] = mover.start(leaving[number], results[number])

        mover.send = send
        nears = [Near(mover, *pair) for pair in zip(sources, targets)]
        kernel(mover, *places, *nears, *raws, *smalls, *leaving, *raw_results, *own)
        for number in range(len(outs)):
            send(number)
        mover.finish()

    return pl.pallas_call(
        body,
        out_shape=tuple(jax.ShapeDtypeStruct(s, t) for s, t in (*outs, *raw_outs)),
        in_specs=specs,
        out_specs=tuple([far] * (len(outs) + len(raw_outs))),
        scratch_shapes=[*scratch, *buffers, pltpu.SemaphoreType.DMA((COPIES,))],
        cost_estimate=pl.CostEstimate(
            flops=us * 2_000_000_000, bytes_accessed=us * 10_000_000, transcendentals=0
        ),
        compiler_params=pltpu.CompilerParams(vmem_limit_bytes=60 * 1024 * 1024),
    )(*operands)


def to_all(x, axes):
    n = lax.axis_size(axes)
    return lax.all_to_all(jnp.broadcast_to(x[None], (n, *x.shape)), axes, 0, 0, tiled=True)


def exchange(x, axes):
    return lax.all_to_all(x, axes, 0, 0, tiled=True)


def sum_of_all(x, axes):
    return jnp.sum(exchange(x, axes).astype(f32), axis=0)


def swap_core(x):
    return lax.ppermute(x, "c", [(0, 1), (1, 0)])


def flips_x(parts):
    flip_high = lax.ppermute(parts[0], "xh", [(0, 1), (1, 0)])
    flip_low = lax.ppermute(parts[1], "xl", [(0, 1), (1, 0)])
    flip_both = lax.ppermute(parts[2], ("xl", "xh"), [(0, 3), (1, 2), (2, 1), (3, 0)])
    return flip_high, flip_low, flip_both


def at_place(x, place):
    return lax.dynamic_index_in_dim(x, place, 0, keepdims=False)


def sum_over_x(x, x_at):
    found = flips_x([at_place(x, x_at ^ k) for k in range(1, 4)])
    total = at_place(x, x_at).astype(f32)
    for part in found:
        total = total + part.astype(f32)
    return total


def both_rows(core_ref, own, other):
    first = core_ref[0] == 0
    pair = [ref.here()[...].astype(f32) for ref in (own, other)]
    pair = [jnp.where(first, rows[:, 0:HALF], rows[:, HALF:]) for rows in pair]
    return jnp.where(
        first, jnp.concatenate(pair, axis=0), jnp.concatenate(pair[::-1], axis=0)
    ).astype(bf16)


def arrange_kernel(mover, core_ref, *refs):
    owns, others, ffns, small = refs[0:6], refs[6:12], refs[12:15], refs[15]
    out_ref, first_ref, row_ref = refs[16:]
    for k in range(4):
        out_ref[16 * k : 16 * k + 16, :] = both_rows(core_ref, owns[k + 2], others[k + 2])
    for k in range(3):
        out_ref[64:240, k * 128 : (k + 1) * 128] = ffns[k].here()[...]
    out_ref[64:240, 384:] = jnp.zeros((176, 128), bf16)
    mover.send(0)
    for k in range(2):
        row_ref[16 * k : 16 * k + 16, 0:HALF] = both_rows(core_ref, owns[k], others[k])
    row_ref[:, HALF:] = jnp.broadcast_to(small.here()[0:1, :], (32, 128))
    for p in range(16):
        mover.start(row_ref, first_ref.at[p])


def spread_kernel(
    mover, core_ref, own, high, low, both, memory, memory2, other_ref, ffn_ref, memory_4_ref
):
    x_at = core_ref[2]
    refs = [x.here() for x in (own, high, low, both)]
    for k, ref in enumerate(refs):
        other_ref[x_at ^ k] = ref[0:64, :]
        ffn_ref[x_at ^ k] = ref[64:240, 0:384]
    mover.send(0)
    mover.send(1)
    for k, ref in enumerate((memory.here(), memory2.here())):
        for p in range(4):
            mover.start(ref, memory_4_ref.at[p, pl.ds(64 * k, 64), :])


def start_place(mover, core, mine_ref, theirs_ref, weights_ref, which):
    numbers = []
    for at, k in enumerate(which):
        numbers.append([])
        for x in range(4):
            xl, xh = x // 2, x % 2
            rows = pl.ds(16 * k, 16)
            for half, ref in ((core, mine_ref), (1 - core, theirs_ref)):
                numbers[-1].append(
                    mover.start(ref.at[:, x, rows, :], weights_ref.at[half, at, xl, :, xh])
                )
    return numbers


def start_place_first(mover, core, x_at, mine_refs, theirs_refs, weights_ref):
    numbers = []
    for at in range(2):
        numbers.append([])
        rows = pl.ds(16 * at, 16)
        for flip in range(4):
            x = x_at ^ flip
            for half, refs in ((core, mine_refs), (1 - core, theirs_refs)):
                target = weights_ref.at[half, at, x // 2, :, x % 2]
                source = refs[flip].at[:, rows, pl.ds(0, HALF)]
                numbers[-1].append(mover.start(source, target))
    return numbers


def placed_halves(mover, weights_ref, at, numbers):
    for number in numbers[at]:
        mover.wait(number)
    return [half_of(weights_ref, at, half) for half in range(2)]


def half_of(weights_ref, at, half):
    return weights_ref[half, at].reshape(D, HALF)


def iotas(rows, cols):
    return [lax.broadcasted_iota(jnp.int32, (rows, cols), k) for k in range(2)]


def one_hot(condition):
    return condition.astype(f32).astype(bf16)


def lanes_of(core, k):
    d, lane = iotas(D, 128)
    return one_hot((lane == 8 * k + d % 8) & ((d // 8) % 2 == core))


def chip_of():
    p, d = iotas(64, D)
    return d // 16 == p


def chip_along(p):
    x, zy = p // 16, p % 16
    return (x // 2) * 32 + zy * 2 + x % 2


def project_kernel(mover, core_ref, tok, *refs):
    mine_refs, theirs_refs, rows_ref = refs[0:4], refs[4:8], refs[8]
    out_ref, gains_ref, table_ref, tokens_ref, weights_ref, small_ref, stage_ref = refs[9:]
    core, head, x_at = (core_ref[k] for k in range(3))
    staged = mover.start(rows_ref.at[:, pl.ds(128, 128), :], stage_ref)
    arrivals = []
    for c, sources in enumerate((mine_refs, theirs_refs)):
        for flip in range(4):
            source = sources[flip].at[:, pl.ds(0, 16), pl.ds(HALF, 128)]
            arrivals.append(mover.start(source, small_ref.at[c, x_at ^ flip]))
    numbers = start_place_first(mover, core, x_at, mine_refs, theirs_refs, weights_ref)
    for number in arrivals:
        mover.wait(number)
    smalls = [(core, small_ref[0, :, :, 0:1, :]), (1 - core, small_ref[1, :, :, 0:1, :])]
    smalls = [(c, small.reshape(64, 128)) for c, small in smalls]
    p, d = iotas(64, D)
    own_chip = d // 16 == chip_along(p)
    gains = []
    for k in range(3):
        spread = sum(dot_nt(small, lanes_of(c, k)) for c, small in smalls)
        gains.append(jnp.sum(jnp.where(own_chip, spread, 0.0), axis=0, keepdims=True))
        gains_ref[k : k + 1, :] = gains[-1]
    b, p = iotas(BUCKETS, 64)
    chips = one_hot(chip_along(p) == head * 4 + b // 8)
    b, lane = iotas(BUCKETS, 128)
    column = jnp.zeros((BUCKETS, 1), f32)
    for c, small in smalls:
        hit = (lane == 24 + b % 4) & ((b // 4) % 2 == c)
        found = jnp.where(hit, dot(chips, small), 0.0)
        column = column + jnp.sum(found, axis=1, keepdims=True)
    table_ref[...] = jnp.broadcast_to(column, (BUCKETS, 128))
    mover.send(1)
    mover.send(2)

    x = tok.here()[...].reshape(128, D).astype(f32)
    normed = (x * inverse_rms(x) * gains[0]).astype(bf16)
    mover.wait(staged)
    mover.start(stage_ref, tokens_ref)
    wq = placed_halves(mover, weights_ref, 0, numbers)
    for half in range(2):
        q = (dot(normed, wq[half]) * scaling).astype(bf16)
        for k in range(8):
            one = q[:, k * 64 : (k + 1) * 64]
            out_ref[half * 8 + k, 0:64, :] = jnp.concatenate([one[0:64], one[64:128]], axis=1)
    wkv = placed_halves(mover, weights_ref, 1, numbers)
    keys = dot(normed, wkv[0]).astype(bf16)
    values = dot(normed, wkv[1]).astype(bf16)
    for n in range(KV_HEADS):
        both = jnp.concatenate(
            [keys[:, n * 64 : (n + 1) * 64], values[:, n * 64 : (n + 1) * 64]], axis=1
        )
        out_ref[2 * n, 64:192, :] = both
        out_ref[2 * n + 1, 64:192, :] = both


def bias_rows(onehot, table):
    return jnp.sum(onehot * table, axis=0, keepdims=True)


def self_kernel(
    mover, qkv, table, other, turned_ref, seg_ref,
    out_ref, o_ref, other_out_ref, p_out_ref, p_ref,
):
    numbers = lax.broadcasted_iota(jnp.int32, (BUCKETS, SEQ), 0)
    onehot = (numbers == turned_ref[...]).astype(f32)
    terms = bias_rows(onehot, table.here()[:, 0:1])
    bias = pltpu.roll(
        jnp.broadcast_to(terms, (BLOCK, SEQ)), 0, 1, stride=1, stride_axis=0
    )
    row = lax.broadcasted_iota(jnp.int32, (BLOCK, BLOCK), 0)
    col = lax.broadcasted_iota(jnp.int32, (BLOCK, BLOCK), 1)
    blocks = [jnp.where(col <= row, bias[:, 0:BLOCK], masked_score)]
    for k in range(1, 4):
        blocks.append(bias[:, SEQ - k * BLOCK : SEQ - (k - 1) * BLOCK])
    same_place = row == col
    qkv_ref = qkv.here()
    for mb in range(2):
        kv = qkv_ref[:, 64 + 64 * mb : 128 + 64 * mb, :].reshape(SEQ, 128)
        keys, values = kv[:, 0:64], kv[:, 64:128]
        segments = seg_ref[mb : mb + 1, :].astype(f32)
        for i in range(4):
            length = (i + 1) * BLOCK
            q = qkv_ref[4 * i : 4 * i + 4, 0:64, :].reshape(BLOCK, 128)
            q = q[:, mb * 64 : (mb + 1) * 64]
            s = dot_nt(q, keys[0:length])
            terms_here = jnp.concatenate([blocks[i - j] for j in range(i + 1)], axis=1)
            seg_q = jnp.where(same_place, segments[:, i * BLOCK : (i + 1) * BLOCK], 0.0)
            seg_q = jnp.sum(seg_q, axis=1, keepdims=True)
            s = jnp.where(seg_q == segments[:, 0:length], s + terms_here, masked_score)
            top = jnp.max(s, axis=-1, keepdims=True)
            e = jnp.exp(s - top)
            total = jnp.sum(e, axis=-1, keepdims=True)
            p = (e * (1.0 / total)).astype(bf16)
            p_ref[mb, i * BLOCK : (i + 1) * BLOCK, 0:length] = p
            o = dot(p, values[0:length])
            o_ref[i * BLOCK : (i + 1) * BLOCK, mb * 64 : (mb + 1) * 64] = o
            out_ref[4 * i : 4 * i + 4, :, mb * 64 : (mb + 1) * 64] = o.astype(bf16).reshape(
                4, 64, 64
            )
        mover.start(p_ref.at[mb], p_out_ref.at[mb])
        if mb == 0:
            mover.start(other.here(), other_out_ref)


def self_back_kernel(
    mover, go, qkv, o, p_all, turned_ref, out_ref, table_ref, diag_ref
):
    diag_ref[...] = jnp.zeros_like(diag_ref)
    qkv_ref, go_ref, o_ref, p_ref = qkv.here(), go.here(), o.here(), p_all.here()
    for mb in range(2):
        lanes = slice(mb * 64, (mb + 1) * 64)
        kv = qkv_ref[:, 64 + 64 * mb : 128 + 64 * mb, :].reshape(SEQ, 128)
        keys, values = kv[:, 0:64], kv[:, 64:128]
        grad_keys = [jnp.zeros((BLOCK, 64), f32) for _ in range(4)]
        grad_values = [jnp.zeros((BLOCK, 64), f32) for _ in range(4)]
        for i in range(4):
            length = (i + 1) * BLOCK
            q = qkv_ref[4 * i : 4 * i + 4, 0:64, :].reshape(BLOCK, 128)[:, lanes]
            go = go_ref[4 * i : 4 * i + 4, :, :].reshape(BLOCK, 128)[:, lanes]
            o = o_ref[i * BLOCK : (i + 1) * BLOCK, lanes]
            centre = jnp.sum(go.astype(f32) * o, axis=-1, keepdims=True)
            p = p_ref[mb, i * BLOCK : (i + 1) * BLOCK, 0:length]
            ds = p.astype(f32) * (dot_nt(go, values[0:length]) - centre)
            for j in range(i + 1):
                diag_ref[i - j] += ds[:, j * BLOCK : (j + 1) * BLOCK]
            ds = ds.astype(bf16)
            gq = (dot(ds, keys[0:length]) * scaling).astype(bf16)
            out_ref[4 * i : 4 * i + 4, 0:64, lanes] = gq.reshape(4, 64, 64)
            for j in range(i + 1):
                part = slice(j * BLOCK, (j + 1) * BLOCK)
                grad_keys[j] += dot_tn(ds[:, part], q)
                grad_values[j] += dot_tn(p[:, part], go)
        for j in range(4):
            both = jnp.concatenate([grad_keys[j], grad_values[j]], axis=1).astype(bf16)
            out_ref[4 * j : 4 * j + 4, 64 + 64 * mb : 128 + 64 * mb, :] = both.reshape(4, 64, 128)
    mover.send(0)
    total = jnp.zeros((8, SEQ), f32)
    for g in range(BLOCK // 8):
        rows = slice(8 * g, 8 * g + 8)
        line = jnp.concatenate(
            [diag_ref[0, rows], diag_ref[3, rows], diag_ref[2, rows], diag_ref[1, rows]], axis=1
        )
        total = total + pltpu.roll(line, (SEQ - 8 * g) % SEQ, 1)
    sums = total[0:1]
    for s in range(1, 8):
        sums = sums + pltpu.roll(total[s : s + 1], SEQ - s, 1)
    numbers = lax.broadcasted_iota(jnp.int32, (BUCKETS, SEQ), 0)
    onehot = (numbers == turned_ref[...]).astype(f32)
    sums = jnp.sum(onehot * sums, axis=1, keepdims=True)
    table_ref[...] = jnp.broadcast_to(sums, (BUCKETS, 128))


def start_memory(mover, mem_ref, mem2_ref, pieces_ref):
    return [
        mover.start(ref.at[:, pl.ds(64 * x, 64), :], pieces_ref.at[c, x])
        for c, ref in enumerate((mem_ref, mem2_ref))
        for x in range(2)
    ]


def memory_kernel(
    mover, core_ref, mem_ref, mem2_ref, mine_ref, theirs_ref, out_ref, weights_ref, pieces_ref
):
    arrivals = start_memory(mover, mem_ref, mem2_ref, pieces_ref)
    numbers = start_place(mover, core_ref[0], mine_ref, theirs_ref, weights_ref, (2,))
    for number in arrivals:
        mover.wait(number)
    wckv = placed_halves(mover, weights_ref, 0, numbers)
    for mb in range(2):
        rows = pieces_ref[:, :, :, 32 * mb : 32 * mb + 32, :].reshape(MEM, D)
        keys = dot(rows, wckv[0]).astype(bf16)
        values = dot(rows, wckv[1]).astype(bf16)
        for n in range(KV_HEADS):
            part = slice(n * 64, (n + 1) * 64)
            out_ref[mb, n] = jnp.concatenate([keys[:, part], values[:, part]], axis=1)


def both_heads(n):
    return [slice((2 * n + k) * 64, (2 * n + k + 1) * 64) for k in range(2)]


def middle_kernel(
    mover, core_ref, att, tok, gains, kv_all, mine_ref, theirs_ref,
    lefts_ref, after_self_ref, queries_ref, p_ref, after_cross_ref, normed_ffn_ref,
    weights_ref, normed_row_ref,
):
    numbers = start_place(mover, core_ref[0], mine_ref, theirs_ref, weights_ref, (0, 1, 3))
    attended_ref, normed_cross_ref, crossed_ref = (lefts_ref.at[k] for k in range(3))
    att_ref, tok_ref, gains_ref = att.here(), tok.here(), gains.here()
    for h in range(HEADS):
        for mb in range(2):
            attended_ref[mb * 64 : (mb + 1) * 64, h * 64 : (h + 1) * 64] = att_ref[
                h, :, mb * 64 : (mb + 1) * 64
            ]
    attended = attended_ref[...]
    x = tok_ref[...].reshape(128, D).astype(f32)
    wo = placed_halves(mover, weights_ref, 0, numbers)
    after_self = x + jnp.concatenate([dot(attended, wo[0]), dot(attended, wo[1])], axis=1)
    after_self_ref[...] = after_self
    mover.send(1)
    normed = (after_self * inverse_rms(after_self) * gains_ref[1:2, :]).astype(bf16)
    normed_cross_ref[...] = normed
    wcq = placed_halves(mover, weights_ref, 1, numbers)
    for half in range(2):
        q = (dot(normed, wcq[half]) * scaling).astype(bf16)
        queries_ref[:, half * HALF : (half + 1) * HALF] = q
    mover.send(2)
    kv_ref = kv_all.here()
    for mb in range(2):
        rows = slice(mb * 64, (mb + 1) * 64)
        scores = []
        for n in range(KV_HEADS):
            first, second = both_heads(n)
            q = jnp.concatenate([queries_ref[rows, first], queries_ref[rows, second]], axis=0)
            scores.append(dot_nt(q, kv_ref[mb, n, :, 0:64]))
        s = jnp.concatenate(scores, axis=0)
        e = jnp.exp(s - jnp.max(s, axis=-1, keepdims=True))
        p = (e * (1.0 / jnp.sum(e, axis=-1, keepdims=True))).astype(bf16)
        p_ref[mb] = p.reshape(KV_HEADS, 128, MEM)
        for n in range(KV_HEADS):
            first, second = both_heads(n)
            o = dot(p[128 * n : 128 * n + 128], kv_ref[mb, n, :, 64:128]).astype(bf16)
            crossed_ref[rows, first] = o[0:64]
            crossed_ref[rows, second] = o[64:128]
    mover.send(3)
    mover.send(0)
    crossed = crossed_ref[...]
    wco = placed_halves(mover, weights_ref, 2, numbers)
    after_cross = after_self + jnp.concatenate([dot(crossed, wco[0]), dot(crossed, wco[1])], axis=1)
    after_cross_ref[...] = after_cross
    mover.send(4)
    normed = after_cross * inverse_rms(after_cross) * gains_ref[2:3, :]
    normed_row_ref[...] = normed.astype(bf16)
    for k in range(4):
        mover.start(normed_row_ref, normed_ffn_ref.at[k])


def start_cotangents(mover, sources, targets):
    return [
        mover.start(source.at[:, pl.ds(0, 128), :], target)
        for source, target in zip(sources, targets)
    ]


def ffn_kernel(
    mover, w, x, x2, rows_ref, rows2_ref,
    back_ref, back2_ref, hidden_ref, grad_gate_ref, grad_up_ref, weights_ref, g_ref, g2_ref,
):
    arrivals = start_cotangents(mover, (rows_ref, rows2_ref), (g_ref, g2_ref))
    w_ref = w.here()
    for z in range(4):
        for along in range(4):
            t = (along // 2) * 4 + z
            rows = slice((along % 2) * 176, (along % 2) * 176 + 176)
            for k in range(3):
                weights_ref[k, rows, t * 128 : (t + 1) * 128] = w_ref[
                    z, along, :, k * 128 : (k + 1) * 128
                ]

    def tokens(at, x, g, rows, back_ref):
        gate = dot_nt(x, weights_ref[0])
        up = dot_nt(x, weights_ref[1])
        grad_hidden = dot_nt(g, weights_ref[2])
        const = 0.7978845608028654
        inner = const * (gate + 0.044715 * gate * gate * gate)
        tanh = jnp.tanh(inner)
        gelu = 0.5 * gate * (1.0 + tanh)
        slope = 0.5 * (1.0 + tanh) + 0.5 * gate * (1.0 - tanh * tanh) * const * (
            1.0 + 3 * 0.044715 * gate * gate
        )
        hidden_ref[at, rows, :] = (gelu * up).astype(bf16)
        grad_gate = (grad_hidden * up * slope).astype(bf16)
        grad_up = (grad_hidden * gelu).astype(bf16)
        grad_gate_ref[at, rows, :] = grad_gate
        grad_up_ref[at, rows, :] = grad_up
        back = dot(grad_gate, weights_ref[0]) + dot(grad_up, weights_ref[1])
        back_ref[rows, :] = back.astype(bf16)

    mover.send(5)
    sides = ((x2, g2_ref, back2_ref, 1), (x, g_ref, back_ref, 0))
    for x, g, back, at in sides:
        x = x.here()
        mover.wait(arrivals[at])

        def step(i, carry, at=at, x=x, g=g, back=back):
            rows = pl.ds(pl.multiple_of(i * 256, 256), 256)
            two = g[pl.ds(2 * i, 2)].reshape(256, D)
            tokens(at, x[rows, :], two, rows, back)
            return carry

        lax.fori_loop(0, 2, step, 0)
        mover.send(at)


def ffn_rest_kernel(
    mover, hidden, weights, x, x2, grad_gate, grad_up, rows_ref, rows2_ref,
    out2_ref, out_ref, grads_ref, g_ref, g2_ref,
):
    arrivals = start_cotangents(mover, (rows_ref, rows2_ref), (g_ref, g2_ref))
    hidden_ref, weights_ref = hidden.here(), weights.here()
    for at, ref in ((1, out2_ref), (0, out_ref)):
        ref[...] = dot(hidden_ref[at], weights_ref[2]).astype(bf16)
        mover.send(1 - at)
    x_ref, x2_ref = x.here(), x2.here()
    for number in arrivals:
        mover.wait(number)
    grad_gate_ref, grad_up_ref = grad_gate.here(), grad_up.here()
    for t in range(8):
        xl, z = t // 4, t % 4
        cols = slice(t * 128, (t + 1) * 128)
        x_cols = (x_ref[:, cols], x2_ref[:, cols])
        g_cols = (g_ref[:, :, cols].reshape(512, 128), g2_ref[:, :, cols].reshape(512, 128))
        sides = ((grad_gate_ref, x_cols), (grad_up_ref, x_cols), (hidden_ref, g_cols))
        for k, (left, right) in enumerate(sides):
            part = (dot_tn(left[0], right[0]) + dot_tn(left[1], right[1])).astype(bf16)
            for xh in range(2):
                grads_ref[z, xl * 2 + xh, :, k * 128 : (k + 1) * 128] = part[
                    xh * 176 : (xh + 1) * 176
                ]


def middle_back_kernel(
    mover, core_ref, parts, cot, after_cross, gains, queries, after_self,
    mine_ref, theirs_ref, kv_all_ref, p_all_ref,
    att_ref, rights_ref, grad_kv_ref, grad_after_self_ref, grad_gains_ref,
    grad_crossed_ref, weights_ref, kv_ref, p_ref,
):
    xh = core_ref[2] % 2
    numbers = start_place(mover, core_ref[0], mine_ref, theirs_ref, weights_ref, (3,))
    arrivals = [mover.start(kv_all_ref, kv_ref), mover.start(p_all_ref, p_ref)]
    later = weights_ref.at[:, pl.ds(1, 2)]
    numbers += start_place(mover, core_ref[0], mine_ref, theirs_ref, later, (1, 0))
    self_branch_ref, grad_queries_ref, cross_branch_ref = (rights_ref.at[k] for k in range(3))
    parts_ref, gains_ref = parts.here(), gains.here()
    e = parts_ref[0].astype(f32)
    for k in range(1, 4):
        e = e + parts_ref[k].astype(f32)
    grad_a, grad_gain = norm_back(after_cross.here()[...], gains_ref[2:3, :], e)
    grad_gains_ref[1:2, :] = grad_gain
    grad_after_cross = cot.here()[...].reshape(128, D).astype(f32) + grad_a
    branch = grad_after_cross.astype(bf16)
    cross_branch_ref[...] = branch
    wco = placed_halves(mover, weights_ref, 0, numbers)
    grad_crossed_ref[...] = (
        dot_nt(branch[:, 0:HALF], wco[0]) + dot_nt(branch[:, HALF:], wco[1])
    ).astype(bf16)
    queries_ref = queries.here()
    for number in arrivals:
        mover.wait(number)
    for mb in range(2):
        rows = slice(mb * 64, (mb + 1) * 64)
        grads = []
        for n in range(KV_HEADS):
            first, second = both_heads(n)
            go = jnp.concatenate(
                [grad_crossed_ref[rows, first], grad_crossed_ref[rows, second]], axis=0
            )
            grads.append(dot_nt(go, kv_ref[mb, n, :, 64:128]))
        gp = jnp.concatenate(grads, axis=0)
        wide = p_ref[mb].reshape(KV_HEADS * 128, MEM).astype(f32)
        centre = jnp.sum(wide * gp, axis=-1, keepdims=True)
        all_ds = (wide * (gp - centre)).astype(bf16)
        for n in range(KV_HEADS):
            first, second = both_heads(n)
            q = jnp.concatenate([queries_ref[rows, first], queries_ref[rows, second]], axis=0)
            go = jnp.concatenate(
                [grad_crossed_ref[rows, first], grad_crossed_ref[rows, second]], axis=0
            )
            ds, p = all_ds[128 * n : 128 * n + 128], p_ref[mb, n]
            gq = (dot(ds, kv_ref[mb, n, :, 0:64]) * scaling).astype(bf16)
            grad_queries_ref[rows, first] = gq[0:64]
            grad_queries_ref[rows, second] = gq[64:128]
            gk = dot_tn(ds, q).astype(bf16).reshape(2, 2, 4, 32, 64)
            gv = dot_tn(p, go).astype(bf16).reshape(2, 2, 4, 32, 64)
            for x in range(2):
                at = xh ^ x
                grad_kv_ref[:, :, at, mb, :, n * 64 : (n + 1) * 64] = gk[:, x]
                grad_kv_ref[:, :, at, mb, :, HALF + n * 64 : HALF + (n + 1) * 64] = gv[:, x]
    mover.send(2)
    gq = grad_queries_ref[...]
    wcq = placed_halves(mover, weights_ref, 1, numbers)
    e = dot_nt(gq[:, 0:HALF], wcq[0]) + dot_nt(gq[:, HALF:], wcq[1])
    grad_a, grad_gain = norm_back(after_self.here()[...], gains_ref[1:2, :], e)
    grad_gains_ref[0:1, :] = grad_gain
    grad_after_self = grad_after_cross + grad_a
    grad_after_self_ref[...] = grad_after_self
    mover.send(3)
    branch = grad_after_self.astype(bf16)
    self_branch_ref[...] = branch
    mover.send(1)
    wo = placed_halves(mover, weights_ref, 2, numbers)
    back = (dot_nt(branch[:, 0:HALF], wo[0]) + dot_nt(branch[:, HALF:], wo[1])).astype(bf16)
    for h in range(HEADS):
        one = back[:, h * 64 : (h + 1) * 64]
        att_ref[h] = jnp.concatenate([one[0:64], one[64:128]], axis=1)


def half_columns(core, x):
    return jnp.where(core == 0, x[:, 0:HALF], x[:, HALF:])


def weights_kernel(
    mover, core_ref, lefts, lefts2, rights, rights2, grad_kv, grad_kv2, part, part2,
    mem_ref, mem2_ref, out_ref, whole_ref, grad_mem_ref, pieces_ref,
):
    core, xh = core_ref[0], core_ref[2] % 2
    arrivals = start_memory(mover, mem_ref, mem2_ref, pieces_ref)
    rights_ref, rights2_ref = rights.here(), rights2.here()
    lefts_ref, lefts2_ref = lefts.here(), lefts2.here()

    def put(k, whole):
        whole = whole.astype(bf16).reshape(2, 4, 8, 16, HALF)
        for xl in range(2):
            out_ref[:, 8 * xl : 8 * xl + 8, 16 * k : 16 * k + 16, :] = whole[xl]

    for k in range(3):
        left = jnp.concatenate([lefts_ref[k], lefts2_ref[k]], axis=0)
        right = jnp.concatenate(
            [half_columns(core, rights_ref[k]), half_columns(core, rights2_ref[k])], axis=0
        )
        put((0, 1, 3)[k], dot_tn(left, right))
    total = jnp.zeros((D, HALF), f32)
    kv_ref, kv2_ref = grad_kv.here(), grad_kv2.here()
    grad_mem_ref[...] = (kv_ref[0].astype(f32) + kv2_ref[1].astype(f32)).astype(bf16)
    mover.send(2)
    for number in arrivals:
        mover.wait(number)
    for c in range(2):
        for x in range(2):
            at = xh ^ x
            own = half_columns(core, kv_ref[c, :, at].reshape(256, D)).astype(f32)
            both = own + half_columns(core, kv2_ref[1 - c, :, at].reshape(256, D)).astype(f32)
            total = total + dot_tn(pieces_ref[c, x].reshape(256, D), both.astype(bf16))
    put(2, total)
    whole_ref[...] = (part.here()[...].astype(f32) + part2.here()[...].astype(f32)).astype(bf16)


def memory_back_kernel(mover, core_ref, parts, mine_ref, theirs_ref, out_ref, weights_ref):
    numbers = start_place(mover, core_ref[0], mine_ref, theirs_ref, weights_ref, (2,))
    parts_ref = parts.here()
    grad = parts_ref[0].astype(f32)
    for k in range(1, 8):
        grad = grad + parts_ref[k].astype(f32)
    grad = grad.reshape(64, D).astype(bf16)
    wckv = placed_halves(mover, weights_ref, 0, numbers)
    whole = dot_nt(grad[:, 0:HALF], wckv[0]) + dot_nt(grad[:, HALF:], wckv[1])
    out_ref[...] = whole.reshape(2, 32, D)


def unpack(back_ref, out_ref):
    for h in range(HEADS):
        for mb in range(2):
            out_ref[0, mb * 64 : (mb + 1) * 64, h * 64 : (h + 1) * 64] = back_ref[
                h, 0:64, mb * 64 : (mb + 1) * 64
            ]
    for n in range(KV_HEADS):
        both = back_ref[2 * n, 64:192, :].astype(f32) + back_ref[2 * n + 1, 64:192, :].astype(f32)
        both = both.astype(bf16)
        out_ref[1, :, n * 64 : (n + 1) * 64] = both[:, 0:64]
        out_ref[1, :, HALF + n * 64 : HALF + (n + 1) * 64] = both[:, 64:128]


def head_grads_kernel(
    mover, core_ref, back, gains, rows_ref, rows2_ref, far_ref, far2_ref, out_ref, *tokens_refs
):
    core, xh = core_ref[0], core_ref[2] % 2
    near = pl.ds(128, 128)
    sources = (rows_ref.at[:, near, :], rows2_ref.at[:, near, :], far_ref, far2_ref)
    numbers = [mover.start(*pair) for pair in zip(sources, tokens_refs)]
    back_ref = back.here()
    gain = gains.here()[0:1, :]
    total = jnp.zeros((D, 192), f32)
    for k in range(4):
        mover.wait(numbers[k])
        x = tokens_refs[k][...].reshape(512, D).astype(f32)
        normed = (x * inverse_rms(x) * gain).astype(bf16)
        parts = []
        for y in range(4):
            block = back_ref[(y * 2 + (xh ^ (k // 2))) * 2 + (core ^ (k % 2))]
            for mb in range(2):
                lanes = slice(mb * 64, (mb + 1) * 64)
                keyvals = block[64 + 64 * mb : 128 + 64 * mb]
                parts.append(jnp.concatenate([block[0:64, lanes], keyvals], axis=1))
        total = total + dot_tn(normed, jnp.concatenate(parts, axis=0))
    out_ref[...] = total.astype(bf16)


def last_kernel(mover, core_ref, back, tok, grad_after_self, gains, head_grads, gain_others,
                table, *refs):
    mine_refs, theirs_refs = refs[0:4], refs[4:8]
    grad_tok_ref, sums_ref, rights_ref, weights_ref = refs[8:]
    head = core_ref[1]
    numbers = start_place_first(
        mover, core_ref[0], core_ref[2], mine_refs, theirs_refs, weights_ref
    )
    unpack(back.here(), rights_ref)
    sums_ref[:, 0:192] = head_grads.here()[...]
    gq, gkv = rights_ref[0], rights_ref[1]
    wq = placed_halves(mover, weights_ref, 0, numbers)
    e = dot_nt(gq[:, 0:HALF], wq[0]) + dot_nt(gq[:, HALF:], wq[1])
    wkv = placed_halves(mover, weights_ref, 1, numbers)
    e = e + dot_nt(gkv[:, 0:HALF], wkv[0]) + dot_nt(gkv[:, HALF:], wkv[1])
    x = tok.here()[...].reshape(128, D).astype(f32)
    grad_a, grad_gain = norm_back(x, gains.here()[0:1, :], e)
    grad_tok_ref[...] = (grad_after_self.here()[...] + grad_a).reshape(2, 64, D)
    others_ref = gain_others.here()
    lines = [grad_gain, others_ref[0:1, :], others_ref[1:2, :], jnp.zeros((5, D), f32)]
    lines = jnp.concatenate(lines, axis=0).astype(bf16)
    number, lane = iotas(8, 64)
    extra = dot_tn(lines, one_hot(number == lane))
    d, b = iotas(D, BUCKETS)
    entry = (d // 128) * 64 + ((d // 8) % 16) * 4 + d % 8
    found = one_hot((d % 8 < 4) & (entry == head * BUCKETS + b))
    b, lane = iotas(BUCKETS, 64)
    column = jnp.where(lane == 3, table.here()[:, 0:64], 0.0).astype(bf16)
    sums_ref[:, 192:256] = (extra + dot(found, column)).astype(bf16)


def finish_kernel(mover, parts, query_ref, keyval_ref, small_ref):
    parts_ref = parts.here()
    total = parts_ref[0:128, :].astype(f32)
    for t in range(1, 8):
        total = total + parts_ref[128 * t : 128 * t + 128, :].astype(f32)
    heads = [total[8 * h : 8 * h + 8] for h in range(HEADS)]
    small_ref[...] = sum(heads)[:, 128:256]
    for h in range(HEADS):
        query_ref[:, h * 64 : (h + 1) * 64] = heads[h][:, 0:64]
    for n in range(KV_HEADS):
        both = heads[2 * n][:, 64:192] + heads[2 * n + 1][:, 64:192]
        keyval_ref[:, n * 64 : (n + 1) * 64] = both[:, 0:64]
        keyval_ref[:, HALF + n * 64 : HALF + (n + 1) * 64] = both[:, 64:128]


def pass_kernel(mover, source, target_ref):
    target_ref[...] = source.here()[...]


def on_device(
    tokens,
    memory,
    segment_ids,
    buckets,
    w_query,
    w_keyval,
    w_output,
    w_cross_query,
    w_cross_keyval,
    w_cross_output,
    norm_self,
    norm_cross,
    norm_ffn,
    bias_table,
    w_gate,
    w_up,
    w_down,
    cotangent,
):
    core = lax.axis_index("c")
    head = (lax.axis_index("y") * 2 + lax.axis_index("xh")) * 2 + core
    x_at = lax.axis_index("xl") * 2 + lax.axis_index("xh")
    places = jnp.stack([core, head, x_at]).astype(jnp.int32)
    placed_1, placed_2, placed_3 = (
        pltpu.VMEM((2, k, 2, 16, 2, 16, HALF), bf16) for k in (1, 2, 3)
    )

    owns = [w_query, w_keyval, w_output, w_cross_query, w_cross_keyval, w_cross_output]
    others = [swap_core(w) for w in owns]
    small = jnp.concatenate([norm_self, norm_cross, norm_ffn, bias_table])
    small = jnp.broadcast_to(jnp.pad(small, (0, 128 - small.shape[0]))[None], (8, 128))
    memory = memory.reshape(64, D)
    memory_far = lax.ppermute(memory, "xh", [(0, 1), (1, 0)])
    later, first = call(
        arrange_kernel,
        (((240, HALF), bf16),),
        *owns, *others, w_gate.T, w_up.T, w_down, small, us=3, core=places,
        raw_outs=(((16, 32, 640), bf16),), scratch=[pltpu.VMEM((32, 640), bf16)],
        after=(memory_far,),
    )
    rows = jnp.concatenate([cotangent.reshape(128, D), tokens.reshape(128, D)], axis=0)
    rows_mine = lax.all_gather(rows, "y", axis=0)
    along_x = flips_x([later, later, later])
    first = exchange(first, ("z", "y"))
    mine_first = (first, *flips_x([first, first, first]))
    theirs_first = tuple(swap_core(x) for x in mine_first)
    other, ffn_part, memory_4 = call(
        spread_kernel,
        (((4, 64, HALF), bf16), ((4, 176, 384), bf16)),
        later, *along_x, memory, memory_far, us=2, core=places,
        raw_outs=(((4, 128, D), bf16),),
        after=(first,),
    )

    mine_other = lax.all_gather(other, ("z", "y"), axis=0)
    ffn_w = lax.all_gather(ffn_part, "z", axis=0)
    mem_mine = exchange(memory_4, "y")
    mem_theirs = swap_core(mem_mine)

    packed, gains, table, tok_mine = call(
        project_kernel,
        (((16, 192, 128), bf16), ((8, D), f32), ((BUCKETS, 128), f32)),
        tokens, raw=(*mine_first, *theirs_first, rows_mine),
        raw_outs=(((4, 128, D), bf16),),
        scratch=[placed_2, pltpu.VMEM((2, 4, 16, 16, 128), bf16), pltpu.VMEM((4, 128, D), bf16)],
        us=5, core=places, after=(mem_mine,),
    )
    qkv = exchange(packed, FFN)
    turned = jnp.roll(buckets[::-1], 1).reshape(1, SEQ)
    att, o_self, mine_other, p_self = call(
        self_kernel,
        (((16, 64, 128), bf16), ((SEQ, 128), f32)),
        qkv, table, mine_other, small=(turned, segment_ids), us=8,
        raw_outs=(((16, 4, 64, HALF), bf16), ((2, SEQ, SEQ), bf16)),
        scratch=[pltpu.VMEM((2, SEQ, SEQ), bf16)],
    )
    att = exchange(att, FFN)
    theirs_other = swap_core(mine_other)

    rows_theirs = swap_core(rows_mine)
    far_mine = lax.ppermute(tok_mine, "xh", [(0, 1), (1, 0)])
    far_theirs = swap_core(far_mine)
    (kv_mem,) = call(
        memory_kernel,
        (((2, 8, MEM, 128), bf16),),
        raw=(mem_mine, mem_theirs, mine_other, theirs_other),
        scratch=[placed_1, pltpu.VMEM((2, 2, 4, 64, D), bf16)], us=5, core=places,
    )
    lefts, after_self, queries, p_cross, after_cross, normed_ffn = call(
        middle_kernel,
        (
            ((3, 128, D), bf16), ((128, D), f32), ((128, D), bf16), ((2, 8, 128, MEM), bf16),
            ((128, D), f32),
        ),
        att, tokens, gains, kv_mem, raw=(mine_other, theirs_other),
        raw_outs=(((4, 128, D), bf16),),
        scratch=[placed_3, pltpu.VMEM((128, D), bf16)], us=12, core=places,
    )

    x_mine = exchange(normed_ffn, "y").reshape(512, D)
    x_theirs = swap_core(x_mine)
    back, back2, hidden, grad_gate, grad_up, ffn_used = call(
        ffn_kernel,
        (
            ((512, D), bf16), ((512, D), bf16), ((2, 512, 352), bf16), ((2, 512, 352), bf16),
            ((2, 512, 352), bf16), ((3, 352, D), bf16),
        ),
        ffn_w, x_mine, x_theirs, raw=(rows_mine, rows_theirs),
        scratch=[pltpu.VMEM((4, 128, D), bf16)] * 2, us=10,
    )
    back = (back.astype(f32) + swap_core(back2).astype(f32)).astype(bf16)
    grad_normed_ffn = exchange(back.reshape(4, 128, D), "y")

    out2, out, ffn_grads = call(
        ffn_rest_kernel,
        (((512, D), bf16), ((512, D), bf16), ((4, 4, 176, 384), bf16)),
        hidden, ffn_used, x_mine, x_theirs, grad_gate, grad_up, raw=(rows_mine, rows_theirs),
        scratch=[pltpu.VMEM((4, 128, D), bf16)] * 2, us=11, after=(back,),
    )
    ffn_rows = lax.psum_scatter(
        ffn_grads.reshape(4 * 704, 384), "z", scatter_dimension=0, tiled=True
    )

    att, rights, grad_kv, grad_after_self, gain_grads = call(
        middle_back_kernel,
        (
            ((16, 64, 128), bf16), ((3, 128, D), bf16), ((2, 4, 2, 2, 32, D), bf16),
            ((128, D), f32), ((8, D), f32),
        ),
        grad_normed_ffn, cotangent, after_cross, gains, queries, after_self,
        raw=(mine_other, theirs_other, kv_mem, p_cross),
        scratch=[pltpu.VMEM((128, D), bf16), placed_3, pltpu.VMEM((2, 8, MEM, 128), bf16),
                 pltpu.VMEM((2, 8, 128, MEM), bf16)],
        us=15, core=places, after=(ffn_grads, far_mine),
    )
    go = exchange(att, FFN)
    grad_kv2 = swap_core(grad_kv)

    grads_other, out, grad_mem = call(
        weights_kernel,
        (((4, 16, 64, HALF), bf16), ((512, D), bf16), ((4, 2, 2, 32, D), bf16)),
        lefts, swap_core(lefts), rights, swap_core(rights), grad_kv, grad_kv2, out,
        swap_core(out2), raw=(mem_mine, mem_theirs),
        scratch=[pltpu.VMEM((2, 2, 4, 64, D), bf16)],
        us=9, core=places, after=(go, ffn_rows),
    )
    grad_mem = exchange(grad_mem.reshape(8, 2, 32, D), ("y", "xh"))

    back, grad_table = call(
        self_back_kernel,
        (((16, 192, 128), bf16), ((BUCKETS, 128), f32)),
        go, qkv, o_self, p_self, small=(turned,),
        scratch=[pltpu.VMEM((4, BLOCK, BLOCK), f32)], us=7,
    )


    (back,) = call(pass_kernel, (((16, 192, 128), bf16),), back, us=1, after=(grad_mem,))
    out_here = lax.psum_scatter(out, "y", scatter_dimension=0, tiled=True)
    output = (after_cross + out_here.astype(f32)).reshape(2, 64, D)

    rows_other = lax.psum_scatter(
        grads_other.reshape(16 * 256, HALF), "z", scatter_dimension=0, tiled=True
    )

    (head_grads,) = call(
        head_grads_kernel,
        (((D, 192), bf16),),
        back, gains, raw=(rows_mine, rows_theirs, far_mine, far_theirs),
        scratch=[pltpu.VMEM((4, 128, D), bf16)] * 4, us=4, core=places,
    )
    back = exchange(back, FFN)
    (grad_memory,) = call(
        memory_back_kernel,
        (((2, 32, D), f32),),
        grad_mem, raw=(mine_other, theirs_other), scratch=[placed_1], us=3, core=places,
    )
    grad_tokens, sums = call(
        last_kernel,
        (((2, 64, D), f32), ((D, 256), bf16)),
        back, tokens, grad_after_self, gains, head_grads, gain_grads, grad_table,
        raw=(*mine_first, *theirs_first), scratch=[pltpu.VMEM((2, 128, D), bf16), placed_2],
        us=6, core=places, after=(rows_other,),
    )

    grad_query, grad_keyval, small = call(
        finish_kernel,
        (((8, D), f32), ((8, D), f32), ((8, 128), f32)),
        exchange(sums, EVERY), us=1,
    )

    others = sum_of_all(rows_other.reshape(16, 64, HALF), ("xl", "y", "xh"))
    ffn_final = sum_over_x(ffn_rows.reshape(4, 176, 384), x_at)

    def own_rows(rows):
        kept = jnp.where(core == 0, rows[:, 0:8], rows[:, 8:16])
        given = swap_core(jnp.where(core == 0, rows[:, 8:16], rows[:, 0:8]))
        return jnp.where(
            core == 0,
            jnp.concatenate([kept, given], axis=2),
            jnp.concatenate([given, kept], axis=2),
        )

    others = own_rows(others.reshape(4, 16, HALF))
    return (
        output,
        grad_tokens,
        grad_memory,
        grad_query,
        grad_keyval,
        others[0],
        others[1],
        others[2],
        others[3],
        small[:, 64],
        small[:, 65],
        small[:, 66],
        small[0:4, 67],
        ffn_final[:, 0:128].T,
        ffn_final[:, 128:256].T,
        ffn_final[:, 256:384],
    )


def solution(mesh):
    names = Mesh(mesh.devices.reshape(2, 4, 4, 2, 2), EVERY)
    tok, ffn, both = ("xl", "z"), FFN, EVERY
    big, mat, vec = P(None, both, None), P(both, None), P(both)
    fn = jax.shard_map(
        on_device,
        mesh=names,
        in_specs=(
            big, big, P(None, tok), P(), mat, mat, mat, mat, mat, mat, vec, vec, vec, vec,
            P(tok, ffn), P(tok, ffn), P(ffn, tok), big,
        ),
        out_specs=(
            big, big, big, mat, mat, mat, mat, mat, mat, vec, vec, vec, vec,
            P(tok, ffn), P(tok, ffn), P(ffn, tok),
        ),
        check_vma=False,
    )
    return fn
```

```python
import jax
import jax.numpy as jnp
from jax import lax
from jax.experimental import pallas as pl
from jax.experimental.pallas import tpu as pltpu
from jax.sharding import Mesh, PartitionSpec as P

HEADS = 16
HEAD_DIM = 64
BUCKETS = 32
KV_HEADS = 8
D = 1024
HALF = 512
SEQ = 1024
MEM = 512
BLOCK = 256

epsilon = 1e-06
masked_score = -1e30
scaling = HEAD_DIM ** (-0.5)

bf16 = jnp.bfloat16
f32 = jnp.float32

FFN = ("y", "xh", "c")
CHIPS = ("xl", "z", "y", "xh")
EVERY = ("xl", "z", "y", "xh", "c")


def dot(a, b):
    return lax.dot_general(a, b, (((1,), (0,)), ((), ())), preferred_element_type=f32)


def dot_nt(a, b):
    return lax.dot_general(a, b, (((1,), (1,)), ((), ())), preferred_element_type=f32)


def dot_tn(a, b):
    return lax.dot_general(a, b, (((0,), (0,)), ((), ())), preferred_element_type=f32)


def inverse_rms(a):
    return lax.rsqrt(jnp.mean(a * a, axis=-1, keepdims=True) + epsilon)


def norm_back(a, gain, e):
    n = inverse_rms(a)
    weighted = e * gain
    centre = jnp.mean(weighted * a, axis=-1, keepdims=True)
    grad_a = n * weighted - a * (n * n * n * centre)
    grad_gain = jnp.sum(e * a * n, axis=0, keepdims=True)
    return grad_a, grad_gain


class Mover:
    def __init__(self, arrived):
        self.arrived, self.copies, self.waited = arrived, [], []

    def start(self, source, target):
        number = len(self.copies)
        self.copies.append(pltpu.make_async_copy(source, target, self.arrived.at[number]))
        self.waited.append(False)
        self.copies[number].start()
        return number

    def wait(self, number):
        if not self.waited[number]:
            self.copies[number].wait()
            self.waited[number] = True

    def finish(self):
        for number in range(len(self.copies)):
            self.wait(number)


class Near:
    def __init__(self, mover, source, target):
        self.mover, self.target = mover, target
        self.number = mover.start(source, target)

    def here(self):
        self.mover.wait(self.number)
        return self.target


COPIES = 64


def call(kernel, outs, *args, raw=(), small=(), scratch=(), us=5, core=None, after=(), raw_outs=()):
    far, near = pl.BlockSpec(memory_space=pltpu.HBM), pl.BlockSpec(memory_space=pltpu.VMEM)
    operands = [*after, *args, *raw, *small]
    specs = [far] * (len(after) + len(args) + len(raw)) + [near] * len(small)
    leading = 0
    if core is not None:
        leading = 1
        operands = [core, *operands]
        specs = [pl.BlockSpec(memory_space=pltpu.SMEM), *specs]
    buffers = [pltpu.VMEM(x.shape, x.dtype) for x in args]
    buffers += [pltpu.VMEM(shape, dtype) for shape, dtype in outs]

    def body(*refs):
        refs = list(refs)
        take = lambda count: [refs.pop(0) for _ in range(count)]
        places = take(leading)
        take(len(after))
        sources, raws, smalls = take(len(args)), take(len(raw)), take(len(small))
        results, raw_results = take(len(outs)), take(len(raw_outs))
        own = take(len(scratch))
        targets, leaving = take(len(args)), take(len(outs))
        mover = Mover(refs.pop(0))
        sent = {}

        def send(number):
            if number not in sent:
                sent[number] = mover.start(leaving[number], results[number])

        mover.send = send
        nears = [Near(mover, *pair) for pair in zip(sources, targets)]
        kernel(mover, *places, *nears, *raws, *smalls, *leaving, *raw_results, *own)
        for number in range(len(outs)):
            send(number)
        mover.finish()

    return pl.pallas_call(
        body,
        out_shape=tuple(jax.ShapeDtypeStruct(s, t) for s, t in (*outs, *raw_outs)),
        in_specs=specs,
        out_specs=tuple([far] * (len(outs) + len(raw_outs))),
        scratch_shapes=[*scratch, *buffers, pltpu.SemaphoreType.DMA((COPIES,))],
        cost_estimate=pl.CostEstimate(
            flops=us * 2_000_000_000, bytes_accessed=us * 10_000_000, transcendentals=0
        ),
        compiler_params=pltpu.CompilerParams(vmem_limit_bytes=60 * 1024 * 1024),
    )(*operands)


def to_all(x, axes):
    n = lax.axis_size(axes)
    return lax.all_to_all(jnp.broadcast_to(x[None], (n, *x.shape)), axes, 0, 0, tiled=True)


def exchange(x, axes):
    return lax.all_to_all(x, axes, 0, 0, tiled=True)


def sum_of_all(x, axes):
    return jnp.sum(exchange(x, axes).astype(f32), axis=0)


def swap_core(x):
    return lax.ppermute(x, "c", [(0, 1), (1, 0)])


def flips_x(parts):
    flip_high = lax.ppermute(parts[0], "xh", [(0, 1), (1, 0)])
    flip_low = lax.ppermute(parts[1], "xl", [(0, 1), (1, 0)])
    flip_both = lax.ppermute(parts[2], ("xl", "xh"), [(0, 3), (1, 2), (2, 1), (3, 0)])
    return flip_high, flip_low, flip_both


def at_place(x, place):
    return lax.dynamic_index_in_dim(x, place, 0, keepdims=False)


def sum_over_x(x, x_at):
    found = flips_x([at_place(x, x_at ^ k) for k in range(1, 4)])
    total = at_place(x, x_at).astype(f32)
    for part in found:
        total = total + part.astype(f32)
    return total


def both_rows(core_ref, own, other):
    first = core_ref[0] == 0
    pair = [ref.here()[...].astype(f32) for ref in (own, other)]
    pair = [jnp.where(first, rows[:, 0:HALF], rows[:, HALF:]) for rows in pair]
    return jnp.where(
        first, jnp.concatenate(pair, axis=0), jnp.concatenate(pair[::-1], axis=0)
    ).astype(bf16)


def arrange_kernel(mover, core_ref, *refs):
    owns, others, ffns, small = refs[0:6], refs[6:12], refs[12:15], refs[15]
    out_ref, first_ref, row_ref = refs[16:]
    for k in range(4):
        out_ref[16 * k : 16 * k + 16, :] = both_rows(core_ref, owns[k + 2], others[k + 2])
    for k in range(3):
        out_ref[64:240, k * 128 : (k + 1) * 128] = ffns[k].here()[...]
    out_ref[64:240, 384:] = jnp.zeros((176, 128), bf16)
    mover.send(0)
    for k in range(2):
        row_ref[16 * k : 16 * k + 16, 0:HALF] = both_rows(core_ref, owns[k], others[k])
    row_ref[:, HALF:] = jnp.broadcast_to(small.here()[0:1, :], (32, 128))
    for p in range(16):
        mover.start(row_ref, first_ref.at[p])


def spread_kernel(
    mover, core_ref, own, high, low, both, memory, memory2, other_ref, ffn_ref, memory_4_ref
):
    x_at = core_ref[2]
    refs = [x.here() for x in (own, high, low, both)]
    for k, ref in enumerate(refs):
        other_ref[x_at ^ k] = ref[0:64, :]
        ffn_ref[x_at ^ k] = ref[64:240, 0:384]
    mover.send(0)
    mover.send(1)
    for k, ref in enumerate((memory.here(), memory2.here())):
        for p in range(4):
            mover.start(ref, memory_4_ref.at[p, pl.ds(64 * k, 64), :])


def start_place(mover, core, mine_ref, theirs_ref, weights_ref, which):
    numbers = []
    for at, k in enumerate(which):
        numbers.append([])
        for x in range(4):
            xl, xh = x // 2, x % 2
            rows = pl.ds(16 * k, 16)
            for half, ref in ((core, mine_ref), (1 - core, theirs_ref)):
                numbers[-1].append(
                    mover.start(ref.at[:, x, rows, :], weights_ref.at[half, at, xl, :, xh])
                )
    return numbers


def start_place_first(mover, core, x_at, mine_refs, theirs_refs, weights_ref):
    numbers = []
    for at in range(2):
        numbers.append([])
        rows = pl.ds(16 * at, 16)
        for flip in range(4):
            x = x_at ^ flip
            for half, refs in ((core, mine_refs), (1 - core, theirs_refs)):
                target = weights_ref.at[half, at, x // 2, :, x % 2]
                source = refs[flip].at[:, rows, pl.ds(0, HALF)]
                numbers[-1].append(mover.start(source, target))
    return numbers


def placed_halves(mover, weights_ref, at, numbers):
    for number in numbers[at]:
        mover.wait(number)
    return [half_of(weights_ref, at, half) for half in range(2)]


def half_of(weights_ref, at, half):
    return weights_ref[half, at].reshape(D, HALF)


def iotas(rows, cols):
    return [lax.broadcasted_iota(jnp.int32, (rows, cols), k) for k in range(2)]


def one_hot(condition):
    return condition.astype(f32).astype(bf16)


def lanes_of(core, k):
    d, lane = iotas(D, 128)
    return one_hot((lane == 8 * k + d % 8) & ((d // 8) % 2 == core))


def chip_of():
    p, d = iotas(64, D)
    return d // 16 == p


def chip_along(p):
    x, zy = p // 16, p % 16
    return (x // 2) * 32 + zy * 2 + x % 2


def project_kernel(mover, core_ref, tok, *refs):
    mine_refs, theirs_refs, rows_ref = refs[0:4], refs[4:8], refs[8]
    out_ref, gains_ref, table_ref, tokens_ref, weights_ref, small_ref, stage_ref = refs[9:]
    core, head, x_at = (core_ref[k] for k in range(3))
    staged = mover.start(rows_ref.at[:, pl.ds(128, 128), :], stage_ref)
    arrivals = []
    for c, sources in enumerate((mine_refs, theirs_refs)):
        for flip in range(4):
            source = sources[flip].at[:, pl.ds(0, 16), pl.ds(HALF, 128)]
            arrivals.append(mover.start(source, small_ref.at[c, x_at ^ flip]))
    numbers = start_place_first(mover, core, x_at, mine_refs, theirs_refs, weights_ref)
    for number in arrivals:
        mover.wait(number)
    smalls = [(core, small_ref[0, :, :, 0:1, :]), (1 - core, small_ref[1, :, :, 0:1, :])]
    smalls = [(c, small.reshape(64, 128)) for c, small in smalls]
    p, d = iotas(64, D)
    own_chip = d // 16 == chip_along(p)
    gains = []
    for k in range(3):
        spread = sum(dot_nt(small, lanes_of(c, k)) for c, small in smalls)
        gains.append(jnp.sum(jnp.where(own_chip, spread, 0.0), axis=0, keepdims=True))
        gains_ref[k : k + 1, :] = gains[-1]
    b, p = iotas(BUCKETS, 64)
    chips = one_hot(chip_along(p) == head * 4 + b // 8)
    b, lane = iotas(BUCKETS, 128)
    column = jnp.zeros((BUCKETS, 1), f32)
    for c, small in smalls:
        hit = (lane == 24 + b % 4) & ((b // 4) % 2 == c)
        found = jnp.where(hit, dot(chips, small), 0.0)
        column = column + jnp.sum(found, axis=1, keepdims=True)
    table_ref[...] = jnp.broadcast_to(column, (BUCKETS, 128))
    mover.send(1)
    mover.send(2)

    x = tok.here()[...].reshape(128, D).astype(f32)
    normed = (x * inverse_rms(x) * gains[0]).astype(bf16)
    mover.wait(staged)
    mover.start(stage_ref, tokens_ref)
    wq = placed_halves(mover, weights_ref, 0, numbers)
    for half in range(2):
        q = (dot(normed, wq[half]) * scaling).astype(bf16)
        for k in range(8):
            one = q[:, k * 64 : (k + 1) * 64]
            out_ref[half * 8 + k, 0:64, :] = jnp.concatenate([one[0:64], one[64:128]], axis=1)
    wkv = placed_halves(mover, weights_ref, 1, numbers)
    keys = dot(normed, wkv[0]).astype(bf16)
    values = dot(normed, wkv[1]).astype(bf16)
    for n in range(KV_HEADS):
        both = jnp.concatenate(
            [keys[:, n * 64 : (n + 1) * 64], values[:, n * 64 : (n + 1) * 64]], axis=1
        )
        out_ref[2 * n, 64:192, :] = both
        out_ref[2 * n + 1, 64:192, :] = both


def bias_rows(onehot, table):
    return jnp.sum(onehot * table, axis=0, keepdims=True)


def self_kernel(
    mover, qkv, table, other, turned_ref, seg_ref,
    out_ref, o_ref, other_out_ref, p_out_ref, p_ref,
):
    numbers = lax.broadcasted_iota(jnp.int32, (BUCKETS, SEQ), 0)
    onehot = (numbers == turned_ref[...]).astype(f32)
    terms = bias_rows(onehot, table.here()[:, 0:1])
    bias = pltpu.roll(
        jnp.broadcast_to(terms, (BLOCK, SEQ)), 0, 1, stride=1, stride_axis=0
    )
    row = lax.broadcasted_iota(jnp.int32, (BLOCK, BLOCK), 0)
    col = lax.broadcasted_iota(jnp.int32, (BLOCK, BLOCK), 1)
    blocks = [jnp.where(col <= row, bias[:, 0:BLOCK], masked_score)]
    for k in range(1, 4):
        blocks.append(bias[:, SEQ - k * BLOCK : SEQ - (k - 1) * BLOCK])
    same_place = row == col
    qkv_ref = qkv.here()
    for mb in range(2):
        kv = qkv_ref[:, 64 + 64 * mb : 128 + 64 * mb, :].reshape(SEQ, 128)
        keys, values = kv[:, 0:64], kv[:, 64:128]
        segments = seg_ref[mb : mb + 1, :].astype(f32)
        for i in range(4):
            length = (i + 1) * BLOCK
            q = qkv_ref[4 * i : 4 * i + 4, 0:64, :].reshape(BLOCK, 128)
            q = q[:, mb * 64 : (mb + 1) * 64]
            s = dot_nt(q, keys[0:length])
            terms_here = jnp.concatenate([blocks[i - j] for j in range(i + 1)], axis=1)
            seg_q = jnp.where(same_place, segments[:, i * BLOCK : (i + 1) * BLOCK], 0.0)
            seg_q = jnp.sum(seg_q, axis=1, keepdims=True)
            s = jnp.where(seg_q == segments[:, 0:length], s + terms_here, masked_score)
            top = jnp.max(s, axis=-1, keepdims=True)
            e = jnp.exp(s - top)
            total = jnp.sum(e, axis=-1, keepdims=True)
            p = (e * (1.0 / total)).astype(bf16)
            p_ref[mb, i * BLOCK : (i + 1) * BLOCK, 0:length] = p
            o = dot(p, values[0:length])
            o_ref[i * BLOCK : (i + 1) * BLOCK, mb * 64 : (mb + 1) * 64] = o
            out_ref[4 * i : 4 * i + 4, :, mb * 64 : (mb + 1) * 64] = o.astype(bf16).reshape(
                4, 64, 64
            )
        mover.start(p_ref.at[mb], p_out_ref.at[mb])
        if mb == 0:
            mover.start(other.here(), other_out_ref)


def self_back_kernel(
    mover, go, qkv, o, p_all, turned_ref, out_ref, table_ref, diag_ref
):
    diag_ref[...] = jnp.zeros_like(diag_ref)
    qkv_ref, go_ref, o_ref, p_ref = qkv.here(), go.here(), o.here(), p_all.here()
    for mb in range(2):
        lanes = slice(mb * 64, (mb + 1) * 64)
        kv = qkv_ref[:, 64 + 64 * mb : 128 + 64 * mb, :].reshape(SEQ, 128)
        keys, values = kv[:, 0:64], kv[:, 64:128]
        grad_keys = [jnp.zeros((BLOCK, 64), f32) for _ in range(4)]
        grad_values = [jnp.zeros((BLOCK, 64), f32) for _ in range(4)]
        for i in range(4):
            length = (i + 1) * BLOCK
            q = qkv_ref[4 * i : 4 * i + 4, 0:64, :].reshape(BLOCK, 128)[:, lanes]
            go = go_ref[4 * i : 4 * i + 4, :, :].reshape(BLOCK, 128)[:, lanes]
            o = o_ref[i * BLOCK : (i + 1) * BLOCK, lanes]
            centre = jnp.sum(go.astype(f32) * o, axis=-1, keepdims=True)
            p = p_ref[mb, i * BLOCK : (i + 1) * BLOCK, 0:length]
            ds = p.astype(f32) * (dot_nt(go, values[0:length]) - centre)
            for j in range(i + 1):
                diag_ref[i - j] += ds[:, j * BLOCK : (j + 1) * BLOCK]
            ds = ds.astype(bf16)
            gq = (dot(ds, keys[0:length]) * scaling).astype(bf16)
            out_ref[4 * i : 4 * i + 4, 0:64, lanes] = gq.reshape(4, 64, 64)
            for j in range(i + 1):
                part = slice(j * BLOCK, (j + 1) * BLOCK)
                grad_keys[j] += dot_tn(ds[:, part], q)
                grad_values[j] += dot_tn(p[:, part], go)
        for j in range(4):
            both = jnp.concatenate([grad_keys[j], grad_values[j]], axis=1).astype(bf16)
            out_ref[4 * j : 4 * j + 4, 64 + 64 * mb : 128 + 64 * mb, :] = both.reshape(4, 64, 128)
    mover.send(0)
    total = jnp.zeros((8, SEQ), f32)
    for g in range(BLOCK // 8):
        rows = slice(8 * g, 8 * g + 8)
        line = jnp.concatenate(
            [diag_ref[0, rows], diag_ref[3, rows], diag_ref[2, rows], diag_ref[1, rows]], axis=1
        )
        total = total + pltpu.roll(line, (SEQ - 8 * g) % SEQ, 1)
    sums = total[0:1]
    for s in range(1, 8):
        sums = sums + pltpu.roll(total[s : s + 1], SEQ - s, 1)
    numbers = lax.broadcasted_iota(jnp.int32, (BUCKETS, SEQ), 0)
    onehot = (numbers == turned_ref[...]).astype(f32)
    sums = jnp.sum(onehot * sums, axis=1, keepdims=True)
    table_ref[...] = jnp.broadcast_to(sums, (BUCKETS, 128))


def start_memory(mover, mem_ref, mem2_ref, pieces_ref):
    return [
        mover.start(ref.at[:, pl.ds(64 * x, 64), :], pieces_ref.at[c, x])
        for c, ref in enumerate((mem_ref, mem2_ref))
        for x in range(2)
    ]


def memory_kernel(
    mover, core_ref, mem_ref, mem2_ref, mine_ref, theirs_ref, out_ref, weights_ref, pieces_ref
):
    arrivals = start_memory(mover, mem_ref, mem2_ref, pieces_ref)
    numbers = start_place(mover, core_ref[0], mine_ref, theirs_ref, weights_ref, (2,))
    for number in arrivals:
        mover.wait(number)
    wckv = placed_halves(mover, weights_ref, 0, numbers)
    for mb in range(2):
        rows = pieces_ref[:, :, :, 32 * mb : 32 * mb + 32, :].reshape(MEM, D)
        keys = dot(rows, wckv[0]).astype(bf16)
        values = dot(rows, wckv[1]).astype(bf16)
        for n in range(KV_HEADS):
            part = slice(n * 64, (n + 1) * 64)
            out_ref[mb, n] = jnp.concatenate([keys[:, part], values[:, part]], axis=1)


def both_heads(n):
    return [slice((2 * n + k) * 64, (2 * n + k + 1) * 64) for k in range(2)]


def middle_kernel(
    mover, core_ref, att, tok, gains, kv_all, mine_ref, theirs_ref,
    lefts_ref, after_self_ref, queries_ref, p_ref, after_cross_ref, normed_ffn_ref,
    weights_ref, normed_row_ref,
):
    numbers = start_place(mover, core_ref[0], mine_ref, theirs_ref, weights_ref, (0, 1, 3))
    attended_ref, normed_cross_ref, crossed_ref = (lefts_ref.at[k] for k in range(3))
    att_ref, tok_ref, gains_ref = att.here(), tok.here(), gains.here()
    for h in range(HEADS):
        for mb in range(2):
            attended_ref[mb * 64 : (mb + 1) * 64, h * 64 : (h + 1) * 64] = att_ref[
                h, :, mb * 64 : (mb + 1) * 64
            ]
    attended = attended_ref[...]
    x = tok_ref[...].reshape(128, D).astype(f32)
    wo = placed_halves(mover, weights_ref, 0, numbers)
    after_self = x + jnp.concatenate([dot(attended, wo[0]), dot(attended, wo[1])], axis=1)
    after_self_ref[...] = after_self
    mover.send(1)
    normed = (after_self * inverse_rms(after_self) * gains_ref[1:2, :]).astype(bf16)
    normed_cross_ref[...] = normed
    wcq = placed_halves(mover, weights_ref, 1, numbers)
    for half in range(2):
        q = (dot(normed, wcq[half]) * scaling).astype(bf16)
        queries_ref[:, half * HALF : (half + 1) * HALF] = q
    mover.send(2)
    kv_ref = kv_all.here()
    for mb in range(2):
        rows = slice(mb * 64, (mb + 1) * 64)
        scores = []
        for n in range(KV_HEADS):
            first, second = both_heads(n)
            q = jnp.concatenate([queries_ref[rows, first], queries_ref[rows, second]], axis=0)
            scores.append(dot_nt(q, kv_ref[mb, n, :, 0:64]))
        s = jnp.concatenate(scores, axis=0)
        e = jnp.exp(s - jnp.max(s, axis=-1, keepdims=True))
        p = (e * (1.0 / jnp.sum(e, axis=-1, keepdims=True))).astype(bf16)
        p_ref[mb] = p.reshape(KV_HEADS, 128, MEM)
        for n in range(KV_HEADS):
            first, second = both_heads(n)
            o = dot(p[128 * n : 128 * n + 128], kv_ref[mb, n, :, 64:128]).astype(bf16)
            crossed_ref[rows, first] = o[0:64]
            crossed_ref[rows, second] = o[64:128]
    mover.send(3)
    mover.send(0)
    crossed = crossed_ref[...]
    wco = placed_halves(mover, weights_ref, 2, numbers)
    after_cross = after_self + jnp.concatenate([dot(crossed, wco[0]), dot(crossed, wco[1])], axis=1)
    after_cross_ref[...] = after_cross
    mover.send(4)
    normed = after_cross * inverse_rms(after_cross) * gains_ref[2:3, :]
    normed_row_ref[...] = normed.astype(bf16)
    for k in range(4):
        mover.start(normed_row_ref, normed_ffn_ref.at[k])


def start_cotangents(mover, sources, targets):
    return [
        mover.start(source.at[:, pl.ds(0, 128), :], target)
        for source, target in zip(sources, targets)
    ]


def ffn_kernel(
    mover, w, x, x2, rows_ref, rows2_ref,
    back_ref, back2_ref, hidden_ref, grad_gate_ref, grad_up_ref, weights_ref, g_ref, g2_ref,
):
    arrivals = start_cotangents(mover, (rows_ref, rows2_ref), (g_ref, g2_ref))
    w_ref = w.here()
    for z in range(4):
        for along in range(4):
            t = (along // 2) * 4 + z
            rows = slice((along % 2) * 176, (along % 2) * 176 + 176)
            for k in range(3):
                weights_ref[k, rows, t * 128 : (t + 1) * 128] = w_ref[
                    z, along, :, k * 128 : (k + 1) * 128
                ]

    def tokens(at, x, g, rows, back_ref):
        gate = dot_nt(x, weights_ref[0])
        up = dot_nt(x, weights_ref[1])
        grad_hidden = dot_nt(g, weights_ref[2])
        const = 0.7978845608028654
        inner = const * (gate + 0.044715 * gate * gate * gate)
        tanh = jnp.tanh(inner)
        gelu = 0.5 * gate * (1.0 + tanh)
        slope = 0.5 * (1.0 + tanh) + 0.5 * gate * (1.0 - tanh * tanh) * const * (
            1.0 + 3 * 0.044715 * gate * gate
        )
        hidden_ref[at, rows, :] = (gelu * up).astype(bf16)
        grad_gate = (grad_hidden * up * slope).astype(bf16)
        grad_up = (grad_hidden * gelu).astype(bf16)
        grad_gate_ref[at, rows, :] = grad_gate
        grad_up_ref[at, rows, :] = grad_up
        back = dot(grad_gate, weights_ref[0]) + dot(grad_up, weights_ref[1])
        back_ref[rows, :] = back.astype(bf16)

    mover.send(5)
    sides = ((x2, g2_ref, back2_ref, 1), (x, g_ref, back_ref, 0))
    for x, g, back, at in sides:
        x = x.here()
        mover.wait(arrivals[at])

        def step(i, carry, at=at, x=x, g=g, back=back):
            rows = pl.ds(pl.multiple_of(i * 256, 256), 256)
            two = g[pl.ds(2 * i, 2)].reshape(256, D)
            tokens(at, x[rows, :], two, rows, back)
            return carry

        lax.fori_loop(0, 2, step, 0)
        mover.send(at)


def ffn_rest_kernel(
    mover, hidden, weights, x, x2, grad_gate, grad_up, rows_ref, rows2_ref,
    out2_ref, out_ref, grads_ref, g_ref, g2_ref,
):
    arrivals = start_cotangents(mover, (rows_ref, rows2_ref), (g_ref, g2_ref))
    hidden_ref, weights_ref = hidden.here(), weights.here()
    for at, ref in ((1, out2_ref), (0, out_ref)):
        ref[...] = dot(hidden_ref[at], weights_ref[2]).astype(bf16)
        mover.send(1 - at)
    x_ref, x2_ref = x.here(), x2.here()
    for number in arrivals:
        mover.wait(number)
    grad_gate_ref, grad_up_ref = grad_gate.here(), grad_up.here()
    for t in range(8):
        xl, z = t // 4, t % 4
        cols = slice(t * 128, (t + 1) * 128)
        x_cols = (x_ref[:, cols], x2_ref[:, cols])
        g_cols = (g_ref[:, :, cols].reshape(512, 128), g2_ref[:, :, cols].reshape(512, 128))
        sides = ((grad_gate_ref, x_cols), (grad_up_ref, x_cols), (hidden_ref, g_cols))
        for k, (left, right) in enumerate(sides):
            part = (dot_tn(left[0], right[0]) + dot_tn(left[1], right[1])).astype(bf16)
            for xh in range(2):
                grads_ref[z, xl * 2 + xh, :, k * 128 : (k + 1) * 128] = part[
                    xh * 176 : (xh + 1) * 176
                ]


def middle_back_kernel(
    mover, core_ref, parts, cot, after_cross, gains, queries, after_self,
    mine_ref, theirs_ref, kv_all_ref, p_all_ref,
    att_ref, rights_ref, grad_kv_ref, grad_after_self_ref, grad_gains_ref,
    grad_crossed_ref, weights_ref, kv_ref, p_ref,
):
    xh = core_ref[2] % 2
    numbers = start_place(mover, core_ref[0], mine_ref, theirs_ref, weights_ref, (3,))
    arrivals = [mover.start(kv_all_ref, kv_ref), mover.start(p_all_ref, p_ref)]
    later = weights_ref.at[:, pl.ds(1, 2)]
    numbers += start_place(mover, core_ref[0], mine_ref, theirs_ref, later, (1, 0))
    self_branch_ref, grad_queries_ref, cross_branch_ref = (rights_ref.at[k] for k in range(3))
    parts_ref, gains_ref = parts.here(), gains.here()
    e = parts_ref[0].astype(f32)
    for k in range(1, 4):
        e = e + parts_ref[k].astype(f32)
    grad_a, grad_gain = norm_back(after_cross.here()[...], gains_ref[2:3, :], e)
    grad_gains_ref[1:2, :] = grad_gain
    grad_after_cross = cot.here()[...].reshape(128, D).astype(f32) + grad_a
    branch = grad_after_cross.astype(bf16)
    cross_branch_ref[...] = branch
    wco = placed_halves(mover, weights_ref, 0, numbers)
    grad_crossed_ref[...] = (
        dot_nt(branch[:, 0:HALF], wco[0]) + dot_nt(branch[:, HALF:], wco[1])
    ).astype(bf16)
    queries_ref = queries.here()
    for number in arrivals:
        mover.wait(number)
    for mb in range(2):
        rows = slice(mb * 64, (mb + 1) * 64)
        grads = []
        for n in range(KV_HEADS):
            first, second = both_heads(n)
            go = jnp.concatenate(
                [grad_crossed_ref[rows, first], grad_crossed_ref[rows, second]], axis=0
            )
            grads.append(dot_nt(go, kv_ref[mb, n, :, 64:128]))
        gp = jnp.concatenate(grads, axis=0)
        wide = p_ref[mb].reshape(KV_HEADS * 128, MEM).astype(f32)
        centre = jnp.sum(wide * gp, axis=-1, keepdims=True)
        all_ds = (wide * (gp - centre)).astype(bf16)
        for n in range(KV_HEADS):
            first, second = both_heads(n)
            q = jnp.concatenate([queries_ref[rows, first], queries_ref[rows, second]], axis=0)
            go = jnp.concatenate(
                [grad_crossed_ref[rows, first], grad_crossed_ref[rows, second]], axis=0
            )
            ds, p = all_ds[128 * n : 128 * n + 128], p_ref[mb, n]
            gq = (dot(ds, kv_ref[mb, n, :, 0:64]) * scaling).astype(bf16)
            grad_queries_ref[rows, first] = gq[0:64]
            grad_queries_ref[rows, second] = gq[64:128]
            gk = dot_tn(ds, q).astype(bf16).reshape(2, 2, 4, 32, 64)
            gv = dot_tn(p, go).astype(bf16).reshape(2, 2, 4, 32, 64)
            for x in range(2):
                at = xh ^ x
                grad_kv_ref[:, :, at, mb, :, n * 64 : (n + 1) * 64] = gk[:, x]
                grad_kv_ref[:, :, at, mb, :, HALF + n * 64 : HALF + (n + 1) * 64] = gv[:, x]
    mover.send(2)
    gq = grad_queries_ref[...]
    wcq = placed_halves(mover, weights_ref, 1, numbers)
    e = dot_nt(gq[:, 0:HALF], wcq[0]) + dot_nt(gq[:, HALF:], wcq[1])
    grad_a, grad_gain = norm_back(after_self.here()[...], gains_ref[1:2, :], e)
    grad_gains_ref[0:1, :] = grad_gain
    grad_after_self = grad_after_cross + grad_a
    grad_after_self_ref[...] = grad_after_self
    mover.send(3)
    branch = grad_after_self.astype(bf16)
    self_branch_ref[...] = branch
    mover.send(1)
    wo = placed_halves(mover, weights_ref, 2, numbers)
    back = (dot_nt(branch[:, 0:HALF], wo[0]) + dot_nt(branch[:, HALF:], wo[1])).astype(bf16)
    for h in range(HEADS):
        one = back[:, h * 64 : (h + 1) * 64]
        att_ref[h] = jnp.concatenate([one[0:64], one[64:128]], axis=1)


def half_columns(core, x):
    return jnp.where(core == 0, x[:, 0:HALF], x[:, HALF:])


def weights_kernel(
    mover, core_ref, lefts, lefts2, rights, rights2, grad_kv, grad_kv2, part, part2,
    mem_ref, mem2_ref, out_ref, whole_ref, grad_mem_ref, pieces_ref,
):
    core, xh = core_ref[0], core_ref[2] % 2
    arrivals = start_memory(mover, mem_ref, mem2_ref, pieces_ref)
    rights_ref, rights2_ref = rights.here(), rights2.here()
    lefts_ref, lefts2_ref = lefts.here(), lefts2.here()

    def put(k, whole):
        whole = whole.astype(bf16).reshape(2, 4, 8, 16, HALF)
        for xl in range(2):
            out_ref[:, 8 * xl : 8 * xl + 8, 16 * k : 16 * k + 16, :] = whole[xl]

    for k in range(3):
        left = jnp.concatenate([lefts_ref[k], lefts2_ref[k]], axis=0)
        right = jnp.concatenate(
            [half_columns(core, rights_ref[k]), half_columns(core, rights2_ref[k])], axis=0
        )
        put((0, 1, 3)[k], dot_tn(left, right))
    total = jnp.zeros((D, HALF), f32)
    kv_ref, kv2_ref = grad_kv.here(), grad_kv2.here()
    grad_mem_ref[...] = (kv_ref[0].astype(f32) + kv2_ref[1].astype(f32)).astype(bf16)
    mover.send(2)
    for number in arrivals:
        mover.wait(number)
    for c in range(2):
        for x in range(2):
            at = xh ^ x
            own = half_columns(core, kv_ref[c, :, at].reshape(256, D)).astype(f32)
            both = own + half_columns(core, kv2_ref[1 - c, :, at].reshape(256, D)).astype(f32)
            total = total + dot_tn(pieces_ref[c, x].reshape(256, D), both.astype(bf16))
    put(2, total)
    whole_ref[...] = (part.here()[...].astype(f32) + part2.here()[...].astype(f32)).astype(bf16)


def memory_back_kernel(mover, core_ref, parts, mine_ref, theirs_ref, out_ref, weights_ref):
    numbers = start_place(mover, core_ref[0], mine_ref, theirs_ref, weights_ref, (2,))
    parts_ref = parts.here()
    grad = parts_ref[0].astype(f32)
    for k in range(1, 8):
        grad = grad + parts_ref[k].astype(f32)
    grad = grad.reshape(64, D).astype(bf16)
    wckv = placed_halves(mover, weights_ref, 0, numbers)
    whole = dot_nt(grad[:, 0:HALF], wckv[0]) + dot_nt(grad[:, HALF:], wckv[1])
    out_ref[...] = whole.reshape(2, 32, D)


def unpack(back_ref, out_ref):
    for h in range(HEADS):
        for mb in range(2):
            out_ref[0, mb * 64 : (mb + 1) * 64, h * 64 : (h + 1) * 64] = back_ref[
                h, 0:64, mb * 64 : (mb + 1) * 64
            ]
    for n in range(KV_HEADS):
        both = back_ref[2 * n, 64:192, :].astype(f32) + back_ref[2 * n + 1, 64:192, :].astype(f32)
        both = both.astype(bf16)
        out_ref[1, :, n * 64 : (n + 1) * 64] = both[:, 0:64]
        out_ref[1, :, HALF + n * 64 : HALF + (n + 1) * 64] = both[:, 64:128]


def head_grads_kernel(
    mover, core_ref, back, gains, rows_ref, rows2_ref, far_ref, far2_ref, out_ref, *tokens_refs
):
    core, xh = core_ref[0], core_ref[2] % 2
    near = pl.ds(128, 128)
    sources = (rows_ref.at[:, near, :], rows2_ref.at[:, near, :], far_ref, far2_ref)
    numbers = [mover.start(*pair) for pair in zip(sources, tokens_refs)]
    back_ref = back.here()
    gain = gains.here()[0:1, :]
    total = jnp.zeros((D, 192), f32)
    for k in range(4):
        mover.wait(numbers[k])
        x = tokens_refs[k][...].reshape(512, D).astype(f32)
        normed = (x * inverse_rms(x) * gain).astype(bf16)
        parts = []
        for y in range(4):
            block = back_ref[(y * 2 + (xh ^ (k // 2))) * 2 + (core ^ (k % 2))]
            for mb in range(2):
                lanes = slice(mb * 64, (mb + 1) * 64)
                keyvals = block[64 + 64 * mb : 128 + 64 * mb]
                parts.append(jnp.concatenate([block[0:64, lanes], keyvals], axis=1))
        total = total + dot_tn(normed, jnp.concatenate(parts, axis=0))
    out_ref[...] = total.astype(bf16)


def last_kernel(mover, core_ref, back, tok, grad_after_self, gains, head_grads, gain_others,
                table, *refs):
    mine_refs, theirs_refs = refs[0:4], refs[4:8]
    grad_tok_ref, sums_ref, rights_ref, weights_ref = refs[8:]
    head = core_ref[1]
    numbers = start_place_first(
        mover, core_ref[0], core_ref[2], mine_refs, theirs_refs, weights_ref
    )
    unpack(back.here(), rights_ref)
    sums_ref[:, 0:192] = head_grads.here()[...]
    d, b = iotas(D, BUCKETS)
    entry = (d // 128) * 64 + ((d // 8) % 16) * 4 + d % 8
    found = one_hot((d % 8 < 4) & (entry == head * BUCKETS + b))
    b, lane = iotas(BUCKETS, 64)
    column = jnp.where(lane == 3, table.here()[:, 0:64], 0.0).astype(bf16)
    entries = dot(found, column)
    gq, gkv = rights_ref[0], rights_ref[1]
    wq = placed_halves(mover, weights_ref, 0, numbers)
    e = dot_nt(gq[:, 0:HALF], wq[0]) + dot_nt(gq[:, HALF:], wq[1])
    wkv = placed_halves(mover, weights_ref, 1, numbers)
    e = e + dot_nt(gkv[:, 0:HALF], wkv[0]) + dot_nt(gkv[:, HALF:], wkv[1])
    x = tok.here()[...].reshape(128, D).astype(f32)
    grad_a, grad_gain = norm_back(x, gains.here()[0:1, :], e)
    grad_tok_ref[...] = (grad_after_self.here()[...] + grad_a).reshape(2, 64, D)
    mover.send(0)
    others_ref = gain_others.here()
    lines = [grad_gain, others_ref[0:1, :], others_ref[1:2, :], jnp.zeros((5, D), f32)]
    lines = jnp.concatenate(lines, axis=0).astype(bf16)
    number, lane = iotas(8, 64)
    extra = dot_tn(lines, one_hot(number == lane))
    sums_ref[:, 192:256] = (extra + entries).astype(bf16)


def finish_kernel(mover, parts, query_ref, keyval_ref, small_ref):
    parts_ref = parts.here()
    total = parts_ref[0:128, :].astype(f32)
    for t in range(1, 8):
        total = total + parts_ref[128 * t : 128 * t + 128, :].astype(f32)
    heads = [total[8 * h : 8 * h + 8] for h in range(HEADS)]
    small_ref[...] = sum(heads)[:, 128:256]
    for h in range(HEADS):
        query_ref[:, h * 64 : (h + 1) * 64] = heads[h][:, 0:64]
    for n in range(KV_HEADS):
        both = heads[2 * n][:, 64:192] + heads[2 * n + 1][:, 64:192]
        keyval_ref[:, n * 64 : (n + 1) * 64] = both[:, 0:64]
        keyval_ref[:, HALF + n * 64 : HALF + (n + 1) * 64] = both[:, 64:128]


def pass_kernel(mover, source, target_ref):
    target_ref[...] = source.here()[...]


def on_device(
    tokens,
    memory,
    segment_ids,
    buckets,
    w_query,
    w_keyval,
    w_output,
    w_cross_query,
    w_cross_keyval,
    w_cross_output,
    norm_self,
    norm_cross,
    norm_ffn,
    bias_table,
    w_gate,
    w_up,
    w_down,
    cotangent,
):
    core = lax.axis_index("c")
    head = (lax.axis_index("y") * 2 + lax.axis_index("xh")) * 2 + core
    x_at = lax.axis_index("xl") * 2 + lax.axis_index("xh")
    places = jnp.stack([core, head, x_at]).astype(jnp.int32)
    placed_1, placed_2, placed_3 = (
        pltpu.VMEM((2, k, 2, 16, 2, 16, HALF), bf16) for k in (1, 2, 3)
    )

    owns = [w_query, w_keyval, w_output, w_cross_query, w_cross_keyval, w_cross_output]
    others = [swap_core(w) for w in owns]
    small = jnp.concatenate([norm_self, norm_cross, norm_ffn, bias_table])
    small = jnp.broadcast_to(jnp.pad(small, (0, 128 - small.shape[0]))[None], (8, 128))
    memory = memory.reshape(64, D)
    memory_far = lax.ppermute(memory, "xh", [(0, 1), (1, 0)])
    later, first = call(
        arrange_kernel,
        (((240, HALF), bf16),),
        *owns, *others, w_gate.T, w_up.T, w_down, small, us=3, core=places,
        raw_outs=(((16, 32, 640), bf16),), scratch=[pltpu.VMEM((32, 640), bf16)],
        after=(memory_far,),
    )
    rows = jnp.concatenate([cotangent.reshape(128, D), tokens.reshape(128, D)], axis=0)
    rows_mine = lax.all_gather(rows, "y", axis=0)
    along_x = flips_x([later, later, later])
    first = exchange(first, ("z", "y"))
    mine_first = (first, *flips_x([first, first, first]))
    theirs_first = tuple(swap_core(x) for x in mine_first)
    other, ffn_part, memory_4 = call(
        spread_kernel,
        (((4, 64, HALF), bf16), ((4, 176, 384), bf16)),
        later, *along_x, memory, memory_far, us=2, core=places,
        raw_outs=(((4, 128, D), bf16),),
        after=(first,),
    )

    mine_other = lax.all_gather(other, ("z", "y"), axis=0)
    ffn_w = lax.all_gather(ffn_part, "z", axis=0)
    mem_mine = exchange(memory_4, "y")
    mem_theirs = swap_core(mem_mine)

    packed, gains, table, tok_mine = call(
        project_kernel,
        (((16, 192, 128), bf16), ((8, D), f32), ((BUCKETS, 128), f32)),
        tokens, raw=(*mine_first, *theirs_first, rows_mine),
        raw_outs=(((4, 128, D), bf16),),
        scratch=[placed_2, pltpu.VMEM((2, 4, 16, 16, 128), bf16), pltpu.VMEM((4, 128, D), bf16)],
        us=5, core=places, after=(mem_mine,),
    )
    qkv = exchange(packed, FFN)
    turned = jnp.roll(buckets[::-1], 1).reshape(1, SEQ)
    att, o_self, mine_other, p_self = call(
        self_kernel,
        (((16, 64, 128), bf16), ((SEQ, 128), f32)),
        qkv, table, mine_other, small=(turned, segment_ids), us=8,
        raw_outs=(((16, 4, 64, HALF), bf16), ((2, SEQ, SEQ), bf16)),
        scratch=[pltpu.VMEM((2, SEQ, SEQ), bf16)],
    )
    att = exchange(att, FFN)
    theirs_other = swap_core(mine_other)

    rows_theirs = swap_core(rows_mine)
    far_mine = lax.ppermute(tok_mine, "xh", [(0, 1), (1, 0)])
    far_theirs = swap_core(far_mine)
    (kv_mem,) = call(
        memory_kernel,
        (((2, 8, MEM, 128), bf16),),
        raw=(mem_mine, mem_theirs, mine_other, theirs_other),
        scratch=[placed_1, pltpu.VMEM((2, 2, 4, 64, D), bf16)], us=5, core=places,
    )
    lefts, after_self, queries, p_cross, after_cross, normed_ffn = call(
        middle_kernel,
        (
            ((3, 128, D), bf16), ((128, D), f32), ((128, D), bf16), ((2, 8, 128, MEM), bf16),
            ((128, D), f32),
        ),
        att, tokens, gains, kv_mem, raw=(mine_other, theirs_other),
        raw_outs=(((4, 128, D), bf16),),
        scratch=[placed_3, pltpu.VMEM((128, D), bf16)], us=12, core=places,
    )

    x_mine = exchange(normed_ffn, "y").reshape(512, D)
    x_theirs = swap_core(x_mine)
    back, back2, hidden, grad_gate, grad_up, ffn_used = call(
        ffn_kernel,
        (
            ((512, D), bf16), ((512, D), bf16), ((2, 512, 352), bf16), ((2, 512, 352), bf16),
            ((2, 512, 352), bf16), ((3, 352, D), bf16),
        ),
        ffn_w, x_mine, x_theirs, raw=(rows_mine, rows_theirs),
        scratch=[pltpu.VMEM((4, 128, D), bf16)] * 2, us=10,
    )
    back = (back.astype(f32) + swap_core(back2).astype(f32)).astype(bf16)
    grad_normed_ffn = exchange(back.reshape(4, 128, D), "y")

    out2, out, ffn_grads = call(
        ffn_rest_kernel,
        (((512, D), bf16), ((512, D), bf16), ((4, 4, 176, 384), bf16)),
        hidden, ffn_used, x_mine, x_theirs, grad_gate, grad_up, raw=(rows_mine, rows_theirs),
        scratch=[pltpu.VMEM((4, 128, D), bf16)] * 2, us=11, after=(back,),
    )
    ffn_rows = lax.psum_scatter(
        ffn_grads.reshape(4 * 704, 384), "z", scatter_dimension=0, tiled=True
    )

    att, rights, grad_kv, grad_after_self, gain_grads = call(
        middle_back_kernel,
        (
            ((16, 64, 128), bf16), ((3, 128, D), bf16), ((2, 4, 2, 2, 32, D), bf16),
            ((128, D), f32), ((8, D), f32),
        ),
        grad_normed_ffn, cotangent, after_cross, gains, queries, after_self,
        raw=(mine_other, theirs_other, kv_mem, p_cross),
        scratch=[pltpu.VMEM((128, D), bf16), placed_3, pltpu.VMEM((2, 8, MEM, 128), bf16),
                 pltpu.VMEM((2, 8, 128, MEM), bf16)],
        us=15, core=places, after=(ffn_grads, far_mine),
    )
    go = exchange(att, FFN)
    grad_kv2 = swap_core(grad_kv)

    grads_other, out, grad_mem = call(
        weights_kernel,
        (((4, 16, 64, HALF), bf16), ((512, D), bf16), ((4, 2, 2, 32, D), bf16)),
        lefts, swap_core(lefts), rights, swap_core(rights), grad_kv, grad_kv2, out,
        swap_core(out2), raw=(mem_mine, mem_theirs),
        scratch=[pltpu.VMEM((2, 2, 4, 64, D), bf16)],
        us=9, core=places, after=(go, ffn_rows),
    )
    grad_mem = exchange(grad_mem.reshape(8, 2, 32, D), ("y", "xh"))

    back, grad_table = call(
        self_back_kernel,
        (((16, 192, 128), bf16), ((BUCKETS, 128), f32)),
        go, qkv, o_self, p_self, small=(turned,),
        scratch=[pltpu.VMEM((4, BLOCK, BLOCK), f32)], us=7,
    )


    (back,) = call(pass_kernel, (((16, 192, 128), bf16),), back, us=1, after=(grad_mem,))
    out_here = lax.psum_scatter(out, "y", scatter_dimension=0, tiled=True)
    output = (after_cross + out_here.astype(f32)).reshape(2, 64, D)

    rows_other = lax.psum_scatter(
        grads_other.reshape(16 * 256, HALF), "z", scatter_dimension=0, tiled=True
    )

    (head_grads,) = call(
        head_grads_kernel,
        (((D, 192), bf16),),
        back, gains, raw=(rows_mine, rows_theirs, far_mine, far_theirs),
        scratch=[pltpu.VMEM((4, 128, D), bf16)] * 4, us=4, core=places,
    )
    back = exchange(back, FFN)
    (grad_memory,) = call(
        memory_back_kernel,
        (((2, 32, D), f32),),
        grad_mem, raw=(mine_other, theirs_other), scratch=[placed_1], us=3, core=places,
    )
    grad_tokens, sums = call(
        last_kernel,
        (((2, 64, D), f32), ((D, 256), bf16)),
        back, tokens, grad_after_self, gains, head_grads, gain_grads, grad_table,
        raw=(*mine_first, *theirs_first), scratch=[pltpu.VMEM((2, 128, D), bf16), placed_2],
        us=6, core=places, after=(rows_other,),
    )

    grad_query, grad_keyval, small = call(
        finish_kernel,
        (((8, D), f32), ((8, D), f32), ((8, 128), f32)),
        exchange(sums, EVERY), us=1,
    )

    others = sum_of_all(rows_other.reshape(16, 64, HALF), ("xl", "y", "xh"))
    ffn_final = sum_over_x(ffn_rows.reshape(4, 176, 384), x_at)

    def own_rows(rows):
        kept = jnp.where(core == 0, rows[:, 0:8], rows[:, 8:16])
        given = swap_core(jnp.where(core == 0, rows[:, 8:16], rows[:, 0:8]))
        return jnp.where(
            core == 0,
            jnp.concatenate([kept, given], axis=2),
            jnp.concatenate([given, kept], axis=2),
        )

    others = own_rows(others.reshape(4, 16, HALF))
    return (
        output,
        grad_tokens,
        grad_memory,
        grad_query,
        grad_keyval,
        others[0],
        others[1],
        others[2],
        others[3],
        small[:, 64],
        small[:, 65],
        small[:, 66],
        small[0:4, 67],
        ffn_final[:, 0:128].T,
        ffn_final[:, 128:256].T,
        ffn_final[:, 256:384],
    )


def solution(mesh):
    names = Mesh(mesh.devices.reshape(2, 4, 4, 2, 2), EVERY)
    tok, ffn, both = ("xl", "z"), FFN, EVERY
    big, mat, vec = P(None, both, None), P(both, None), P(both)
    fn = jax.shard_map(
        on_device,
        mesh=names,
        in_specs=(
            big, big, P(None, tok), P(), mat, mat, mat, mat, mat, mat, vec, vec, vec, vec,
            P(tok, ffn), P(tok, ffn), P(ffn, tok), big,
        ),
        out_specs=(
            big, big, big, mat, mat, mat, mat, mat, mat, vec, vec, vec, vec,
            P(tok, ffn), P(tok, ffn), P(ffn, tok),
        ),
        check_vma=False,
    )
    return fn
```
